32 devices in a mesh: parts: 2 (over x), fsdp: 16 (over z, y, core).
Axes of the slice: x: 2, y: 2, z: 4, core: 2. Of those that a mesh axis runs over, the one named last changes fastest.
Arguments:
- inputs: bfloat16 [8192, 8192], P(('parts', 'fsdp')), parts along dimension 0, may hold values from -6 to 6
- cotangent: bfloat16 [8192, 1024], P(('parts', 'fsdp')), parts along dimension 0, may hold values from -1.5 to 1.5
- frozen_value_weight: bfloat16 [8192, 1024], P('fsdp'), may hold values from -0.0625 to 0.0625
- adapter_down_weights: bfloat16 [1024, 131072], P('parts', 'fsdp'), parts along dimension 0, may hold values from -0.0625 to 0.0625
- adapter_up_weights: bfloat16 [1024, 16384], P('parts', 'fsdp'), parts along dimension 0, may hold values from -0.1875 to 0.1875
- padded_block_adapter: int32 [64], P('parts'), parts along dimension 0, may hold values from 0 to 511
- block_live_rows: int32 [64], P('parts'), parts along dimension 0, may hold values from 1 to 128, 2560 in all
- adapter_storage_row: int32 [1024], P('parts'), parts along dimension 0, may hold values from 0 to 511, each once
Outputs:
- input_gradient: bfloat16 [8192, 8192], P(('parts', 'fsdp')), parts along dimension 0
- down_grad: float32 [1024, 131072], P('parts', 'fsdp'), parts along dimension 0
- up_grad: float32 [1024, 16384], P('parts', 'fsdp'), parts along dimension 0
The draws below stay inside these ranges and needn't reach their ends.
There are 2 independent parts, one for each index of `parts`. The reference program is written for one: setup_inputs(seed, part) draws one part's arguments, and reference() takes and returns one part's arrays. A program takes and returns all parts, laid end to end along the dimension named above; an argument that names none is the same for every part. Nothing has to cross between parts.
Inputs may be any that keep to these rules, and one draw needn't show every extreme that they name: `padded_block_adapter`: adapter ids below 512. `adapter_storage_row`: a permutation of the storage rows.
All inputs are finite; a program needn't handle non-finite values.
Results may differ from the reference program's by a relative error of at most 0.0032.
Values may be sent and summed in bfloat16 or wider, within the bound.
No kernel may reach another device: no remote copies, remote signals or barrier semaphores. Data moves between devices by JAX's collectives and lax.ppermute only.
A program may use at most 128 MiB of HBM per device.

```python
import math
import jax
import jax.numpy as jnp
import numpy as np
from jax import lax

MODEL_WIDTH = 8192
ADAPTER_RANK = 16
ADAPTER_GROUP = 512
BLOCK = 128
VALUE_WIDTH = 1024
BLOCKS = 32
TOKENS = 4096


def touch_ends(values, key, low, top_value):
    longest = values.shape.index(max(values.shape))
    spots = []
    for shift in (0, 1):
        where = [jax.random.randint(jax.random.fold_in(key, axis), (), 0, length) for axis, length in enumerate(values.shape)]
        where[longest] = (where[longest] + shift) % values.shape[longest]
        spots.append(tuple(where))
    return values.at[spots[0]].set(low).at[spots[1]].set(top_value)


def block_levels(key, dims, shards, least, high):
    level = 1.0
    for axis_at, parts in shards:
        steps = jax.random.uniform(jax.random.fold_in(jax.random.fold_in(key, 6), axis_at), (parts,), jnp.float32, least / len(shards), high / len(shards))
        level = level * jnp.repeat(jnp.exp(steps), dims[axis_at] // parts).reshape((-1,) + (1,) * (len(dims) - 1 - axis_at))
    return level


def rank_table(amount, slope):
    weights = [(1 << 20) // math.isqrt(grade ** slope) + 1 for grade in range(1, amount + 1)]
    spread = 1 + sum(weights) // (1 << 30)
    return np.cumsum(np.array([max(1, weight // spread) for weight in weights]))


def ranked(key, dims, amount, lean):
    table = rank_table(amount, lean)
    lot = jax.random.randint(jax.random.fold_in(key, 1), dims, 0, int(table[amount - 1]))
    rank = jnp.searchsorted(jnp.asarray(table, jnp.int32), lot, side="right")
    return jax.random.permutation(jax.random.fold_in(key, 2), amount)[rank].astype(jnp.int32)


def profile(number_of, total, most, skew):
    loads = [(1 << 20) // math.isqrt(grade ** skew) + 1 for grade in range(2, number_of + 1)]
    spare, counts = total - most - (number_of - 1), [1] * (number_of - 1)
    while spare > 0:
        movable = [i for i in range(number_of - 1) if counts[i] < most]
        whole, left = sum([loads[i] for i in movable]), spare
        for i in movable:
            addition = min(most - counts[i], max(1, left * loads[i] // whole), spare)
            counts[i] = counts[i] + addition
            spare = spare - addition
    return np.array([most] + counts)


def uneven(own_key, number_of, total, bound, slope):
    if number_of == 2:
        one = jax.random.randint(own_key, (), max(1, total - bound), min(bound, total - 1) + 1)
        return jnp.stack([one, total - one])
    lengths = jnp.asarray(profile(number_of, total, bound, slope), jnp.int32)
    pairs = (number_of - 1) // 2
    donor, receiver = lengths[1:1 + 2 * pairs:2], lengths[2:2 + 2 * pairs:2]
    slack = jnp.minimum(donor - 1, bound - receiver)
    passed = jax.random.randint(jax.random.fold_in(own_key, 1), (pairs,), 0, 1 << 20) % (slack + 1)
    lengths = lengths.at[1:1 + 2 * pairs:2].set(donor - passed).at[2:2 + 2 * pairs:2].set(receiver + passed)
    return lengths[jax.random.permutation(jax.random.fold_in(own_key, 2), number_of)]


def gaussian(rng, extent, scale, bound, cuts=(), held_as=jnp.bfloat16):
    result = scale * jax.random.normal(rng, extent, jnp.float32)
    if cuts:
        result = result * block_levels(rng, extent, cuts, -0.22, 0.18)
    return jnp.clip(result, -bound, bound).astype(held_as)


def setup_inputs(seed: int = 0, part: int = 0) -> dict:
    key_list = jax.random.split(jax.random.key(seed), 9)
    part_keys = jax.random.split(jax.random.fold_in(key_list[8], part), 9)
    return {
        "inputs": gaussian(part_keys[0], (TOKENS, MODEL_WIDTH), 1.0, 6.0, ((0, 16),)),
        "cotangent": gaussian(part_keys[1], (TOKENS, VALUE_WIDTH), 0.25, 1.5, ((0, 16),)),
        "frozen_value_weight": gaussian(key_list[2], (MODEL_WIDTH, VALUE_WIDTH), MODEL_WIDTH ** -0.5, 0.0625, ((0, 16),)),
        "adapter_down_weights": gaussian(part_keys[3], (ADAPTER_GROUP, MODEL_WIDTH * ADAPTER_RANK), MODEL_WIDTH ** -0.5, 0.0625, ((1, 16),)),
        "adapter_up_weights": gaussian(part_keys[4], (ADAPTER_GROUP, ADAPTER_RANK * VALUE_WIDTH), VALUE_WIDTH ** -0.5, 0.1875, ((1, 16),)),
        "padded_block_adapter": touch_ends(ranked(part_keys[5], (BLOCKS,), ADAPTER_GROUP, 2), jax.random.fold_in(part_keys[5], 3), 0, ADAPTER_GROUP - 1).astype(jnp.int32),
        "block_live_rows": uneven(part_keys[6], BLOCKS, 5 * BLOCKS * BLOCK // 8, BLOCK, 1).astype(jnp.int32),
        "adapter_storage_row": jax.random.permutation(part_keys[7], ADAPTER_GROUP).astype(jnp.int32),
    }


adapter_scale = 2.0


def slot_lookup(padded_block_adapter, adapter_storage_row):
    matches = padded_block_adapter[:, None] == jnp.arange(ADAPTER_GROUP, dtype=jnp.int32)[None, :]
    return jnp.sum(jnp.where(matches, adapter_storage_row[None, :], 0), axis=1).astype(jnp.int32)


def reference(inputs, cotangent, frozen_value_weight, adapter_down_weights, adapter_up_weights, padded_block_adapter, block_live_rows, adapter_storage_row):
    block_storage_row = slot_lookup(padded_block_adapter, adapter_storage_row)
    positions = jnp.arange(BLOCK, dtype=jnp.int32)
    live_mask = positions[None, :] < block_live_rows[:, None]
    blocked_cot = cotangent.reshape(BLOCKS, BLOCK, VALUE_WIDTH)
    masked = jnp.where(live_mask[:, :, None], blocked_cot, jnp.zeros_like(blocked_cot))
    blocked_in = inputs.reshape(BLOCKS, BLOCK, MODEL_WIDTH)
    weight_wide = frozen_value_weight.astype(jnp.float32)
    highest_precision = lax.Precision.HIGHEST

    def one_block(block_item):
        rows_in, rows_cot, current_storage_row = block_item
        down_weight_matrix = adapter_down_weights[current_storage_row].astype(jnp.float32).reshape(MODEL_WIDTH, ADAPTER_RANK)
        up_weight_matrix = adapter_up_weights[current_storage_row].astype(jnp.float32).reshape(ADAPTER_RANK, VALUE_WIDTH)
        full_width_input = rows_in.astype(jnp.float32)
        full_width_cotangent = rows_cot.astype(jnp.float32)
        frozen_gradient = jnp.dot(full_width_cotangent, weight_wide.T, precision=highest_precision)
        rank_projection = lax.optimization_barrier(jnp.dot(full_width_input, down_weight_matrix, precision=highest_precision).astype(jnp.bfloat16))
        rank_projection = rank_projection.astype(jnp.float32)
        rank_space_gradient = lax.optimization_barrier(jnp.dot(full_width_cotangent, up_weight_matrix.T, precision=highest_precision).astype(jnp.bfloat16))
        rank_space_gradient = rank_space_gradient.astype(jnp.float32)
        output_gradient_rows = (frozen_gradient + adapter_scale * jnp.dot(rank_space_gradient, down_weight_matrix.T, precision=highest_precision)).astype(jnp.bfloat16)
        partial_down_weight = adapter_scale * jnp.dot(full_width_input.T, rank_space_gradient, precision=highest_precision).reshape(MODEL_WIDTH * ADAPTER_RANK)
        partial_up_weight = adapter_scale * jnp.dot(rank_projection.T, full_width_cotangent, precision=highest_precision).reshape(ADAPTER_RANK * VALUE_WIDTH)
        return output_gradient_rows, partial_down_weight, partial_up_weight

    output_gradient_rows, partial_down_weight, partial_up_weight = lax.map(one_block, (blocked_in, masked, block_storage_row))
    onehot = (jnp.arange(ADAPTER_GROUP, dtype=jnp.int32)[:, None] == block_storage_row[None, :]).astype(jnp.float32)
    down_grad = jnp.dot(onehot, partial_down_weight, precision=highest_precision)
    up_grad = jnp.dot(onehot, partial_up_weight, precision=highest_precision)
    return output_gradient_rows.reshape(TOKENS, MODEL_WIDTH), down_grad, up_grad
```

```python
import functools

import jax
import jax.numpy as jnp
from jax import lax
from jax.experimental import pallas as pl
from jax.experimental.pallas import tpu as pltpu
from jax.sharding import PartitionSpec as P

ADAPTER_RANK = 16
ADAPTER_GROUP = 512
BLOCK = 128
LANES = 128
VMEM_LIMIT = 48 * 1024 * 1024

adapter_scale = 2.0


def slot_lookup(padded_block_adapter, adapter_storage_row):
    matches = padded_block_adapter[:, None] == jnp.arange(ADAPTER_GROUP, dtype=jnp.int32)[None, :]
    return jnp.sum(jnp.where(matches, adapter_storage_row[None, :], 0), axis=1)


def iota(shape, axis):
    return lax.broadcasted_iota(jnp.int32, shape, axis)


def dot_t(a, b):
    return lax.dot_general(a, b, (((1,), (1,)), ((), ())), preferred_element_type=jnp.float32)


def dot_n(a, b, precision=None):
    return lax.dot_general(
        a, b, (((1,), (0,)), ((), ())), precision=precision, preferred_element_type=jnp.float32
    )


def dot_0(a, b):
    return lax.dot_general(a, b, (((0,), (0,)), ((), ())), preferred_element_type=jnp.float32)


def spread_rows(flat, count):
    rows = count * 8
    repeat = (iota((rows, count), 0) // 8 == iota((rows, count), 1)).astype(jnp.bfloat16)
    wide = dot_n(repeat, flat)
    mine = iota((rows, LANES), 1) // 16 == iota((rows, LANES), 0) % 8
    return jnp.where(mine, wide, 0.0).astype(jnp.bfloat16)


def tiles_kernel(own_cot, far_cot, left, right, own_out, far_out):
    step = pl.program_id(0)
    half = pl.num_programs(0) // 2

    def part(weight):
        own_out[...] = dot_t(own_cot[...], weight[...])
        far_out[...] = dot_t(far_cot[...], weight[...]).astype(far_out.dtype)

    pl.when(step < half)(lambda: part(left))
    pl.when(step >= half)(lambda: part(right))


def product_tiles(own_cot, far_cot, left, right):
    rows, depth = own_cot.shape
    width = left.shape[0]
    tile = 256
    per = width // tile
    whole = pl.BlockSpec((rows, depth), lambda i: (0, 0))
    return pl.pallas_call(
        tiles_kernel,
        grid=(2 * per,),
        in_specs=[
            whole,
            whole,
            pl.BlockSpec((tile, depth), lambda i: (jnp.minimum(i, per - 1), 0)),
            pl.BlockSpec((tile, depth), lambda i: (jnp.maximum(i - per, 0), 0)),
        ],
        out_specs=[
            pl.BlockSpec((rows, tile), lambda i: (0, i)),
            pl.BlockSpec((rows, tile), lambda i: (0, i)),
        ],
        out_shape=[
            jax.ShapeDtypeStruct((rows, 2 * width), jnp.float32),
            jax.ShapeDtypeStruct((rows, 2 * width), jnp.bfloat16),
        ],
        compiler_params=pltpu.CompilerParams(vmem_limit_bytes=VMEM_LIMIT),
        cost_estimate=pl.CostEstimate(
            flops=8 * rows * depth * width, bytes_accessed=6 * 1024 * 1024, transcendentals=0
        ),
        name="product_tiles",
    )(own_cot, far_cot, left, right)


def low_rank_columns(g8, a_rows, chunk):
    parts = []
    for k in range(a_rows.shape[0]):
        spread = spread_rows(a_rows[k], chunk)
        parts.append(dot_t(g8[k * BLOCK : (k + 1) * BLOCK, :], spread))
    return adapter_scale * jnp.concatenate(parts, axis=0)


def finish_kernel(meta, own, far, g8, a_rows, _, out):
    half = own.shape[1]
    lr = low_rank_columns(g8[...], a_rows[...], a_rows.shape[1])
    mine, other = own[...], far[...].astype(jnp.float32)
    first = meta[0] == 0
    out[:, :half] = (jnp.where(first, mine, other) + lr[:, :half]).astype(out.dtype)
    out[:, half:] = (jnp.where(first, other, mine) + lr[:, half:]).astype(out.dtype)


def finish_columns(meta, own, far, g8, a_flat, out):
    rows, both = own.shape
    half = both // 2
    chunk = 2 * half * ADAPTER_RANK // LANES
    blocks = a_flat.shape[0]
    return pl.pallas_call(
        finish_kernel,
        grid_spec=pltpu.PrefetchScalarGridSpec(
            num_scalar_prefetch=1,
            grid=(2,),
            in_specs=[
                pl.BlockSpec((rows, half), lambda j, m: (0, j)),
                pl.BlockSpec((rows, half), lambda j, m: (0, j)),
                pl.BlockSpec((rows, LANES), lambda j, m: (0, 0)),
                pl.BlockSpec((blocks, chunk, LANES), lambda j, m: (0, m[1 + j], 0)),
                pl.BlockSpec(memory_space=pl.ANY),
            ],
            out_specs=pl.BlockSpec((rows, 2 * half), lambda j, m: (0, m[1 + j])),
        ),
        out_shape=jax.ShapeDtypeStruct(out.shape, out.dtype),
        input_output_aliases={5: 0},
        compiler_params=pltpu.CompilerParams(vmem_limit_bytes=VMEM_LIMIT),
        cost_estimate=pl.CostEstimate(
            flops=8 * rows * LANES * half, bytes_accessed=3 * 1024 * 1024, transcendentals=0
        ),
        name="finish_columns",
    )(meta, own, far, g8, a_flat, out)


def own_kernel(meta, cot, first, second, g8, a_rows, out):
    half = first.shape[0]
    lr = low_rank_columns(g8[...], a_rows[...], a_rows.shape[1])
    out[:, :half] = (dot_t(cot[...], first[...]) + lr[:, :half]).astype(out.dtype)
    out[:, half:] = (dot_t(cot[...], second[...]) + lr[:, half:]).astype(out.dtype)


def own_columns(meta, cot, first, second, g8, a_flat, width):
    rows, depth = cot.shape
    half = first.shape[0]
    chunk = 2 * half * ADAPTER_RANK // LANES
    blocks = a_flat.shape[0]
    return pl.pallas_call(
        own_kernel,
        grid_spec=pltpu.PrefetchScalarGridSpec(
            num_scalar_prefetch=1,
            grid=(1,),
            in_specs=[
                pl.BlockSpec((rows, depth), lambda j, m: (0, 0)),
                pl.BlockSpec((half, depth), lambda j, m: (0, 0)),
                pl.BlockSpec((half, depth), lambda j, m: (0, 0)),
                pl.BlockSpec((rows, LANES), lambda j, m: (0, 0)),
                pl.BlockSpec((blocks, chunk, LANES), lambda j, m: (0, m[0], 0)),
            ],
            out_specs=pl.BlockSpec((rows, 2 * half), lambda j, m: (0, m[0])),
        ),
        out_shape=jax.ShapeDtypeStruct((rows, width), jnp.bfloat16),
        compiler_params=pltpu.CompilerParams(vmem_limit_bytes=VMEM_LIMIT),
        cost_estimate=pl.CostEstimate(
            flops=4 * rows * depth * half, bytes_accessed=4 * 1024 * 1024, transcendentals=0
        ),
        name="own_columns",
    )(meta, cot, first, second, g8, a_flat)


def adapter_kernel(x, cot, recv, sent, g8_out):
    devices = recv.shape[0]
    rows = x.shape[0]
    blocks = rows // BLOCK
    width = x.shape[1]
    chunk = width * ADAPTER_RANK // LANES // devices
    up_chunk = cot.shape[1] * ADAPTER_RANK // LANES // devices
    columns = width // devices
    tiles = cot.shape[1] // LANES
    lane = iota((BLOCK, LANES), 1)
    square_from, square_to = iota((LANES, LANES), 0), iota((LANES, LANES), 1)
    gather_rank = (square_from // 8 == square_to % 16).astype(jnp.float32)
    gather_low = (square_from % 16 == square_to // 8).astype(jnp.float32)
    fold = (iota((chunk, columns), 0) == iota((chunk, columns), 1) // 8).astype(jnp.bfloat16)
    own_lanes = iota((columns, LANES), 1) // 16 == iota((columns, LANES), 0) % 8
    down_rows = blocks * chunk
    b_all = recv[:, down_rows : down_rows + blocks * up_chunk, :].astype(jnp.float32)
    ups = []
    for k in range(blocks):
        m = cot[k * BLOCK : (k + 1) * BLOCK, :]
        b_flat = b_all[:, k * up_chunk : (k + 1) * up_chunk, :].reshape(devices * up_chunk, LANES)
        b_flat = b_flat.astype(jnp.bfloat16)
        total = jnp.zeros((BLOCK, LANES), jnp.float32)
        for t in range(tiles):
            part = dot_t(m[:, t * LANES : (t + 1) * LANES], b_flat)
            total = total + jnp.where(lane % tiles == t, part, 0.0)
        g8 = dot_n(total, gather_rank, lax.Precision.HIGHEST).astype(jnp.bfloat16)
        g8_out[k * BLOCK : (k + 1) * BLOCK, :] = g8
        low = jnp.zeros((BLOCK, LANES), jnp.float32)
        for j in range(devices):
            x_part = x[k * BLOCK : (k + 1) * BLOCK, j * columns : (j + 1) * columns]
            spread = spread_rows(recv[j, k * chunk : (k + 1) * chunk, :], chunk)
            low = low + dot_n(x_part, spread)
            wide = jnp.where(own_lanes, dot_0(x_part, g8), 0.0).astype(jnp.bfloat16)
            folded = adapter_scale * dot_n(fold, wide)
            sent[j, k * chunk : (k + 1) * chunk, :] = folded.astype(sent.dtype)
        low8 = dot_n(low, gather_low, lax.Precision.HIGHEST).astype(jnp.bfloat16)
        up = dot_0(low8, m)
        flat = jnp.zeros((LANES, LANES), jnp.float32)
        row = iota((LANES, LANES), 0)
        for t in range(tiles):
            flat = flat + jnp.where(row % tiles == t, up[:, t * LANES : (t + 1) * LANES], 0.0)
        ups.append((adapter_scale * flat).reshape(devices, up_chunk, LANES))
    sent[:, down_rows : down_rows + blocks * up_chunk, :] = jnp.concatenate(ups, axis=1).astype(
        sent.dtype
    )


def adapter_terms(x, cot, recv):
    rows = x.shape[0]
    return pl.pallas_call(
        adapter_kernel,
        out_shape=[
            jax.ShapeDtypeStruct(recv.shape, jnp.bfloat16),
            jax.ShapeDtypeStruct((rows, LANES), jnp.bfloat16),
        ],
        compiler_params=pltpu.CompilerParams(vmem_limit_bytes=VMEM_LIMIT),
        cost_estimate=pl.CostEstimate(
            flops=8 * rows * x.shape[1] * LANES, bytes_accessed=8 * 1024 * 1024, transcendentals=0
        ),
        name="adapter_terms",
    )(x, cot, recv)


def ring_body(
    inputs,
    cotangent,
    frozen_value_weight,
    adapter_down_weights,
    adapter_up_weights,
    padded_block_adapter,
    block_live_rows,
    adapter_storage_row,
    *,
    devices,
):
    chips = devices // 2
    token_rows, hidden_width = inputs.shape
    block_count = token_rows // BLOCK
    all_blocks = padded_block_adapter.shape[0]
    shard = frozen_value_weight.shape[0]
    index = lax.axis_index("fsdp")
    core, chip = index % 2, index // 2
    part = lax.axis_index("parts")
    order = list(range(0, chips, 2)) + list(range(chips - 1, 0, -2))
    place = {c: i for i, c in enumerate(order)}
    order_array = jnp.array(order, jnp.int32)
    my_place = jnp.array([place[c] for c in range(chips)], jnp.int32)[chip]
    ring = []
    for c in range(chips):
        ring.append((2 * c, 2 * order[(place[c] + 1) % chips]))
        ring.append((2 * c + 1, 2 * order[(place[c] - 1) % chips] + 1))
    cores = [(i, i ^ 1) for i in range(devices)]
    across = [(0, 1), (1, 0)]

    live_rows = lax.dynamic_slice_in_dim(block_live_rows, index * block_count, block_count)
    positions = jnp.arange(BLOCK, dtype=jnp.int32)
    live_mask = positions[None, :] < live_rows[:, None]
    blocked_cot = cotangent.reshape(block_count, BLOCK, -1)
    masked = jnp.where(live_mask[:, :, None], blocked_cot, jnp.zeros_like(blocked_cot)).reshape(
        cotangent.shape
    )
    far_masked = lax.ppermute(masked, "parts", across)
    other_shard = lax.ppermute(frozen_value_weight, "fsdp", cores)
    first_shard = jnp.where(core == 0, frozen_value_weight, other_shard)
    second_shard = jnp.where(core == 0, other_shard, frozen_value_weight)
    travelling = jnp.where(part == 0, first_shard, second_shard)

    slots = slot_lookup(padded_block_adapter, adapter_storage_row)
    per_down = adapter_down_weights.shape[1] // LANES
    per_up = adapter_up_weights.shape[1] // LANES
    down_rows = jnp.take(adapter_down_weights, slots, axis=0).reshape(devices, -1, LANES)
    up_rows = jnp.take(adapter_up_weights, slots, axis=0).reshape(devices, -1, LANES)
    payload = jnp.concatenate([down_rows, up_rows], axis=1)
    recv = lax.all_to_all(payload, "fsdp", split_axis=0, concat_axis=0, tiled=True)
    sent, g8 = adapter_terms(inputs, masked, recv)
    a_flat = (
        recv[:, : block_count * per_down, :]
        .reshape(devices, block_count, per_down, LANES)
        .transpose(1, 0, 2, 3)
        .reshape(block_count, devices * per_down, LANES)
    )
    grads = lax.all_to_all(sent, "fsdp", split_axis=0, concat_axis=0, tiled=True)

    held = []
    for step in range(chips // 2 - 1):
        travelling = lax.ppermute(travelling, "fsdp", ring)
        forwarded = lax.ppermute(travelling, "fsdp", cores)
        own, far = product_tiles(masked, far_masked, travelling, forwarded)
        far = lax.ppermute(far, "parts", across)
        direction = jnp.where(core == 0, -1, 1)
        near_chip = order_array[(my_place + direction * (step + 1)) % chips]
        far_chip = order_array[(my_place - direction * (step + 1)) % chips]
        held.append((jnp.stack([part, near_chip, far_chip]).astype(jnp.int32), own, far))
    piece = lax.dynamic_slice_in_dim(travelling, core * (shard // 2), shard // 2)
    piece = lax.ppermute(piece, "fsdp", ring)
    other_piece = lax.ppermute(piece, "fsdp", cores)
    last = jnp.concatenate(
        [
            jnp.where(core == 0, piece, other_piece),
            jnp.where(core == 0, other_piece, piece),
        ],
        axis=0,
    )
    own_last = dot_t(masked, last)
    far_last = lax.ppermute(dot_t(far_masked, last).astype(jnp.bfloat16), "parts", across)

    out = own_columns(
        chip[None].astype(jnp.int32), masked, first_shard, second_shard, g8, a_flat, hidden_width
    )
    for meta, own, far in held:
        out = finish_columns(meta, own, far, g8, a_flat, out)
    opposite = order_array[(my_place + chips // 2) % chips]
    meta = jnp.stack([part, opposite]).astype(jnp.int32)
    out = finish_last(meta, own_last, far_last, g8, a_flat, out)

    onehot = (
        jnp.arange(ADAPTER_GROUP, dtype=jnp.int32)[:, None] == slots[None, :]
    ).astype(jnp.bfloat16)
    down = grads[:, : block_count * per_down, :].reshape(all_blocks, per_down * LANES)
    up = grads[:, block_count * per_down :, :].reshape(all_blocks, per_up * LANES)
    down_grad = jnp.dot(onehot, down, preferred_element_type=jnp.float32)
    up_grad = jnp.dot(onehot, up, preferred_element_type=jnp.float32)
    return (out, down_grad, up_grad)


def finish_last(meta, own, far, g8, a_flat, out):
    rows, half = own.shape
    chunk = 2 * half * ADAPTER_RANK // LANES
    blocks = a_flat.shape[0]
    return pl.pallas_call(
        finish_kernel,
        grid_spec=pltpu.PrefetchScalarGridSpec(
            num_scalar_prefetch=1,
            grid=(1,),
            in_specs=[
                pl.BlockSpec((rows, half), lambda j, m: (0, 0)),
                pl.BlockSpec((rows, half), lambda j, m: (0, 0)),
                pl.BlockSpec((rows, LANES), lambda j, m: (0, 0)),
                pl.BlockSpec((blocks, chunk, LANES), lambda j, m: (0, m[1], 0)),
                pl.BlockSpec(memory_space=pl.ANY),
            ],
            out_specs=pl.BlockSpec((rows, 2 * half), lambda j, m: (0, m[1])),
        ),
        out_shape=jax.ShapeDtypeStruct(out.shape, out.dtype),
        input_output_aliases={5: 0},
        compiler_params=pltpu.CompilerParams(vmem_limit_bytes=VMEM_LIMIT),
        cost_estimate=pl.CostEstimate(
            flops=4 * rows * LANES * half, bytes_accessed=2 * 1024 * 1024, transcendentals=0
        ),
        name="finish_last",
    )(meta, own, far, g8, a_flat, out)


def gather_body(
    inputs,
    cotangent,
    frozen_value_weight,
    adapter_down_weights,
    adapter_up_weights,
    padded_block_adapter,
    block_live_rows,
    adapter_storage_row,
):
    hidden_width = inputs.shape[1]
    kv_width = cotangent.shape[1]
    token_rows = inputs.shape[0]
    block_count = token_rows // BLOCK
    first_block = lax.axis_index("fsdp") * block_count
    live_rows = lax.dynamic_slice_in_dim(block_live_rows, first_block, block_count)
    positions = jnp.arange(BLOCK, dtype=jnp.int32)
    live_mask = positions[None, :] < live_rows[:, None]
    blocked_cot = cotangent.reshape(block_count, BLOCK, kv_width)
    masked_blocks = jnp.where(live_mask[:, :, None], blocked_cot, jnp.zeros_like(blocked_cot))
    masked = masked_blocks.reshape(token_rows, kv_width)
    block_storage_row = slot_lookup(padded_block_adapter, adapter_storage_row)
    down_weight_rows = jnp.take(adapter_down_weights, block_storage_row, axis=0)
    up_weight_rows = jnp.take(adapter_up_weights, block_storage_row, axis=0)
    down_mine, up_mine = (
        lax.all_to_all(down_weight_rows, "fsdp", split_axis=0, concat_axis=1, tiled=True),
        lax.all_to_all(up_weight_rows, "fsdp", split_axis=0, concat_axis=1, tiled=True),
    )
    frozen_gradient = lax.dot_general(
        masked,
        lax.all_gather(frozen_value_weight, "fsdp", axis=0, tiled=True),
        (((1,), (1,)), ((), ())),
        preferred_element_type=jnp.float32,
    )
    down_weight_matrix = down_mine.reshape(block_count, hidden_width, ADAPTER_RANK)
    up_weight_matrix = up_mine.reshape(block_count, ADAPTER_RANK, kv_width)
    blocked_in = inputs.reshape(block_count, BLOCK, hidden_width)
    rank_projection = jnp.einsum(
        "kbd,kdr->kbr", blocked_in, down_weight_matrix, preferred_element_type=jnp.float32
    ).astype(jnp.bfloat16)
    rank_space_gradient = jnp.einsum(
        "kbv,krv->kbr", masked_blocks, up_weight_matrix, preferred_element_type=jnp.float32
    ).astype(jnp.bfloat16)
    adapter_gradient_term = adapter_scale * jnp.einsum(
        "kbr,kdr->kbd", rank_space_gradient, down_weight_matrix, preferred_element_type=jnp.float32
    )
    input_gradient = (
        frozen_gradient + adapter_gradient_term.reshape(token_rows, hidden_width)
    ).astype(jnp.bfloat16)
    partial_down_weight = adapter_scale * jnp.einsum(
        "kbd,kbr->kdr", blocked_in, rank_space_gradient, preferred_element_type=jnp.float32
    )
    partial_up_weight = adapter_scale * jnp.einsum(
        "kbr,kbv->krv", rank_projection, masked_blocks, preferred_element_type=jnp.float32
    )
    partial_down_weight = partial_down_weight.reshape(block_count, hidden_width * ADAPTER_RANK)
    partial_up_weight = partial_up_weight.reshape(block_count, ADAPTER_RANK * kv_width)
    recv_down, recv_up = (
        lax.all_to_all(partial_down_weight, "fsdp", split_axis=1, concat_axis=0, tiled=True),
        lax.all_to_all(partial_up_weight, "fsdp", split_axis=1, concat_axis=0, tiled=True),
    )
    onehot = (
        jnp.arange(ADAPTER_GROUP, dtype=jnp.int32)[:, None] == block_storage_row[None, :]
    ).astype(jnp.float32)
    highest_precision = lax.Precision.HIGHEST
    down_grad = jnp.dot(
        onehot, recv_down, precision=highest_precision, preferred_element_type=jnp.float32
    )
    up_grad = jnp.dot(
        onehot, recv_up, precision=highest_precision, preferred_element_type=jnp.float32
    )
    return (input_gradient, down_grad, up_grad)


def solution(mesh):
    devices = mesh.shape["fsdp"]
    in_specs = (
        P(("parts", "fsdp"), None),
        P(("parts", "fsdp"), None),
        P("fsdp", None),
        P("parts", "fsdp"),
        P("parts", "fsdp"),
        P("parts"),
        P("parts"),
        P("parts"),
    )
    out_specs = (P(("parts", "fsdp"), None), P("parts", "fsdp"), P("parts", "fsdp"))

    def program(*arrays):
        shard = arrays[2].shape[0] // devices
        if mesh.shape["parts"] == 2 and devices % 4 == 0 and shard % 256 == 0:
            body = functools.partial(ring_body, devices=devices)
        else:
            body = gather_body
        return jax.shard_map(
            body, mesh=mesh, in_specs=in_specs, out_specs=out_specs, check_vma=False
        )(*arrays)

    return program
```

```python
import functools

import jax
import jax.numpy as jnp
import numpy as np
from jax import lax
from jax.experimental import pallas as pl
from jax.experimental.pallas import tpu as pltpu
from jax.sharding import PartitionSpec as P

ADAPTER_RANK = 16
ADAPTER_GROUP = 512
BLOCK = 128
LANES = 128
PARAMS = pltpu.CompilerParams(vmem_limit_bytes=48 * 1024 * 1024)
SMALL = pl.CostEstimate(flops=1, bytes_accessed=1, transcendentals=0)

adapter_scale = 2.0


def slot_lookup(padded_block_adapter, adapter_storage_row):
    matches = padded_block_adapter[:, None] == jnp.arange(ADAPTER_GROUP, dtype=jnp.int32)[None, :]
    return jnp.sum(jnp.where(matches, adapter_storage_row[None, :], 0), axis=1)


def iota(shape, axis):
    return lax.broadcasted_iota(jnp.int32, shape, axis)


def dot_t(a, b):
    return lax.dot_general(a, b, (((1,), (1,)), ((), ())), preferred_element_type=jnp.float32)


def dot_n(a, b, precision=None):
    return lax.dot_general(
        a, b, (((1,), (0,)), ((), ())), precision=precision, preferred_element_type=jnp.float32
    )


def dot_0(a, b):
    return lax.dot_general(a, b, (((0,), (0,)), ((), ())), preferred_element_type=jnp.float32)


def lane_cat(parts):
    return jnp.concatenate(parts, axis=-1)


def mask_kernel(meta, live, cot, out):
    row = iota((BLOCK, cot.shape[1]), 0)
    for k in range(cot.shape[0] // BLOCK):
        rows = slice(k * BLOCK, (k + 1) * BLOCK)
        value = cot[rows, :].astype(jnp.float32)
        out[rows, :] = jnp.where(row < live[meta[0] + k], value, 0.0).astype(out.dtype)


def mask_rows(meta, block_live_rows, cotangent):
    whole = pl.BlockSpec(cotangent.shape, lambda i, *_: (0, 0))
    return pl.pallas_call(
        mask_kernel,
        grid_spec=pltpu.PrefetchScalarGridSpec(
            num_scalar_prefetch=2, grid=(1,), in_specs=[whole], out_specs=whole
        ),
        out_shape=jax.ShapeDtypeStruct(cotangent.shape, cotangent.dtype),
        compiler_params=PARAMS,
        cost_estimate=SMALL,
        name="mask_rows",
    )(meta, block_live_rows, cotangent)


def rank_major_order(transposed):
    shape = (8 * LANES, 8 * LANES)
    near, far = (1, 0) if transposed else (0, 1)
    a, b = iota(shape, near), iota(shape, far)
    return ((a % LANES) * 8 + a // LANES == b).astype(jnp.bfloat16)


def gather_kernel(adapter, storage, down, up, payload, dbuf, ubuf, dscr, uscr, cols, dsem, usem):
    blocks = adapter.shape[0]
    devices = payload.shape[0]
    group = dbuf.shape[1]
    per_down, per_up = down.shape[1] // LANES, up.shape[1] // LANES
    down_rows = 2 * per_down

    def copies(b):
        slot = storage[adapter[b]]
        start = pl.multiple_of((slot // group) * group, group)
        return (
            slot % group,
            pltpu.make_async_copy(down.at[pl.ds(start, group), :], dbuf.at[b], dsem.at[b]),
            pltpu.make_async_copy(up.at[pl.ds(start, group), :], ubuf.at[b], usem.at[b]),
        )

    def begin(b, carry):
        _, first, second = copies(b)
        first.start()
        second.start()
        return carry

    lax.fori_loop(0, blocks, begin, 0)
    order = rank_major_order(False)

    def one(j, carry):
        wide, narrow = [], []
        for k in range(2):
            b = 2 * j + k
            row, first, second = copies(b)
            first.wait()
            second.wait()
            late = row >= 8
            line = row % 8
            value = dbuf[b].astype(jnp.float32)
            value = jnp.where(late, value[8:], value[:8])
            for t in range(per_down):
                dscr[k, 8 * t : 8 * t + 8, :] = value[:, t * LANES : (t + 1) * LANES]
            wide.append(dscr[k, pl.ds(line, per_down, stride=8), :])
            value = ubuf[b].astype(jnp.float32)
            value = jnp.where(late, value[8:], value[:8])
            for t in range(per_up):
                uscr[k, 8 * t : 8 * t + 8, :] = value[:, t * LANES : (t + 1) * LANES]
            narrow.append(uscr[k, pl.ds(line, per_up, stride=8), :])
        turned = jnp.concatenate(wide, axis=0).T
        start = pl.multiple_of(j * ADAPTER_RANK, ADAPTER_RANK)
        for lo in range(8):
            piece = turned[lo * ADAPTER_RANK : (lo + 1) * ADAPTER_RANK, :]
            cols[pl.ds(start, ADAPTER_RANK), lo * LANES : (lo + 1) * LANES] = piece.astype(cols.dtype)
        payload[j, down_rows:, :] = jnp.concatenate(narrow, axis=0).astype(payload.dtype)
        return carry

    lax.fori_loop(0, devices, one, 0)
    result = dot_n(cols[...], order).astype(payload.dtype).reshape(devices, ADAPTER_RANK, 8 * LANES)
    for q in range(8):
        payload[:, q * ADAPTER_RANK : (q + 1) * ADAPTER_RANK, :] = result[
            :, :, q * LANES : (q + 1) * LANES
        ]


def gather_rows(padded_block_adapter, adapter_storage_row, down, up, devices):
    blocks = padded_block_adapter.shape[0]
    per_down, per_up = down.shape[1] // LANES, up.shape[1] // LANES
    group = 16
    rows = 2 * (per_down + per_up)
    shape = (devices, rows, LANES)
    return pl.pallas_call(
        gather_kernel,
        grid_spec=pltpu.PrefetchScalarGridSpec(
            num_scalar_prefetch=2,
            grid=(1,),
            in_specs=[pl.BlockSpec(memory_space=pl.ANY)] * 2,
            out_specs=pl.BlockSpec(shape, lambda i, *_: (0, 0, 0)),
            scratch_shapes=[
                pltpu.VMEM((blocks, group, down.shape[1]), down.dtype),
                pltpu.VMEM((blocks, group, up.shape[1]), up.dtype),
                pltpu.VMEM((2, 8 * per_down, LANES), jnp.float32),
                pltpu.VMEM((2, 8 * per_up, LANES), jnp.float32),
                pltpu.VMEM((devices * ADAPTER_RANK, 8 * LANES), jnp.bfloat16),
                pltpu.SemaphoreType.DMA((blocks,)),
                pltpu.SemaphoreType.DMA((blocks,)),
            ],
        ),
        out_shape=jax.ShapeDtypeStruct(shape, jnp.bfloat16),
        compiler_params=PARAMS,
        cost_estimate=SMALL,
        name="gather_rows",
    )(padded_block_adapter, adapter_storage_row, down, up)


def adapter_kernel(x, cot, recv, sent, g_out, low_scr, gt_scr):
    step = pl.program_id(0)
    devices = recv.shape[0]
    blocks = x.shape[0] // BLOCK
    span = x.shape[1]
    tiles = cot.shape[1] // LANES
    up_chunk = tiles * ADAPTER_RANK // devices
    down_rows = recv.shape[1] - blocks * up_chunk
    per = down_rows // blocks // ADAPTER_RANK
    here = span // LANES // per

    @pl.when(step == 0)
    def _():
        lane = iota((BLOCK, LANES), 1)
        gather_rank = (iota((LANES, LANES), 0) // 8 == iota((LANES, LANES), 1)).astype(jnp.float32)
        b_all = recv[:, down_rows:, :].astype(jnp.float32)
        for k in range(blocks):
            m = cot[k * BLOCK : (k + 1) * BLOCK, :]
            b_flat = b_all[:, k * up_chunk : (k + 1) * up_chunk, :].reshape(LANES, LANES)
            b_flat = b_flat.astype(jnp.bfloat16)
            total = jnp.zeros((BLOCK, LANES), jnp.float32)
            for t in range(tiles):
                part = dot_t(m[:, t * LANES : (t + 1) * LANES], b_flat)
                total = total + jnp.where(lane % tiles == t, part, 0.0)
            g = dot_n(total, gather_rank, lax.Precision.HIGHEST).astype(jnp.bfloat16)
            g_out[k * BLOCK : (k + 1) * BLOCK, :] = g
            gt_scr[k] = g.astype(jnp.float32).T[:ADAPTER_RANK, :].astype(jnp.bfloat16)
        low_scr[...] = jnp.zeros_like(low_scr)

    for k in range(blocks):
        part = x[k * BLOCK : (k + 1) * BLOCK, :]
        first = k * per * ADAPTER_RANK
        a = lane_cat(
            [
                recv[step * here + j, first + q * ADAPTER_RANK : first + (q + 1) * ADAPTER_RANK, :]
                for j in range(here)
                for q in range(per)
            ]
        )
        low_scr[k] += dot_t(part, a)
        grad = (adapter_scale * dot_n(gt_scr[k], part)).astype(sent.dtype)
        for j in range(here):
            for q in range(per):
                tile = j * per + q
                sent[
                    step * here + j, first + q * ADAPTER_RANK : first + (q + 1) * ADAPTER_RANK, :
                ] = grad[:, tile * LANES : (tile + 1) * LANES]

    @pl.when(step == pl.num_programs(0) - 1)
    def _():
        ups = []
        row = iota((LANES, LANES), 0)
        spread = (iota((ADAPTER_RANK, LANES), 1) // 8 == iota((ADAPTER_RANK, LANES), 0)).astype(
            jnp.bfloat16
        )
        for k in range(blocks):
            low8 = dot_n(low_scr[k].astype(jnp.bfloat16), spread).astype(jnp.bfloat16)
            up = dot_0(low8, cot[k * BLOCK : (k + 1) * BLOCK, :])
            flat = jnp.zeros((LANES, LANES), jnp.float32)
            for t in range(tiles):
                flat = flat + jnp.where(row % tiles == t, up[:, t * LANES : (t + 1) * LANES], 0.0)
            ups.append((adapter_scale * flat).reshape(devices, up_chunk, LANES))
        sent[:, down_rows:, :] = jnp.concatenate(ups, axis=1).astype(sent.dtype)


def adapter_terms(x, cot, recv):
    rows, width = x.shape
    blocks = rows // BLOCK
    steps = 8
    whole = pl.BlockSpec(recv.shape, lambda i: (0, 0, 0))
    return pl.pallas_call(
        adapter_kernel,
        grid=(steps,),
        in_specs=[
            pl.BlockSpec((rows, width // steps), lambda i: (0, i)),
            pl.BlockSpec(cot.shape, lambda i: (0, 0)),
            whole,
        ],
        out_specs=[whole, pl.BlockSpec((rows, LANES), lambda i: (0, 0))],
        out_shape=[
            jax.ShapeDtypeStruct(recv.shape, jnp.bfloat16),
            jax.ShapeDtypeStruct((rows, LANES), jnp.bfloat16),
        ],
        scratch_shapes=[
            pltpu.VMEM((blocks, BLOCK, ADAPTER_RANK), jnp.float32),
            pltpu.VMEM((blocks, ADAPTER_RANK, BLOCK), jnp.bfloat16),
        ],
        compiler_params=PARAMS,
        cost_estimate=SMALL,
        name="adapter_terms",
    )(x, cot, recv)


def zero_kernel(down, up, zeros, sems):
    zeros[...] = jnp.zeros_like(zeros)
    rows = zeros.shape[0]
    count = down.shape[0] // rows
    copies = []
    for i in range(count):
        part = pl.ds(i * rows, rows)
        copies.append(pltpu.make_async_copy(zeros, down.at[part, :], sems.at[2 * i]))
        copies.append(
            pltpu.make_async_copy(zeros.at[:, : up.shape[1]], up.at[part, :], sems.at[2 * i + 1])
        )
    for copy in copies:
        copy.start()
    for copy in copies:
        copy.wait()


def zero_grads(after, down_shape, up_shape):
    rows = 64
    count = down_shape[0] // rows

    def kernel(after, down, up, zeros, sems):
        zero_kernel(down, up, zeros, sems)

    return pl.pallas_call(
        kernel,
        in_specs=[pl.BlockSpec(memory_space=pl.ANY)],
        out_specs=[pl.BlockSpec(memory_space=pl.ANY)] * 2,
        out_shape=[
            jax.ShapeDtypeStruct(down_shape, jnp.float32),
            jax.ShapeDtypeStruct(up_shape, jnp.float32),
        ],
        scratch_shapes=[
            pltpu.VMEM((rows, down_shape[1]), jnp.float32),
            pltpu.SemaphoreType.DMA((2 * count,)),
        ],
        compiler_params=PARAMS,
        cost_estimate=SMALL,
        name="zero_grads",
    )(after)


def scatter_kernel(
    adapter, storage, recv, _down, _up, down, up, table, dacc, uacc, dscr, uscr, drow, urow, dsem, usem
):
    blocks = adapter.shape[0]
    devices = recv.shape[0]
    per_down, per_up = down.shape[1] // LANES, up.shape[1] // LANES
    down_rows = 2 * per_down

    def mark(i, carry):
        b = blocks - 1 - i
        table[storage[adapter[b]]] = b
        return carry

    lax.fori_loop(0, blocks, mark, 0)
    dacc[...] = jnp.zeros_like(dacc)
    uacc[...] = jnp.zeros_like(uacc)
    value = lane_cat([recv[:, q * ADAPTER_RANK : (q + 1) * ADAPTER_RANK, :] for q in range(8)])
    value = dot_n(value.reshape(devices * ADAPTER_RANK, 8 * LANES), rank_major_order(True))
    for j in range(devices):
        part = value[j * ADAPTER_RANK : (j + 1) * ADAPTER_RANK, :]
        turned = jnp.concatenate(
            [part[:, lo * LANES : (lo + 1) * LANES] for lo in range(8)], axis=0
        ).T
        narrow = recv[j, down_rows:, :].astype(jnp.float32)
        for k in range(2):
            first = table[storage[adapter[2 * j + k]]]
            dacc[first] += turned[k * per_down : (k + 1) * per_down, :]
            uacc[first] += narrow[k * per_up : (k + 1) * per_up, :]
    for g in range(blocks // 8):
        for i in range(8):
            dscr[pl.ds(i, per_down, stride=8), :] = dacc[8 * g + i]
            uscr[pl.ds(i, per_up, stride=8), :] = uacc[8 * g + i]
        for t in range(per_down):
            drow[8 * g : 8 * g + 8, t * LANES : (t + 1) * LANES] = dscr[8 * t : 8 * t + 8, :]
        for t in range(per_up):
            urow[8 * g : 8 * g + 8, t * LANES : (t + 1) * LANES] = uscr[8 * t : 8 * t + 8, :]

    def copies(b):
        slot = storage[adapter[b]]
        return (
            table[slot] == b,
            pltpu.make_async_copy(drow.at[pl.ds(b, 1), :], down.at[pl.ds(slot, 1), :], dsem.at[b]),
            pltpu.make_async_copy(urow.at[pl.ds(b, 1), :], up.at[pl.ds(slot, 1), :], usem.at[b]),
        )

    def begin(b, carry):
        mine, first, second = copies(b)

        @pl.when(mine)
        def _():
            first.start()
            second.start()

        return carry

    def end(b, carry):
        mine, first, second = copies(b)

        @pl.when(mine)
        def _():
            first.wait()
            second.wait()

        return carry

    lax.fori_loop(0, blocks, begin, 0)
    lax.fori_loop(0, blocks, end, 0)


def scatter_rows(padded_block_adapter, adapter_storage_row, recv, down, up):
    blocks = padded_block_adapter.shape[0]
    per_down, per_up = down.shape[1] // LANES, up.shape[1] // LANES
    return pl.pallas_call(
        scatter_kernel,
        grid_spec=pltpu.PrefetchScalarGridSpec(
            num_scalar_prefetch=2,
            grid=(1,),
            in_specs=[
                pl.BlockSpec(recv.shape, lambda i, *_: (0, 0, 0)),
                pl.BlockSpec(memory_space=pl.ANY),
                pl.BlockSpec(memory_space=pl.ANY),
            ],
            out_specs=[pl.BlockSpec(memory_space=pl.ANY)] * 2,
            scratch_shapes=[
                pltpu.SMEM((ADAPTER_GROUP,), jnp.int32),
                pltpu.VMEM((blocks, per_down, LANES), jnp.float32),
                pltpu.VMEM((blocks, per_up, LANES), jnp.float32),
                pltpu.VMEM((8 * per_down, LANES), jnp.float32),
                pltpu.VMEM((8 * per_up, LANES), jnp.float32),
                pltpu.VMEM((blocks, per_down * LANES), jnp.float32),
                pltpu.VMEM((blocks, per_up * LANES), jnp.float32),
                pltpu.SemaphoreType.DMA((blocks,)),
                pltpu.SemaphoreType.DMA((blocks,)),
            ],
        ),
        out_shape=[
            jax.ShapeDtypeStruct(down.shape, down.dtype),
            jax.ShapeDtypeStruct(up.shape, up.dtype),
        ],
        input_output_aliases={3: 0, 4: 1},
        compiler_params=PARAMS,
        cost_estimate=SMALL,
        name="scatter_rows",
    )(padded_block_adapter, adapter_storage_row, recv, down, up)


def far_kernel(cot, left, right, out):
    step = pl.program_id(0)
    half = pl.num_programs(0) // 2

    def part(weight):
        out[...] = dot_t(cot[...], weight[...]).astype(out.dtype)

    pl.when(step < half)(lambda: part(left))
    pl.when(step >= half)(lambda: part(right))


def far_product(cot, left, right):
    rows, depth = cot.shape
    width = left.shape[0]
    tile = 256
    per = width // tile
    return pl.pallas_call(
        far_kernel,
        grid=(2 * per,),
        in_specs=[
            pl.BlockSpec((rows, depth), lambda i: (0, 0)),
            pl.BlockSpec((tile, depth), lambda i: (jnp.minimum(i, per - 1), 0)),
            pl.BlockSpec((tile, depth), lambda i: (jnp.maximum(i - per, 0), 0)),
        ],
        out_specs=pl.BlockSpec((rows, tile), lambda i: (0, i)),
        out_shape=jax.ShapeDtypeStruct((rows, 2 * width), jnp.bfloat16),
        compiler_params=PARAMS,
        cost_estimate=SMALL,
        name="far_product",
    )(cot, left, right)


def low_rank_columns(index, per_device, g, recv, width):
    blocks = g.shape[0] // BLOCK
    per = per_device * width // LANES
    parts = []
    for k in range(blocks):
        first = (k * per + (index % per_device) * (width // LANES)) * ADAPTER_RANK
        a = lane_cat(
            [
                recv[0, pl.ds(pl.multiple_of(first + q * ADAPTER_RANK, ADAPTER_RANK), ADAPTER_RANK), :]
                for q in range(width // LANES)
            ]
        )
        parts.append(dot_n(g[k * BLOCK : (k + 1) * BLOCK, :ADAPTER_RANK], a))
    return adapter_scale * jnp.concatenate(parts, axis=0)


def own_columns(meta, at, cot, left, right, g, recv, out, width, columns):
    rows, depth = cot.shape
    span = left.shape[0]
    per_device = columns // span

    def kernel(meta, cot, left, right, g, recv, *rest):
        step = pl.program_id(0)
        result = rest[-1]
        lr = low_rank_columns(meta[at + step], per_device, g, recv, span)

        def part(weight):
            result[...] = (dot_t(cot[...], weight[...]) + lr).astype(result.dtype)

        pl.when(step == 0)(lambda: part(left))
        pl.when(step == 1)(lambda: part(right))

    return pl.pallas_call(
        kernel,
        grid_spec=pltpu.PrefetchScalarGridSpec(
            num_scalar_prefetch=1,
            grid=(2,),
            in_specs=[
                pl.BlockSpec((rows, depth), lambda j, m: (0, 0)),
                pl.BlockSpec((span, depth), lambda j, m: (0, 0)),
                pl.BlockSpec((span, depth), lambda j, m: (0, 0)),
                pl.BlockSpec((rows, LANES), lambda j, m: (0, 0)),
                pl.BlockSpec((1,) + recv.shape[1:], lambda j, m: (m[at + j] // per_device, 0, 0)),
            ]
            + ([] if out is None else [pl.BlockSpec(memory_space=pl.ANY)]),
            out_specs=pl.BlockSpec((rows, span), lambda j, m: (0, m[at + j])),
        ),
        out_shape=jax.ShapeDtypeStruct((rows, width), jnp.bfloat16),
        input_output_aliases={} if out is None else {6: 0},
        compiler_params=PARAMS,
        cost_estimate=SMALL,
        name="own_columns",
    )(meta, cot, left, right, g, recv, *([] if out is None else [out]))


def far_columns(meta, at, far, g, recv, out, columns):
    rows, both = far.shape
    span = both // 2
    per_device = columns // span

    def kernel(meta, far, g, recv, _, result):
        lr = low_rank_columns(meta[at + pl.program_id(0)], per_device, g, recv, span)
        result[...] = (far[...].astype(jnp.float32) + lr).astype(result.dtype)

    return pl.pallas_call(
        kernel,
        grid_spec=pltpu.PrefetchScalarGridSpec(
            num_scalar_prefetch=1,
            grid=(2,),
            in_specs=[
                pl.BlockSpec((rows, span), lambda j, m: (0, j)),
                pl.BlockSpec((rows, LANES), lambda j, m: (0, 0)),
                pl.BlockSpec((1,) + recv.shape[1:], lambda j, m: (m[at + j] // per_device, 0, 0)),
                pl.BlockSpec(memory_space=pl.ANY),
            ],
            out_specs=pl.BlockSpec((rows, span), lambda j, m: (0, m[at + j])),
        ),
        out_shape=jax.ShapeDtypeStruct(out.shape, out.dtype),
        input_output_aliases={4: 0},
        compiler_params=PARAMS,
        cost_estimate=SMALL,
        name="far_columns",
    )(meta, far, g, recv, out)


def ring_table(devices):
    chips = devices // 2
    order = list(range(0, chips, 2)) + list(range(chips - 1, 0, -2))
    place = {c: i for i, c in enumerate(order)}
    ring = []
    for c in range(chips):
        ring.append((2 * c, 2 * order[(place[c] + 1) % chips]))
        ring.append((2 * c + 1, 2 * order[(place[c] - 1) % chips] + 1))
    table = []
    for part in range(2):
        for index in range(devices):
            chip, core = index // 2, index % 2
            way = 2 * core - 1
            row = [2 * index, index, index ^ 1]
            for step in range(1, chips // 2):
                pair = [order[(place[chip] + sign * way * step) % chips] for sign in (1, -1)]
                row += [2 * c + part for c in pair] + [2 * c + 1 - part for c in pair]
            last = order[(place[chip] + chips // 2) % chips]
            row += [2 * (2 * last + part) + h for h in (core, 1 - core)]
            row += [2 * (2 * last + 1 - part) + h for h in (core, 1 - core)]
            table.append(row)
    return ring, np.array(table, np.int32)


def ring_body(
    inputs,
    cotangent,
    frozen_value_weight,
    adapter_down_weights,
    adapter_up_weights,
    padded_block_adapter,
    block_live_rows,
    adapter_storage_row,
    *,
    devices,
):
    chips = devices // 2
    shard = frozen_value_weight.shape[0]
    width = inputs.shape[1]
    index, part = lax.axis_index("fsdp"), lax.axis_index("parts")
    core = index % 2
    ring, table = ring_table(devices)
    meta = lax.dynamic_index_in_dim(jnp.asarray(table), part * devices + index, keepdims=False)
    cores = [(i, i ^ 1) for i in range(devices)]
    across = [(0, 1), (1, 0)]

    other_shard = lax.ppermute(frozen_value_weight, "fsdp", cores)
    masked = mask_rows(meta, block_live_rows, cotangent)
    far_masked = lax.ppermute(masked, "parts", across)
    travelling = jnp.where(part == core, frozen_value_weight, other_shard)

    adapter, travelling = after(padded_block_adapter, travelling)
    payload = gather_rows(
        adapter, adapter_storage_row, adapter_down_weights, adapter_up_weights, devices
    )
    recv = lax.all_to_all(payload, "fsdp", split_axis=0, concat_axis=0, tiled=True)

    pairs, fars = [], []
    previous = payload
    for step in range(chips // 2):
        if step == chips // 2 - 1:
            travelling = lax.dynamic_slice_in_dim(travelling, core * (shard // 2), shard // 2)
        travelling = lax.ppermute(travelling, "fsdp", ring)
        forwarded = lax.ppermute(travelling, "fsdp", cores)
        pairs.append((travelling, forwarded))
        product = far_product(far_masked, travelling, forwarded)
        fars.append(lax.ppermute(product, "parts", across))
        if step == 0:
            down, up = zero_grads(product, adapter_down_weights.shape, adapter_up_weights.shape)
            cot, _, _ = after(masked, product, down)
            sent, g = adapter_terms(inputs, cot, recv)
            grads = lax.all_to_all(sent, "fsdp", split_axis=0, concat_axis=0, tiled=True)

    out = own_columns(
        meta, 1, masked, frozen_value_weight, other_shard, g, recv, None, width, shard
    )
    for step in range(chips // 2):
        out = own_columns(meta, 3 + 4 * step, masked, *pairs[step], g, recv, out, width, shard)
        out = far_columns(meta, 5 + 4 * step, fars[step], g, recv, out, shard)
    down_grad, up_grad = scatter_rows(padded_block_adapter, adapter_storage_row, grads, down, up)
    return (out, down_grad, up_grad)


def after(value, *earlier):
    return lax.optimization_barrier((value,) + earlier)


def gather_body(
    inputs,
    cotangent,
    frozen_value_weight,
    adapter_down_weights,
    adapter_up_weights,
    padded_block_adapter,
    block_live_rows,
    adapter_storage_row,
):
    hidden_width = inputs.shape[1]
    kv_width = cotangent.shape[1]
    token_rows = inputs.shape[0]
    block_count = token_rows // BLOCK
    first_block = lax.axis_index("fsdp") * block_count
    live_rows = lax.dynamic_slice_in_dim(block_live_rows, first_block, block_count)
    positions = jnp.arange(BLOCK, dtype=jnp.int32)
    live_mask = positions[None, :] < live_rows[:, None]
    blocked_cot = cotangent.reshape(block_count, BLOCK, kv_width)
    masked_blocks = jnp.where(live_mask[:, :, None], blocked_cot, jnp.zeros_like(blocked_cot))
    masked = masked_blocks.reshape(token_rows, kv_width)
    block_storage_row = slot_lookup(padded_block_adapter, adapter_storage_row)
    down_weight_rows = jnp.take(adapter_down_weights, block_storage_row, axis=0)
    up_weight_rows = jnp.take(adapter_up_weights, block_storage_row, axis=0)
    down_mine, up_mine = (
        lax.all_to_all(down_weight_rows, "fsdp", split_axis=0, concat_axis=1, tiled=True),
        lax.all_to_all(up_weight_rows, "fsdp", split_axis=0, concat_axis=1, tiled=True),
    )
    frozen_gradient = lax.dot_general(
        masked,
        lax.all_gather(frozen_value_weight, "fsdp", axis=0, tiled=True),
        (((1,), (1,)), ((), ())),
        preferred_element_type=jnp.float32,
    )
    down_weight_matrix = down_mine.reshape(block_count, hidden_width, ADAPTER_RANK)
    up_weight_matrix = up_mine.reshape(block_count, ADAPTER_RANK, kv_width)
    blocked_in = inputs.reshape(block_count, BLOCK, hidden_width)
    rank_projection = jnp.einsum(
        "kbd,kdr->kbr", blocked_in, down_weight_matrix, preferred_element_type=jnp.float32
    ).astype(jnp.bfloat16)
    rank_space_gradient = jnp.einsum(
        "kbv,krv->kbr", masked_blocks, up_weight_matrix, preferred_element_type=jnp.float32
    ).astype(jnp.bfloat16)
    adapter_gradient_term = adapter_scale * jnp.einsum(
        "kbr,kdr->kbd", rank_space_gradient, down_weight_matrix, preferred_element_type=jnp.float32
    )
    input_gradient = (
        frozen_gradient + adapter_gradient_term.reshape(token_rows, hidden_width)
    ).astype(jnp.bfloat16)
    partial_down_weight = adapter_scale * jnp.einsum(
        "kbd,kbr->kdr", blocked_in, rank_space_gradient, preferred_element_type=jnp.float32
    )
    partial_up_weight = adapter_scale * jnp.einsum(
        "kbr,kbv->krv", rank_projection, masked_blocks, preferred_element_type=jnp.float32
    )
    partial_down_weight = partial_down_weight.reshape(block_count, hidden_width * ADAPTER_RANK)
    partial_up_weight = partial_up_weight.reshape(block_count, ADAPTER_RANK * kv_width)
    recv_down, recv_up = (
        lax.all_to_all(partial_down_weight, "fsdp", split_axis=1, concat_axis=0, tiled=True),
        lax.all_to_all(partial_up_weight, "fsdp", split_axis=1, concat_axis=0, tiled=True),
    )
    onehot = (
        jnp.arange(ADAPTER_GROUP, dtype=jnp.int32)[:, None] == block_storage_row[None, :]
    ).astype(jnp.float32)
    highest_precision = lax.Precision.HIGHEST
    down_grad = jnp.dot(
        onehot, recv_down, precision=highest_precision, preferred_element_type=jnp.float32
    )
    up_grad = jnp.dot(
        onehot, recv_up, precision=highest_precision, preferred_element_type=jnp.float32
    )
    return (input_gradient, down_grad, up_grad)


def solution(mesh):
    devices = mesh.shape["fsdp"]
    in_specs = (
        P(("parts", "fsdp"), None),
        P(("parts", "fsdp"), None),
        P("fsdp", None),
        P("parts", "fsdp"),
        P("parts", "fsdp"),
        P("parts"),
        P("parts"),
        P("parts"),
    )
    out_specs = (P(("parts", "fsdp"), None), P("parts", "fsdp"), P("parts", "fsdp"))

    def program(*arrays):
        shard = arrays[2].shape[0] // devices
        rows = arrays[0].shape[0] // devices // 2
        adapter_tiles = arrays[3].shape[1] // devices // LANES
        fits = rows == 2 * BLOCK and 2 * adapter_tiles == LANES and shard % 512 == 0
        if mesh.shape["parts"] == 2 and devices % 4 == 0 and fits:
            body = functools.partial(ring_body, devices=devices)
        else:
            body = gather_body
        return jax.shard_map(
            body, mesh=mesh, in_specs=in_specs, out_specs=out_specs, check_vma=False
        )(*arrays)

    return program
```

```python
import functools

import jax
import jax.numpy as jnp
import numpy as np
from jax import lax
from jax.experimental import pallas as pl
from jax.experimental.pallas import tpu as pltpu
from jax.sharding import PartitionSpec as P

ADAPTER_RANK = 16
ADAPTER_GROUP = 512
BLOCK = 128
LANES = 128
MIB = 1024 * 1024
ZERO_ROWS = 64
PARAMS = pltpu.CompilerParams(vmem_limit_bytes=16 * MIB)
WIDE_PARAMS = pltpu.CompilerParams(vmem_limit_bytes=24 * MIB)
IN_VMEM = pl.BlockSpec(memory_space=pltpu.VMEM)
IN_SMEM = pl.BlockSpec(memory_space=pltpu.SMEM)
IN_HBM = pl.BlockSpec(memory_space=pltpu.HBM)
SMALL = pl.CostEstimate(flops=1, bytes_accessed=1, transcendentals=0)

adapter_scale = 2.0


def slot_lookup(padded_block_adapter, adapter_storage_row):
    matches = padded_block_adapter[:, None] == jnp.arange(ADAPTER_GROUP, dtype=jnp.int32)[None, :]
    return jnp.sum(jnp.where(matches, adapter_storage_row[None, :], 0), axis=1)


def iota(shape, axis):
    return lax.broadcasted_iota(jnp.int32, shape, axis)


def dot_t(a, b):
    return lax.dot_general(a, b, (((1,), (1,)), ((), ())), preferred_element_type=jnp.float32)


def dot_n(a, b, precision=None):
    return lax.dot_general(
        a, b, (((1,), (0,)), ((), ())), precision=precision, preferred_element_type=jnp.float32
    )


def dot_0(a, b):
    return lax.dot_general(a, b, (((0,), (0,)), ((), ())), preferred_element_type=jnp.float32)


def lane_cat(parts):
    return jnp.concatenate(parts, axis=-1)


def mask_kernel(meta, live, cot, out):
    row = iota((BLOCK, cot.shape[1]), 0)
    for k in range(cot.shape[0] // BLOCK):
        rows = slice(k * BLOCK, (k + 1) * BLOCK)
        value = cot[rows, :].astype(jnp.float32)
        out[rows, :] = jnp.where(row < live[meta[0] + k], value, 0.0).astype(out.dtype)


def mask_rows(meta, block_live_rows, cotangent):
    return pl.pallas_call(
        mask_kernel,
        in_specs=[IN_SMEM, IN_SMEM, IN_VMEM],
        out_specs=IN_VMEM,
        out_shape=jax.ShapeDtypeStruct(cotangent.shape, cotangent.dtype),
        compiler_params=PARAMS,
        cost_estimate=SMALL,
        name="mask_rows",
    )(meta, block_live_rows, cotangent)


def rank_major_order(transposed):
    shape = (8 * LANES, 8 * LANES)
    near, far = (1, 0) if transposed else (0, 1)
    a, b = iota(shape, near), iota(shape, far)
    return ((a % LANES) * 8 + a // LANES == b).astype(jnp.bfloat16)


def zero_copies(zeros, target, sems, first, rows):
    part = zeros if target.shape[1] == zeros.shape[1] else zeros.at[:, : target.shape[1]]
    return [
        pltpu.make_async_copy(part, target.at[pl.ds(start, ZERO_ROWS), :], sems.at[i])
        for i, start in enumerate(range(first, first + rows, ZERO_ROWS))
    ]


def gather_kernel(
    adapter, storage, down, up, payload, grads, dbuf, ubuf, dscr, uscr, cols, zeros, dsem, usem, zsem
):
    blocks = adapter.shape[0]
    devices = payload.shape[0]
    group = dbuf.shape[1]
    per_down, per_up = down.shape[1] // LANES, up.shape[1] // LANES
    down_rows = 2 * per_down

    def copies(b):
        slot = storage[adapter[b]]
        start = pl.multiple_of((slot // group) * group, group)
        return (
            slot % group,
            pltpu.make_async_copy(down.at[pl.ds(start, group), :], dbuf.at[b], dsem.at[b]),
            pltpu.make_async_copy(up.at[pl.ds(start, group), :], ubuf.at[b], usem.at[b]),
        )

    def begin(b, carry):
        _, first, second = copies(b)
        first.start()
        second.start()
        return carry

    lax.fori_loop(0, blocks, begin, 0)
    zeros[...] = jnp.zeros_like(zeros)
    fills = zero_copies(zeros, grads, zsem, 0, grads.shape[0] // 2)
    for copy in fills:
        copy.start()
    order = rank_major_order(False)

    def one(j, carry):
        wide, narrow = [], []
        for k in range(2):
            b = 2 * j + k
            row, first, second = copies(b)
            first.wait()
            second.wait()
            late = row >= 8
            line = row % 8
            value = dbuf[b].astype(jnp.float32)
            value = jnp.where(late, value[8:], value[:8])
            for t in range(per_down):
                dscr[k, 8 * t : 8 * t + 8, :] = value[:, t * LANES : (t + 1) * LANES]
            wide.append(dscr[k, pl.ds(line, per_down, stride=8), :])
            value = ubuf[b].astype(jnp.float32)
            value = jnp.where(late, value[8:], value[:8])
            for t in range(per_up):
                uscr[k, 8 * t : 8 * t + 8, :] = value[:, t * LANES : (t + 1) * LANES]
            narrow.append(uscr[k, pl.ds(line, per_up, stride=8), :])
        turned = jnp.concatenate(wide, axis=0).T
        start = pl.multiple_of(j * ADAPTER_RANK, ADAPTER_RANK)
        for lo in range(8):
            piece = turned[lo * ADAPTER_RANK : (lo + 1) * ADAPTER_RANK, :]
            cols[pl.ds(start, ADAPTER_RANK), lo * LANES : (lo + 1) * LANES] = piece.astype(cols.dtype)
        payload[j, down_rows:, :] = jnp.concatenate(narrow, axis=0).astype(payload.dtype)
        return carry

    lax.fori_loop(0, devices, one, 0)
    result = dot_n(cols[...], order).astype(payload.dtype).reshape(devices, ADAPTER_RANK, 8 * LANES)
    for q in range(8):
        payload[:, q * ADAPTER_RANK : (q + 1) * ADAPTER_RANK, :] = result[
            :, :, q * LANES : (q + 1) * LANES
        ]
    for copy in fills:
        copy.wait()


def gather_rows(padded_block_adapter, adapter_storage_row, down, up, devices):
    blocks = padded_block_adapter.shape[0]
    per_down, per_up = down.shape[1] // LANES, up.shape[1] // LANES
    group = 16
    rows = 2 * (per_down + per_up)
    shape = (devices, rows, LANES)
    return pl.pallas_call(
        gather_kernel,
        in_specs=[IN_SMEM, IN_SMEM, IN_HBM, IN_HBM],
        out_specs=[IN_VMEM, IN_HBM],
        out_shape=[
            jax.ShapeDtypeStruct(shape, jnp.bfloat16),
            jax.ShapeDtypeStruct(down.shape, jnp.float32),
        ],
        scratch_shapes=[
            pltpu.VMEM((blocks, group, down.shape[1]), down.dtype),
            pltpu.VMEM((blocks, group, up.shape[1]), up.dtype),
            pltpu.VMEM((2, 8 * per_down, LANES), jnp.float32),
            pltpu.VMEM((2, 8 * per_up, LANES), jnp.float32),
            pltpu.VMEM((devices * ADAPTER_RANK, 8 * LANES), jnp.bfloat16),
            pltpu.VMEM((ZERO_ROWS, down.shape[1]), jnp.float32),
            pltpu.SemaphoreType.DMA((blocks,)),
            pltpu.SemaphoreType.DMA((blocks,)),
            pltpu.SemaphoreType.DMA((down.shape[0] // 2 // ZERO_ROWS,)),
        ],
        compiler_params=WIDE_PARAMS,
        cost_estimate=SMALL,
        name="gather_rows",
    )(padded_block_adapter, adapter_storage_row, down, up)


def adapter_kernel(x, cot, recv, _, sent, g_out, grads, up_grads, xbuf, zeros, xsem, zsem, usem):
    devices = recv.shape[0]
    blocks = x.shape[0] // BLOCK
    steps = xbuf.shape[0]
    span = xbuf.shape[2]
    tiles = cot.shape[1] // LANES
    up_chunk = tiles * ADAPTER_RANK // devices
    down_rows = recv.shape[1] - blocks * up_chunk
    per = down_rows // blocks // ADAPTER_RANK
    here = span // LANES // per

    loads = [
        pltpu.make_async_copy(x.at[:, i * span : (i + 1) * span], xbuf.at[i], xsem.at[i])
        for i in range(steps)
    ]
    for copy in loads:
        copy.start()
    zeros[...] = jnp.zeros_like(zeros)
    half = grads.shape[0] // 2
    fills = zero_copies(zeros, grads, zsem, half, half)
    fills += zero_copies(zeros, up_grads, usem, 0, up_grads.shape[0])
    for copy in fills:
        copy.start()

    lane = iota((BLOCK, LANES), 1)
    gather_rank = (iota((LANES, LANES), 0) // 8 == iota((LANES, LANES), 1)).astype(jnp.float32)
    b_all = recv[:, down_rows:, :].astype(jnp.float32)
    turned = []
    for k in range(blocks):
        m = cot[k * BLOCK : (k + 1) * BLOCK, :]
        b_flat = b_all[:, k * up_chunk : (k + 1) * up_chunk, :].reshape(LANES, LANES)
        b_flat = b_flat.astype(jnp.bfloat16)
        total = jnp.zeros((BLOCK, LANES), jnp.float32)
        for t in range(tiles):
            part = dot_t(m[:, t * LANES : (t + 1) * LANES], b_flat)
            total = total + jnp.where(lane % tiles == t, part, 0.0)
        g = dot_n(total, gather_rank, lax.Precision.HIGHEST).astype(jnp.bfloat16)
        g_out[k * BLOCK : (k + 1) * BLOCK, :] = g
        turned.append(g.astype(jnp.float32).T[:ADAPTER_RANK, :].astype(jnp.bfloat16))

    lows = [jnp.zeros((BLOCK, ADAPTER_RANK), jnp.float32) for _ in range(blocks)]
    for i in range(steps):
        loads[i].wait()
        for k in range(blocks):
            part = xbuf[i, k * BLOCK : (k + 1) * BLOCK, :]
            first = k * per * ADAPTER_RANK
            spots = [
                (i * here + j, first + q * ADAPTER_RANK) for j in range(here) for q in range(per)
            ]
            a = lane_cat([recv[j, at : at + ADAPTER_RANK, :] for j, at in spots])
            lows[k] = lows[k] + dot_t(part, a)
            grad = (adapter_scale * dot_n(turned[k], part)).astype(sent.dtype)
            for tile, (j, at) in enumerate(spots):
                sent[j, at : at + ADAPTER_RANK, :] = grad[:, tile * LANES : (tile + 1) * LANES]

    ups = []
    row = iota((LANES, LANES), 0)
    spread = (iota((ADAPTER_RANK, LANES), 1) // 8 == iota((ADAPTER_RANK, LANES), 0)).astype(
        jnp.bfloat16
    )
    for k in range(blocks):
        low8 = dot_n(lows[k].astype(jnp.bfloat16), spread).astype(jnp.bfloat16)
        up = dot_0(low8, cot[k * BLOCK : (k + 1) * BLOCK, :])
        flat = jnp.zeros((LANES, LANES), jnp.float32)
        for t in range(tiles):
            flat = flat + jnp.where(row % tiles == t, up[:, t * LANES : (t + 1) * LANES], 0.0)
        ups.append((adapter_scale * flat).reshape(devices, up_chunk, LANES))
    sent[:, down_rows:, :] = jnp.concatenate(ups, axis=1).astype(sent.dtype)
    for copy in fills:
        copy.wait()


def adapter_terms(x, cot, recv, grads, up_shape):
    rows, width = x.shape
    steps = 8
    return pl.pallas_call(
        adapter_kernel,
        in_specs=[IN_HBM, IN_VMEM, IN_VMEM, IN_HBM],
        out_specs=[IN_VMEM, IN_VMEM, IN_HBM, IN_HBM],
        out_shape=[
            jax.ShapeDtypeStruct(recv.shape, jnp.bfloat16),
            jax.ShapeDtypeStruct((rows, LANES), jnp.bfloat16),
            jax.ShapeDtypeStruct(grads.shape, grads.dtype),
            jax.ShapeDtypeStruct(up_shape, jnp.float32),
        ],
        input_output_aliases={3: 2},
        scratch_shapes=[
            pltpu.VMEM((steps, rows, width // steps), x.dtype),
            pltpu.VMEM((ZERO_ROWS, grads.shape[1]), jnp.float32),
            pltpu.SemaphoreType.DMA((steps,)),
            pltpu.SemaphoreType.DMA((grads.shape[0] // 2 // ZERO_ROWS,)),
            pltpu.SemaphoreType.DMA((up_shape[0] // ZERO_ROWS,)),
        ],
        compiler_params=PARAMS,
        cost_estimate=SMALL,
        name="adapter_terms",
    )(x, cot, recv, grads)


def scatter_kernel(
    adapter, storage, recv, _down, _up, down, up, table, dacc, uacc, dscr, uscr, drow, urow, dsem, usem
):
    blocks = adapter.shape[0]
    devices = recv.shape[0]
    per_down, per_up = down.shape[1] // LANES, up.shape[1] // LANES
    down_rows = 2 * per_down

    def mark(i, carry):
        b = blocks - 1 - i
        table[storage[adapter[b]]] = b
        return carry

    lax.fori_loop(0, blocks, mark, 0)
    dacc[...] = jnp.zeros_like(dacc)
    uacc[...] = jnp.zeros_like(uacc)
    value = lane_cat([recv[:, q * ADAPTER_RANK : (q + 1) * ADAPTER_RANK, :] for q in range(8)])
    value = dot_n(value.reshape(devices * ADAPTER_RANK, 8 * LANES), rank_major_order(True))
    for j in range(devices):
        part = value[j * ADAPTER_RANK : (j + 1) * ADAPTER_RANK, :]
        turned = jnp.concatenate(
            [part[:, lo * LANES : (lo + 1) * LANES] for lo in range(8)], axis=0
        ).T
        narrow = recv[j, down_rows:, :].astype(jnp.float32)
        for k in range(2):
            first = table[storage[adapter[2 * j + k]]]
            dacc[first] += turned[k * per_down : (k + 1) * per_down, :]
            uacc[first] += narrow[k * per_up : (k + 1) * per_up, :]
    for g in range(blocks // 8):
        for i in range(8):
            dscr[pl.ds(i, per_down, stride=8), :] = dacc[8 * g + i]
            uscr[pl.ds(i, per_up, stride=8), :] = uacc[8 * g + i]
        for t in range(per_down):
            drow[8 * g : 8 * g + 8, t * LANES : (t + 1) * LANES] = dscr[8 * t : 8 * t + 8, :]
        for t in range(per_up):
            urow[8 * g : 8 * g + 8, t * LANES : (t + 1) * LANES] = uscr[8 * t : 8 * t + 8, :]

    def copies(b):
        slot = storage[adapter[b]]
        return (
            table[slot] == b,
            pltpu.make_async_copy(drow.at[pl.ds(b, 1), :], down.at[pl.ds(slot, 1), :], dsem.at[b]),
            pltpu.make_async_copy(urow.at[pl.ds(b, 1), :], up.at[pl.ds(slot, 1), :], usem.at[b]),
        )

    def begin(b, carry):
        mine, first, second = copies(b)

        @pl.when(mine)
        def _():
            first.start()
            second.start()

        return carry

    def end(b, carry):
        mine, first, second = copies(b)

        @pl.when(mine)
        def _():
            first.wait()
            second.wait()

        return carry

    lax.fori_loop(0, blocks, begin, 0)
    lax.fori_loop(0, blocks, end, 0)


def scatter_rows(padded_block_adapter, adapter_storage_row, recv, down, up):
    blocks = padded_block_adapter.shape[0]
    per_down, per_up = down.shape[1] // LANES, up.shape[1] // LANES
    return pl.pallas_call(
        scatter_kernel,
        in_specs=[IN_SMEM, IN_SMEM, IN_VMEM, IN_HBM, IN_HBM],
        out_specs=[IN_HBM, IN_HBM],
        scratch_shapes=[
            pltpu.SMEM((ADAPTER_GROUP,), jnp.int32),
            pltpu.VMEM((blocks, per_down, LANES), jnp.float32),
            pltpu.VMEM((blocks, per_up, LANES), jnp.float32),
            pltpu.VMEM((8 * per_down, LANES), jnp.float32),
            pltpu.VMEM((8 * per_up, LANES), jnp.float32),
            pltpu.VMEM((blocks, per_down * LANES), jnp.float32),
            pltpu.VMEM((blocks, per_up * LANES), jnp.float32),
            pltpu.SemaphoreType.DMA((blocks,)),
            pltpu.SemaphoreType.DMA((blocks,)),
        ],
        out_shape=[
            jax.ShapeDtypeStruct(down.shape, down.dtype),
            jax.ShapeDtypeStruct(up.shape, up.dtype),
        ],
        input_output_aliases={3: 0, 4: 1},
        compiler_params=PARAMS,
        cost_estimate=SMALL,
        name="scatter_rows",
    )(padded_block_adapter, adapter_storage_row, recv, down, up)


def far_kernel(count, *refs):
    weight = refs[count][...]
    for cot, out in zip(refs[:count], refs[count + 1 :]):
        out[...] = dot_t(cot[...], weight).astype(out.dtype)


def far_products(cots, weight):
    shape = jax.ShapeDtypeStruct((cots[0].shape[0], weight.shape[0]), jnp.bfloat16)
    return pl.pallas_call(
        functools.partial(far_kernel, len(cots)),
        in_specs=[IN_VMEM] * (len(cots) + 1),
        out_specs=[IN_VMEM] * len(cots),
        out_shape=[shape] * len(cots),
        compiler_params=PARAMS,
        cost_estimate=SMALL,
        name="far_products",
    )(*cots, weight)


def finish(meta, at, cot, weights, received, g, recv, out, width, columns):
    rows = cot.shape[0]
    span = weights[0].shape[0] if weights else received[0].shape[1]
    per_device = columns // span
    count = len(weights) + len(received)
    per = columns // LANES

    def kernel(meta, cot, g, recv, *rest):
        sources = rest[:count]
        result, buffer, sems = rest[-3:]
        copies = []
        for i in range(count):
            index = meta[at + i]
            device, inner = index // per_device, (index % per_device) * (span // LANES)
            parts = []
            for k in range(rows // BLOCK):
                tiles = []
                for q in range(span // LANES):
                    first = pl.multiple_of((k * per + inner + q) * ADAPTER_RANK, ADAPTER_RANK)
                    tiles.append(recv[device, pl.ds(first, ADAPTER_RANK), :])
                ours = g[k * BLOCK : (k + 1) * BLOCK, :ADAPTER_RANK]
                parts.append(dot_n(ours, lane_cat(tiles)))
            value = adapter_scale * jnp.concatenate(parts, axis=0)
            if i < len(weights):
                value = value + dot_t(cot[...], sources[i][...])
            else:
                value = value + sources[i][...].astype(jnp.float32)
            buffer[i] = value.astype(buffer.dtype)
            start = pl.multiple_of(index * span, span)
            copies.append(
                pltpu.make_async_copy(buffer.at[i], result.at[:, pl.ds(start, span)], sems.at[i])
            )
            copies[-1].start()
        for copy in copies:
            copy.wait()

    return pl.pallas_call(
        kernel,
        in_specs=[IN_SMEM] + [IN_VMEM] * (3 + count) + ([] if out is None else [IN_HBM]),
        out_specs=IN_HBM,
        out_shape=jax.ShapeDtypeStruct((rows, width), jnp.bfloat16),
        input_output_aliases={} if out is None else {4 + count: 0},
        scratch_shapes=[
            pltpu.VMEM((count, rows, span), jnp.bfloat16),
            pltpu.SemaphoreType.DMA((count,)),
        ],
        compiler_params=PARAMS,
        cost_estimate=SMALL,
        name="finish",
    )(meta, cot, g, recv, *weights, *received, *([] if out is None else [out]))


def ring_table(devices):
    chips = devices // 2
    order = list(range(0, chips, 2)) + list(range(chips - 1, 0, -2))
    place = {c: i for i, c in enumerate(order)}
    ring = []
    for c in range(chips):
        ring.append((2 * c, 2 * order[(place[c] + 1) % chips]))
        ring.append((2 * c + 1, 2 * order[(place[c] - 1) % chips] + 1))
    table = []
    for part in range(2):
        for index in range(devices):
            chip, core = index // 2, index % 2
            way = 2 * core - 1
            row = [2 * index, index, index ^ 1]
            for step in range(1, chips // 2):
                near, far = [order[(place[chip] + sign * way * step) % chips] for sign in (1, -1)]
                row += [2 * near + part, 2 * far + part, 2 * near + 1 - part, 2 * far + 1 - part]
            last = order[(place[chip] + chips // 2) % chips]
            for p in (part, 1 - part):
                row += [2 * (2 * last + p) + core, 2 * (2 * last + p) + 1 - core]
            table.append(row)
    return ring, np.array(table, np.int32)


def ring_body(
    inputs,
    cotangent,
    frozen_value_weight,
    adapter_down_weights,
    adapter_up_weights,
    padded_block_adapter,
    block_live_rows,
    adapter_storage_row,
    *,
    devices,
):
    steps = devices // 4
    shard = frozen_value_weight.shape[0]
    width = inputs.shape[1]
    index, part = lax.axis_index("fsdp"), lax.axis_index("parts")
    core = index % 2
    ring, table = ring_table(devices)
    meta = lax.dynamic_index_in_dim(jnp.asarray(table), part * devices + index, keepdims=False)
    cores = [(i, i ^ 1) for i in range(devices)]
    across = [(0, 1), (1, 0)]
    diagonal = [(p * devices + i, (1 - p) * devices + (i ^ 1)) for p in range(2) for i in range(devices)]

    def cross(products):
        return (
            lax.ppermute(products[0], "fsdp", cores),
            lax.ppermute(products[1], "parts", across),
            lax.ppermute(products[2], ("parts", "fsdp"), diagonal),
        )

    other_shard = lax.ppermute(frozen_value_weight, "fsdp", cores)
    masked = mask_rows(meta, block_live_rows, cotangent)
    core_masked = lax.ppermute(masked, "fsdp", cores)
    far_masked = lax.ppermute(masked, "parts", across)
    diagonal_masked = lax.ppermute(far_masked, "fsdp", cores)
    adapter, _ = after(padded_block_adapter, masked)
    payload, grads = gather_rows(
        adapter, adapter_storage_row, adapter_down_weights, adapter_up_weights, devices
    )
    shards, _ = after((frozen_value_weight, other_shard), payload)
    travelling = jnp.where(part == core, *shards)
    recv = lax.all_to_all(payload, "fsdp", split_axis=0, concat_axis=0, tiled=True)

    pieces, received = [], []
    placed = payload
    out = None
    for step in range(steps):
        travelling, _ = after(travelling, placed)
        if step == steps - 1:
            travelling = lax.dynamic_slice_in_dim(travelling, core * (shard // 2), shard // 2)
        travelling = lax.ppermute(travelling, "fsdp", ring)
        placed = payload if out is None else out
        pieces.append(travelling)
        cots = (core_masked, far_masked, diagonal_masked)
        if step > 0:
            cots, _ = after(cots, out)
        products = far_products(cots, travelling)
        received.append(cross(products))
        if step == 0:
            new, _ = after(recv, products[0])
            sent, g, grads, up_grads = adapter_terms(
                inputs, masked, new, grads, adapter_up_weights.shape
            )
            sums = lax.all_to_all(sent, "fsdp", split_axis=0, concat_axis=0, tiled=True)
            out = finish(
                meta, 1, masked, shards, (), g, recv, None, width, shard
            )
        else:
            out, _ = after(out, products[0])
            at = 4 * step - 1
            out = finish(
                meta, at, masked, pieces[step - 1 : step], received[step - 1], g, recv, out, width, shard
            )
        if step == 1:
            sums, _ = after(sums, out)
            down_grad, up_grad = scatter_rows(
                padded_block_adapter, adapter_storage_row, sums, grads, up_grads
            )
    at = 4 * steps - 1
    out = finish(meta, at, masked, pieces[-1:], (), g, recv, out, width, shard)
    out = finish(meta, at + 1, masked, (), received[-1], g, recv, out, width, shard)
    return (out, down_grad, up_grad)


def after(value, *earlier):
    return lax.optimization_barrier((value,) + earlier)


def gather_body(
    inputs,
    cotangent,
    frozen_value_weight,
    adapter_down_weights,
    adapter_up_weights,
    padded_block_adapter,
    block_live_rows,
    adapter_storage_row,
):
    hidden_width = inputs.shape[1]
    kv_width = cotangent.shape[1]
    token_rows = inputs.shape[0]
    block_count = token_rows // BLOCK
    first_block = lax.axis_index("fsdp") * block_count
    live_rows = lax.dynamic_slice_in_dim(block_live_rows, first_block, block_count)
    positions = jnp.arange(BLOCK, dtype=jnp.int32)
    live_mask = positions[None, :] < live_rows[:, None]
    blocked_cot = cotangent.reshape(block_count, BLOCK, kv_width)
    masked_blocks = jnp.where(live_mask[:, :, None], blocked_cot, jnp.zeros_like(blocked_cot))
    masked = masked_blocks.reshape(token_rows, kv_width)
    block_storage_row = slot_lookup(padded_block_adapter, adapter_storage_row)
    down_weight_rows = jnp.take(adapter_down_weights, block_storage_row, axis=0)
    up_weight_rows = jnp.take(adapter_up_weights, block_storage_row, axis=0)
    down_mine, up_mine = (
        lax.all_to_all(down_weight_rows, "fsdp", split_axis=0, concat_axis=1, tiled=True),
        lax.all_to_all(up_weight_rows, "fsdp", split_axis=0, concat_axis=1, tiled=True),
    )
    frozen_gradient = lax.dot_general(
        masked,
        lax.all_gather(frozen_value_weight, "fsdp", axis=0, tiled=True),
        (((1,), (1,)), ((), ())),
        preferred_element_type=jnp.float32,
    )
    down_weight_matrix = down_mine.reshape(block_count, hidden_width, ADAPTER_RANK)
    up_weight_matrix = up_mine.reshape(block_count, ADAPTER_RANK, kv_width)
    blocked_in = inputs.reshape(block_count, BLOCK, hidden_width)
    rank_projection = jnp.einsum(
        "kbd,kdr->kbr", blocked_in, down_weight_matrix, preferred_element_type=jnp.float32
    ).astype(jnp.bfloat16)
    rank_space_gradient = jnp.einsum(
        "kbv,krv->kbr", masked_blocks, up_weight_matrix, preferred_element_type=jnp.float32
    ).astype(jnp.bfloat16)
    adapter_gradient_term = adapter_scale * jnp.einsum(
        "kbr,kdr->kbd", rank_space_gradient, down_weight_matrix, preferred_element_type=jnp.float32
    )
    input_gradient = (
        frozen_gradient + adapter_gradient_term.reshape(token_rows, hidden_width)
    ).astype(jnp.bfloat16)
    partial_down_weight = adapter_scale * jnp.einsum(
        "kbd,kbr->kdr", blocked_in, rank_space_gradient, preferred_element_type=jnp.float32
    )
    partial_up_weight = adapter_scale * jnp.einsum(
        "kbr,kbv->krv", rank_projection, masked_blocks, preferred_element_type=jnp.float32
    )
    partial_down_weight = partial_down_weight.reshape(block_count, hidden_width * ADAPTER_RANK)
    partial_up_weight = partial_up_weight.reshape(block_count, ADAPTER_RANK * kv_width)
    recv_down, recv_up = (
        lax.all_to_all(partial_down_weight, "fsdp", split_axis=1, concat_axis=0, tiled=True),
        lax.all_to_all(partial_up_weight, "fsdp", split_axis=1, concat_axis=0, tiled=True),
    )
    onehot = (
        jnp.arange(ADAPTER_GROUP, dtype=jnp.int32)[:, None] == block_storage_row[None, :]
    ).astype(jnp.float32)
    highest_precision = lax.Precision.HIGHEST
    down_grad = jnp.dot(
        onehot, recv_down, precision=highest_precision, preferred_element_type=jnp.float32
    )
    up_grad = jnp.dot(
        onehot, recv_up, precision=highest_precision, preferred_element_type=jnp.float32
    )
    return (input_gradient, down_grad, up_grad)


def solution(mesh):
    devices = mesh.shape["fsdp"]
    in_specs = (
        P(("parts", "fsdp"), None),
        P(("parts", "fsdp"), None),
        P("fsdp", None),
        P("parts", "fsdp"),
        P("parts", "fsdp"),
        P("parts"),
        P("parts"),
        P("parts"),
    )
    out_specs = (P(("parts", "fsdp"), None), P("parts", "fsdp"), P("parts", "fsdp"))

    def program(*arrays):
        shard = arrays[2].shape[0] // devices
        rows = arrays[0].shape[0] // devices // 2
        adapter_tiles = arrays[3].shape[1] // devices // LANES
        fits = rows == 2 * BLOCK and 2 * adapter_tiles == LANES and shard % 512 == 0
        if mesh.shape["parts"] == 2 and devices % 4 == 0 and fits:
            body = functools.partial(ring_body, devices=devices)
        else:
            body = gather_body
        return jax.shard_map(
            body, mesh=mesh, in_specs=in_specs, out_specs=out_specs, check_vma=False
        )(*arrays)

    return program
```

```python
import functools

import jax
import jax.numpy as jnp
import numpy as np
from jax import lax
from jax.experimental import pallas as pl
from jax.experimental.pallas import tpu as pltpu
from jax.sharding import PartitionSpec as P

ADAPTER_RANK = 16
ADAPTER_GROUP = 512
BLOCK = 128
LANES = 128
MIB = 1024 * 1024
ZERO_ROWS = 64
PARAMS = pltpu.CompilerParams(vmem_limit_bytes=16 * MIB)
WIDE_PARAMS = pltpu.CompilerParams(vmem_limit_bytes=24 * MIB)
IN_VMEM = pl.BlockSpec(memory_space=pltpu.VMEM)
IN_SMEM = pl.BlockSpec(memory_space=pltpu.SMEM)
IN_HBM = pl.BlockSpec(memory_space=pltpu.HBM)
SMALL = pl.CostEstimate(flops=1, bytes_accessed=1, transcendentals=0)

adapter_scale = 2.0


def slot_lookup(padded_block_adapter, adapter_storage_row):
    matches = padded_block_adapter[:, None] == jnp.arange(ADAPTER_GROUP, dtype=jnp.int32)[None, :]
    return jnp.sum(jnp.where(matches, adapter_storage_row[None, :], 0), axis=1)


def in_hbm(value):
    return pltpu.with_memory_space_constraint(value, pltpu.HBM)


def table_row(table):
    return lax.axis_index("parts") * (table.shape[0] // 2) + lax.axis_index("fsdp")


def iota(shape, axis):
    return lax.broadcasted_iota(jnp.int32, shape, axis)


def dot_t(a, b):
    return lax.dot_general(a, b, (((1,), (1,)), ((), ())), preferred_element_type=jnp.float32)


def dot_n(a, b, precision=None):
    return lax.dot_general(
        a, b, (((1,), (0,)), ((), ())), precision=precision, preferred_element_type=jnp.float32
    )


def dot_0(a, b):
    return lax.dot_general(a, b, (((0,), (0,)), ((), ())), preferred_element_type=jnp.float32)


def lane_cat(parts):
    return jnp.concatenate(parts, axis=-1)


def mask_kernel(table, live, cot, out):
    first = table[table_row(table), 0]
    row = iota((BLOCK, cot.shape[1]), 0)
    for k in range(cot.shape[0] // BLOCK):
        rows = slice(k * BLOCK, (k + 1) * BLOCK)
        value = cot[rows, :].astype(jnp.float32)
        out[rows, :] = jnp.where(row < live[first + k], value, 0.0).astype(out.dtype)


def mask_rows(table, block_live_rows, cotangent):
    return pl.pallas_call(
        mask_kernel,
        in_specs=[IN_SMEM, IN_SMEM, IN_VMEM],
        out_specs=IN_VMEM,
        out_shape=jax.ShapeDtypeStruct(cotangent.shape, cotangent.dtype),
        compiler_params=PARAMS,
        cost_estimate=SMALL,
        name="mask_rows",
    )(in_hbm(table), in_hbm(block_live_rows), in_hbm(cotangent))


def rank_major_order(transposed):
    shape = (8 * LANES, 8 * LANES)
    near, far = (1, 0) if transposed else (0, 1)
    a, b = iota(shape, near), iota(shape, far)
    return ((a % LANES) * 8 + a // LANES == b).astype(jnp.bfloat16)


def gather_kernel(
    adapter, storage, down, up, result, dbuf, ubuf, dscr, uscr, cols, payload, dsem, usem, rsem
):
    blocks = adapter.shape[0]
    devices = result.shape[0]
    group = dbuf.shape[1]
    per_down, per_up = down.shape[1] // LANES, up.shape[1] // LANES
    down_rows = 2 * per_down

    def copies(b):
        slot = storage[adapter[b]]
        start = pl.multiple_of((slot // group) * group, group)
        return (
            slot % group,
            pltpu.make_async_copy(down.at[pl.ds(start, group), :], dbuf.at[b], dsem.at[b]),
            pltpu.make_async_copy(up.at[pl.ds(start, group), :], ubuf.at[b], usem.at[b]),
        )

    def begin(b, carry):
        _, first, second = copies(b)
        first.start()
        second.start()
        return carry

    lax.fori_loop(0, blocks, begin, 0)
    order = rank_major_order(False)

    def one(j, carry):
        wide, narrow = [], []
        for k in range(2):
            b = 2 * j + k
            row, first, second = copies(b)
            first.wait()
            second.wait()
            late = row >= 8
            line = row % 8
            value = dbuf[b].astype(jnp.float32)
            value = jnp.where(late, value[8:], value[:8])
            for t in range(per_down):
                dscr[k, 8 * t : 8 * t + 8, :] = value[:, t * LANES : (t + 1) * LANES]
            wide.append(dscr[k, pl.ds(line, per_down, stride=8), :])
            value = ubuf[b].astype(jnp.float32)
            value = jnp.where(late, value[8:], value[:8])
            for t in range(per_up):
                uscr[k, 8 * t : 8 * t + 8, :] = value[:, t * LANES : (t + 1) * LANES]
            narrow.append(uscr[k, pl.ds(line, per_up, stride=8), :])
        turned = jnp.concatenate(wide, axis=0).T
        start = pl.multiple_of(j * ADAPTER_RANK, ADAPTER_RANK)
        for lo in range(8):
            piece = turned[lo * ADAPTER_RANK : (lo + 1) * ADAPTER_RANK, :]
            cols[pl.ds(start, ADAPTER_RANK), lo * LANES : (lo + 1) * LANES] = piece.astype(cols.dtype)
        payload[j, down_rows:, :] = jnp.concatenate(narrow, axis=0).astype(payload.dtype)
        return carry

    lax.fori_loop(0, devices, one, 0)
    value = dot_n(cols[...], order).astype(payload.dtype).reshape(devices, ADAPTER_RANK, 8 * LANES)
    for q in range(8):
        payload[:, q * ADAPTER_RANK : (q + 1) * ADAPTER_RANK, :] = value[
            :, :, q * LANES : (q + 1) * LANES
        ]
    copy = pltpu.make_async_copy(payload, result, rsem)
    copy.start()
    copy.wait()


def gather_rows(padded_block_adapter, adapter_storage_row, down, up, devices):
    blocks = padded_block_adapter.shape[0]
    per_down, per_up = down.shape[1] // LANES, up.shape[1] // LANES
    group = 16
    rows = 2 * (per_down + per_up)
    shape = (devices, rows, LANES)
    return pl.pallas_call(
        gather_kernel,
        in_specs=[IN_SMEM, IN_SMEM, IN_HBM, IN_HBM],
        out_specs=IN_HBM,
        out_shape=jax.ShapeDtypeStruct(shape, jnp.bfloat16),
        scratch_shapes=[
            pltpu.VMEM((blocks, group, down.shape[1]), down.dtype),
            pltpu.VMEM((blocks, group, up.shape[1]), up.dtype),
            pltpu.VMEM((2, 8 * per_down, LANES), jnp.float32),
            pltpu.VMEM((2, 8 * per_up, LANES), jnp.float32),
            pltpu.VMEM((devices * ADAPTER_RANK, 8 * LANES), jnp.bfloat16),
            pltpu.VMEM(shape, jnp.bfloat16),
            pltpu.SemaphoreType.DMA((blocks,)),
            pltpu.SemaphoreType.DMA((blocks,)),
            pltpu.SemaphoreType.DMA,
        ],
        compiler_params=WIDE_PARAMS,
        cost_estimate=SMALL,
        name="gather_rows",
    )(in_hbm(padded_block_adapter), in_hbm(adapter_storage_row), in_hbm(down), in_hbm(up))


def adapter_kernel(x, cot, recv, result, g_out, xbuf, sent, xsem, rsem):
    devices = recv.shape[0]
    blocks = x.shape[0] // BLOCK
    steps = xbuf.shape[0]
    span = xbuf.shape[2]
    tiles = cot.shape[1] // LANES
    up_chunk = tiles * ADAPTER_RANK // devices
    down_rows = recv.shape[1] - blocks * up_chunk
    per = down_rows // blocks // ADAPTER_RANK
    here = span // LANES // per

    loads = [
        pltpu.make_async_copy(x.at[:, i * span : (i + 1) * span], xbuf.at[i], xsem.at[i])
        for i in range(steps)
    ]
    for copy in loads:
        copy.start()
    lane = iota((BLOCK, LANES), 1)
    gather_rank = (iota((LANES, LANES), 0) // 8 == iota((LANES, LANES), 1)).astype(jnp.float32)
    b_all = recv[:, down_rows:, :].astype(jnp.float32)
    turned = []
    for k in range(blocks):
        m = cot[k * BLOCK : (k + 1) * BLOCK, :]
        b_flat = b_all[:, k * up_chunk : (k + 1) * up_chunk, :].reshape(LANES, LANES)
        b_flat = b_flat.astype(jnp.bfloat16)
        total = jnp.zeros((BLOCK, LANES), jnp.float32)
        for t in range(tiles):
            part = dot_t(m[:, t * LANES : (t + 1) * LANES], b_flat)
            total = total + jnp.where(lane % tiles == t, part, 0.0)
        g = dot_n(total, gather_rank, lax.Precision.HIGHEST).astype(jnp.bfloat16)
        g_out[k * BLOCK : (k + 1) * BLOCK, :] = g
        turned.append(g.astype(jnp.float32).T[:ADAPTER_RANK, :].astype(jnp.bfloat16))

    stores = []
    lows = [jnp.zeros((BLOCK, ADAPTER_RANK), jnp.float32) for _ in range(blocks)]
    for i in range(steps):
        loads[i].wait()
        for k in range(blocks):
            part = xbuf[i, k * BLOCK : (k + 1) * BLOCK, :]
            first = k * per * ADAPTER_RANK
            spots = [
                (i * here + j, first + q * ADAPTER_RANK) for j in range(here) for q in range(per)
            ]
            a = lane_cat([recv[j, at : at + ADAPTER_RANK, :] for j, at in spots])
            lows[k] = lows[k] + dot_t(part, a)
            grad = (adapter_scale * dot_n(turned[k], part)).astype(sent.dtype)
            for tile, (j, at) in enumerate(spots):
                sent[j, at : at + ADAPTER_RANK, :] = grad[:, tile * LANES : (tile + 1) * LANES]
        part = (pl.ds(i * here, here), pl.ds(0, down_rows), slice(None))
        stores.append(pltpu.make_async_copy(sent.at[part], result.at[part], rsem.at[i]))
        stores[-1].start()

    ups = []
    row = iota((LANES, LANES), 0)
    spread = (iota((ADAPTER_RANK, LANES), 1) // 8 == iota((ADAPTER_RANK, LANES), 0)).astype(
        jnp.bfloat16
    )
    for k in range(blocks):
        low8 = dot_n(lows[k].astype(jnp.bfloat16), spread).astype(jnp.bfloat16)
        up = dot_0(low8, cot[k * BLOCK : (k + 1) * BLOCK, :])
        flat = jnp.zeros((LANES, LANES), jnp.float32)
        for t in range(tiles):
            flat = flat + jnp.where(row % tiles == t, up[:, t * LANES : (t + 1) * LANES], 0.0)
        ups.append((adapter_scale * flat).reshape(devices, up_chunk, LANES))
    sent[:, down_rows:, :] = jnp.concatenate(ups, axis=1).astype(sent.dtype)
    part = (slice(None), pl.ds(down_rows, sent.shape[1] - down_rows), slice(None))
    stores.append(pltpu.make_async_copy(sent.at[part], result.at[part], rsem.at[steps]))
    stores[-1].start()
    for copy in stores:
        copy.wait()


def adapter_terms(x, cot, recv):
    rows, width = x.shape
    steps = 8
    return pl.pallas_call(
        adapter_kernel,
        in_specs=[IN_HBM, IN_VMEM, IN_VMEM],
        out_specs=[IN_HBM, IN_VMEM],
        out_shape=[
            jax.ShapeDtypeStruct(recv.shape, jnp.bfloat16),
            jax.ShapeDtypeStruct((rows, LANES), jnp.bfloat16),
        ],
        scratch_shapes=[
            pltpu.VMEM((steps, rows, width // steps), x.dtype),
            pltpu.VMEM(recv.shape, jnp.bfloat16),
            pltpu.SemaphoreType.DMA((steps,)),
            pltpu.SemaphoreType.DMA((steps + 1,)),
        ],
        compiler_params=PARAMS,
        cost_estimate=SMALL,
        name="adapter_terms",
    )(in_hbm(x), cot, recv)


def zero_kernel(_, down, up, zeros, dsem, usem):
    zeros[...] = jnp.zeros_like(zeros)
    copies = []
    for i in range(down.shape[0] // ZERO_ROWS):
        rows = pl.ds(i * ZERO_ROWS, ZERO_ROWS)
        part = zeros.at[:, : up.shape[1]]
        copies.append(pltpu.make_async_copy(zeros, down.at[rows, :], dsem.at[i]))
        copies.append(pltpu.make_async_copy(part, up.at[rows, :], usem.at[i]))
    for copy in copies:
        copy.start()
    for copy in copies:
        copy.wait()


def zero_grads(earlier, down_shape, up_shape):
    count = down_shape[0] // ZERO_ROWS
    return pl.pallas_call(
        zero_kernel,
        in_specs=[pl.BlockSpec(memory_space=pl.ANY)],
        out_specs=[IN_HBM, IN_HBM],
        out_shape=[
            jax.ShapeDtypeStruct(down_shape, jnp.float32),
            jax.ShapeDtypeStruct(up_shape, jnp.float32),
        ],
        scratch_shapes=[
            pltpu.VMEM((ZERO_ROWS, down_shape[1]), jnp.float32),
            pltpu.SemaphoreType.DMA((count,)),
            pltpu.SemaphoreType.DMA((count,)),
        ],
        compiler_params=PARAMS,
        cost_estimate=SMALL,
        name="zero_grads",
    )(earlier)


def scatter_kernel(
    adapter, storage, recv, _down, _up, down, up, table, dacc, uacc, dscr, uscr, drow, urow, dsem, usem
):
    blocks = adapter.shape[0]
    devices = recv.shape[0]
    per_down, per_up = down.shape[1] // LANES, up.shape[1] // LANES
    down_rows = 2 * per_down

    def mark(i, carry):
        b = blocks - 1 - i
        table[storage[adapter[b]]] = b
        return carry

    lax.fori_loop(0, blocks, mark, 0)
    dacc[...] = jnp.zeros_like(dacc)
    uacc[...] = jnp.zeros_like(uacc)
    value = lane_cat([recv[:, q * ADAPTER_RANK : (q + 1) * ADAPTER_RANK, :] for q in range(8)])
    value = dot_n(value.reshape(devices * ADAPTER_RANK, 8 * LANES), rank_major_order(True))
    for j in range(devices):
        part = value[j * ADAPTER_RANK : (j + 1) * ADAPTER_RANK, :]
        turned = jnp.concatenate(
            [part[:, lo * LANES : (lo + 1) * LANES] for lo in range(8)], axis=0
        ).T
        narrow = recv[j, down_rows:, :].astype(jnp.float32)
        for k in range(2):
            first = table[storage[adapter[2 * j + k]]]
            dacc[first] += turned[k * per_down : (k + 1) * per_down, :]
            uacc[first] += narrow[k * per_up : (k + 1) * per_up, :]
    for g in range(blocks // 8):
        for i in range(8):
            dscr[pl.ds(i, per_down, stride=8), :] = dacc[8 * g + i]
            uscr[pl.ds(i, per_up, stride=8), :] = uacc[8 * g + i]
        for t in range(per_down):
            drow[8 * g : 8 * g + 8, t * LANES : (t + 1) * LANES] = dscr[8 * t : 8 * t + 8, :]
        for t in range(per_up):
            urow[8 * g : 8 * g + 8, t * LANES : (t + 1) * LANES] = uscr[8 * t : 8 * t + 8, :]

    def copies(b):
        slot = storage[adapter[b]]
        return (
            table[slot] == b,
            pltpu.make_async_copy(drow.at[pl.ds(b, 1), :], down.at[pl.ds(slot, 1), :], dsem.at[b]),
            pltpu.make_async_copy(urow.at[pl.ds(b, 1), :], up.at[pl.ds(slot, 1), :], usem.at[b]),
        )

    def begin(b, carry):
        mine, first, second = copies(b)

        @pl.when(mine)
        def _():
            first.start()
            second.start()

        return carry

    def end(b, carry):
        mine, first, second = copies(b)

        @pl.when(mine)
        def _():
            first.wait()
            second.wait()

        return carry

    lax.fori_loop(0, blocks, begin, 0)
    lax.fori_loop(0, blocks, end, 0)


def scatter_rows(padded_block_adapter, adapter_storage_row, recv, down, up):
    blocks = padded_block_adapter.shape[0]
    per_down, per_up = down.shape[1] // LANES, up.shape[1] // LANES
    return pl.pallas_call(
        scatter_kernel,
        in_specs=[IN_SMEM, IN_SMEM, IN_VMEM, IN_HBM, IN_HBM],
        out_specs=[IN_HBM, IN_HBM],
        scratch_shapes=[
            pltpu.SMEM((ADAPTER_GROUP,), jnp.int32),
            pltpu.VMEM((blocks, per_down, LANES), jnp.float32),
            pltpu.VMEM((blocks, per_up, LANES), jnp.float32),
            pltpu.VMEM((8 * per_down, LANES), jnp.float32),
            pltpu.VMEM((8 * per_up, LANES), jnp.float32),
            pltpu.VMEM((blocks, per_down * LANES), jnp.float32),
            pltpu.VMEM((blocks, per_up * LANES), jnp.float32),
            pltpu.SemaphoreType.DMA((blocks,)),
            pltpu.SemaphoreType.DMA((blocks,)),
        ],
        out_shape=[
            jax.ShapeDtypeStruct(down.shape, down.dtype),
            jax.ShapeDtypeStruct(up.shape, up.dtype),
        ],
        input_output_aliases={3: 0, 4: 1},
        compiler_params=PARAMS,
        cost_estimate=SMALL,
        name="scatter_rows",
    )(in_hbm(padded_block_adapter), in_hbm(adapter_storage_row), recv, down, up)


def pick_kernel(own, other, out, sem):
    mine = lax.axis_index("parts") == lax.axis_index("fsdp") % 2

    @pl.when(mine)
    def _():
        copy = pltpu.make_async_copy(own, out, sem)
        copy.start()
        copy.wait()

    @pl.when(jnp.logical_not(mine))
    def _():
        copy = pltpu.make_async_copy(other, out, sem)
        copy.start()
        copy.wait()


def pick(own, other):
    return pl.pallas_call(
        pick_kernel,
        in_specs=[pl.BlockSpec(memory_space=pl.ANY)] * 2,
        out_specs=IN_VMEM,
        out_shape=jax.ShapeDtypeStruct(own.shape, own.dtype),
        scratch_shapes=[pltpu.SemaphoreType.DMA],
        compiler_params=PARAMS,
        cost_estimate=SMALL,
        name="pick",
    )(in_hbm(own), other)


def far_kernel(count, *refs):
    cots, weight, outs = refs[:count], refs[count], refs[count + 1 : 2 * count + 1]
    wbuf, buffer, wsem, sems = refs[2 * count + 1 :]
    tile = wbuf.shape[1]
    loads = [
        pltpu.make_async_copy(weight.at[i * tile : (i + 1) * tile, :], wbuf.at[i], wsem.at[i])
        for i in range(wbuf.shape[0])
    ]
    for copy in loads:
        copy.start()
    stores = [pltpu.make_async_copy(buffer.at[n], outs[n], sems.at[n]) for n in range(count)]
    for i, load in enumerate(loads):
        load.wait()
        for n, cot in enumerate(cots):
            value = dot_t(cot[...], wbuf[i]).astype(buffer.dtype)
            buffer[n, :, i * tile : (i + 1) * tile] = value
            if i == len(loads) - 1:
                stores[n].start()
    for copy in stores:
        copy.wait()


def far_products(cots, weight):
    count, rows, tile = len(cots), cots[0].shape[0], 256
    span, depth = weight.shape
    shape = jax.ShapeDtypeStruct((rows, span), jnp.bfloat16)
    return pl.pallas_call(
        functools.partial(far_kernel, count),
        in_specs=[IN_VMEM] * count + [pl.BlockSpec(memory_space=pl.ANY)],
        out_specs=[IN_HBM] * count,
        out_shape=[shape] * count,
        scratch_shapes=[
            pltpu.VMEM((span // tile, tile, depth), weight.dtype),
            pltpu.VMEM((count, rows, span), jnp.bfloat16),
            pltpu.SemaphoreType.DMA((span // tile,)),
            pltpu.SemaphoreType.DMA((count,)),
        ],
        compiler_params=PARAMS,
        cost_estimate=SMALL,
        name="far_products",
    )(*cots, in_hbm(weight))


def finish(table, at, cot, weights, received, g, recv, out, width, columns):
    rows = cot.shape[0]
    spans = [w.shape[0] for w in weights] + [r.shape[1] for r in received]
    count = len(spans)
    sources = [in_hbm(source) for source in (*weights, *received)]
    per = columns // LANES

    def kernel(table, cot, g, recv, *rest):
        mine = table_row(table)
        given = rest[:count]
        result = rest[-4 - count]
        buffer, sems, loaded = rest[-3 - count], rest[-2 - count], rest[-1 - count : -1]
        load_sems = rest[-1]
        loads = [
            pltpu.make_async_copy(given[i], loaded[i], load_sems.at[i]) for i in range(count)
        ]
        for load in loads:
            load.start()
        copies = []
        for i in range(count):
            index, span = table[mine, at[i]], spans[i]
            per_device = columns // span
            device, inner = index // per_device, (index % per_device) * (span // LANES)
            parts = []
            for k in range(rows // BLOCK):
                tiles = []
                for q in range(span // LANES):
                    first = pl.multiple_of((k * per + inner + q) * ADAPTER_RANK, ADAPTER_RANK)
                    tiles.append(recv[device, pl.ds(first, ADAPTER_RANK), :])
                ours = g[k * BLOCK : (k + 1) * BLOCK, :ADAPTER_RANK]
                parts.append(dot_n(ours, lane_cat(tiles)))
            value = adapter_scale * jnp.concatenate(parts, axis=0)
            loads[i].wait()
            if i < len(weights):
                value = value + dot_t(cot[...], loaded[i][...])
            else:
                value = value + loaded[i][...].astype(jnp.float32)
            buffer[i, :, :span] = value.astype(buffer.dtype)
            start = pl.multiple_of(index * span, span)
            copies.append(
                pltpu.make_async_copy(
                    buffer.at[i, :, :span], result.at[:, pl.ds(start, span)], sems.at[i]
                )
            )
            copies[-1].start()
        for copy in copies:
            copy.wait()

    return pl.pallas_call(
        kernel,
        in_specs=[IN_SMEM]
        + [IN_VMEM] * 3
        + [pl.BlockSpec(memory_space=pl.ANY)] * count
        + ([] if out is None else [IN_HBM]),
        out_specs=IN_HBM,
        out_shape=jax.ShapeDtypeStruct((rows, width), jnp.bfloat16),
        input_output_aliases={} if out is None else {4 + count: 0},
        scratch_shapes=[
            pltpu.VMEM((count, rows, max(spans)), jnp.bfloat16),
            pltpu.SemaphoreType.DMA((count,)),
        ]
        + [pltpu.VMEM(source.shape, source.dtype) for source in sources]
        + [pltpu.SemaphoreType.DMA((count,))],
        compiler_params=WIDE_PARAMS,
        cost_estimate=SMALL,
        name="finish",
    )(in_hbm(table), cot, g, recv, *sources, *([] if out is None else [out]))


def ring_table(devices):
    chips = devices // 2
    order = list(range(0, chips, 2)) + list(range(chips - 1, 0, -2))
    place = {c: i for i, c in enumerate(order)}
    ring = []
    for c in range(chips):
        ring.append((2 * c, 2 * order[(place[c] + 1) % chips]))
        ring.append((2 * c + 1, 2 * order[(place[c] - 1) % chips] + 1))
    table = []
    for part in range(2):
        for index in range(devices):
            chip, core = index // 2, index % 2
            way = 2 * core - 1
            row = [2 * index, index, index ^ 1]
            for step in range(1, chips // 2):
                near, far = [order[(place[chip] + sign * way * step) % chips] for sign in (1, -1)]
                row += [2 * near + part, 2 * far + part, 2 * near + 1 - part, 2 * far + 1 - part]
            last = order[(place[chip] + chips // 2) % chips]
            for p in (part, 1 - part):
                row += [2 * (2 * last + p) + core, 2 * (2 * last + p) + 1 - core]
            table.append(row)
    return ring, np.array(table, np.int32)


def ring_body(
    inputs,
    cotangent,
    frozen_value_weight,
    adapter_down_weights,
    adapter_up_weights,
    padded_block_adapter,
    block_live_rows,
    adapter_storage_row,
    *,
    devices,
):
    steps = devices // 4
    shard = frozen_value_weight.shape[0]
    width = inputs.shape[1]
    core = lax.axis_index("fsdp") % 2
    ring, table = ring_table(devices)
    table = jnp.asarray(table)
    cores = [(i, i ^ 1) for i in range(devices)]
    across = [(0, 1), (1, 0)]
    diagonal = [(p * devices + i, (1 - p) * devices + (i ^ 1)) for p in range(2) for i in range(devices)]

    def cross(products):
        return (
            lax.ppermute(products[0], "fsdp", cores),
            lax.ppermute(products[1], "parts", across),
            lax.ppermute(products[2], ("parts", "fsdp"), diagonal),
        )

    other_shard = lax.ppermute(frozen_value_weight, "fsdp", cores)
    masked = mask_rows(table, block_live_rows, cotangent)
    core_masked = lax.ppermute(masked, "fsdp", cores)
    far_masked = lax.ppermute(masked, "parts", across)
    travelling = pick(frozen_value_weight, other_shard)
    adapter, _, _ = after(padded_block_adapter, masked, travelling)
    payload = gather_rows(
        adapter, adapter_storage_row, adapter_down_weights, adapter_up_weights, devices
    )
    recv = lax.all_to_all(payload, "fsdp", split_axis=0, concat_axis=0, tiled=True)
    far_masked, _ = after(far_masked, payload)
    diagonal_masked = lax.ppermute(far_masked, "fsdp", cores)
    cots = (core_masked, far_masked, diagonal_masked)

    travelling = lax.ppermute(travelling, "fsdp", ring)

    firsts = [3 + 4 * step for step in range(steps)]
    pieces, received = [], []
    for step in range(steps):
        if step == 0:
            travelling, cots, _ = after(travelling, cots, payload)
        elif step == 1:
            travelling, sent, grads, received[0] = after(travelling, sent, grads, received[0])
            sums = lax.all_to_all(sent, "fsdp", split_axis=0, concat_axis=0, tiled=True)
        elif step < steps - 1:
            travelling, out, received[step - 1] = after(travelling, out, received[step - 1])
        pieces.append(travelling)
        if step < steps - 1:
            if step == steps - 2:
                travelling = lax.dynamic_slice_in_dim(travelling, core * (shard // 2), shard // 2)
            travelling = lax.ppermute(travelling, "fsdp", ring)
        products = far_products(cots, pieces[step])
        received.append(cross(products))
        if step == 0:
            grads = zero_grads(products[0], adapter_down_weights.shape, adapter_up_weights.shape)
            recv, _ = after(recv, grads)
            sent, g = adapter_terms(inputs, masked, recv)
        if step == steps - 2 - 1:
            cot, _ = after(masked, products[0])
            weights = (frozen_value_weight, other_shard, *pieces)
            at = [1, 2] + firsts[: step + 1] + [firsts[0] + i for i in range(1, 4)]
            out = finish(table, at, cot, weights, received[0], g, recv, None, width, shard)
        if step == steps - 2:
            sums, _ = after(sums, products)
            down_grad, up_grad = scatter_rows(
                padded_block_adapter, adapter_storage_row, sums, *grads
            )
            travelling, up_grad = after(travelling, up_grad)
    g, _ = after(g, products)
    at = firsts[-2:] + [first + i for first in firsts[1:-2] for i in range(1, 4)]
    early = sum(received[1:-2], ())
    out = finish(table, at, masked, pieces[-2:], early, g, recv, out, width, shard)
    at = [first + i for first in firsts[-2:] for i in range(1, 4)]
    late = sum(received[-2:], ())
    out = finish(table, at, masked, (), late, g, recv, out, width, shard)
    return (out, down_grad, up_grad)


def after(value, *earlier):
    return lax.optimization_barrier((value,) + earlier)


def gather_body(
    inputs,
    cotangent,
    frozen_value_weight,
    adapter_down_weights,
    adapter_up_weights,
    padded_block_adapter,
    block_live_rows,
    adapter_storage_row,
):
    hidden_width = inputs.shape[1]
    kv_width = cotangent.shape[1]
    token_rows = inputs.shape[0]
    block_count = token_rows // BLOCK
    first_block = lax.axis_index("fsdp") * block_count
    live_rows = lax.dynamic_slice_in_dim(block_live_rows, first_block, block_count)
    positions = jnp.arange(BLOCK, dtype=jnp.int32)
    live_mask = positions[None, :] < live_rows[:, None]
    blocked_cot = cotangent.reshape(block_count, BLOCK, kv_width)
    masked_blocks = jnp.where(live_mask[:, :, None], blocked_cot, jnp.zeros_like(blocked_cot))
    masked = masked_blocks.reshape(token_rows, kv_width)
    block_storage_row = slot_lookup(padded_block_adapter, adapter_storage_row)
    down_weight_rows = jnp.take(adapter_down_weights, block_storage_row, axis=0)
    up_weight_rows = jnp.take(adapter_up_weights, block_storage_row, axis=0)
    down_mine, up_mine = (
        lax.all_to_all(down_weight_rows, "fsdp", split_axis=0, concat_axis=1, tiled=True),
        lax.all_to_all(up_weight_rows, "fsdp", split_axis=0, concat_axis=1, tiled=True),
    )
    frozen_gradient = lax.dot_general(
        masked,
        lax.all_gather(frozen_value_weight, "fsdp", axis=0, tiled=True),
        (((1,), (1,)), ((), ())),
        preferred_element_type=jnp.float32,
    )
    down_weight_matrix = down_mine.reshape(block_count, hidden_width, ADAPTER_RANK)
    up_weight_matrix = up_mine.reshape(block_count, ADAPTER_RANK, kv_width)
    blocked_in = inputs.reshape(block_count, BLOCK, hidden_width)
    rank_projection = jnp.einsum(
        "kbd,kdr->kbr", blocked_in, down_weight_matrix, preferred_element_type=jnp.float32
    ).astype(jnp.bfloat16)
    rank_space_gradient = jnp.einsum(
        "kbv,krv->kbr", masked_blocks, up_weight_matrix, preferred_element_type=jnp.float32
    ).astype(jnp.bfloat16)
    adapter_gradient_term = adapter_scale * jnp.einsum(
        "kbr,kdr->kbd", rank_space_gradient, down_weight_matrix, preferred_element_type=jnp.float32
    )
    input_gradient = (
        frozen_gradient + adapter_gradient_term.reshape(token_rows, hidden_width)
    ).astype(jnp.bfloat16)
    partial_down_weight = adapter_scale * jnp.einsum(
        "kbd,kbr->kdr", blocked_in, rank_space_gradient, preferred_element_type=jnp.float32
    )
    partial_up_weight = adapter_scale * jnp.einsum(
        "kbr,kbv->krv", rank_projection, masked_blocks, preferred_element_type=jnp.float32
    )
    partial_down_weight = partial_down_weight.reshape(block_count, hidden_width * ADAPTER_RANK)
    partial_up_weight = partial_up_weight.reshape(block_count, ADAPTER_RANK * kv_width)
    recv_down, recv_up = (
        lax.all_to_all(partial_down_weight, "fsdp", split_axis=1, concat_axis=0, tiled=True),
        lax.all_to_all(partial_up_weight, "fsdp", split_axis=1, concat_axis=0, tiled=True),
    )
    onehot = (
        jnp.arange(ADAPTER_GROUP, dtype=jnp.int32)[:, None] == block_storage_row[None, :]
    ).astype(jnp.float32)
    highest_precision = lax.Precision.HIGHEST
    down_grad = jnp.dot(
        onehot, recv_down, precision=highest_precision, preferred_element_type=jnp.float32
    )
    up_grad = jnp.dot(
        onehot, recv_up, precision=highest_precision, preferred_element_type=jnp.float32
    )
    return (input_gradient, down_grad, up_grad)


def solution(mesh):
    devices = mesh.shape["fsdp"]
    in_specs = (
        P(("parts", "fsdp"), None),
        P(("parts", "fsdp"), None),
        P("fsdp", None),
        P("parts", "fsdp"),
        P("parts", "fsdp"),
        P("parts"),
        P("parts"),
        P("parts"),
    )
    out_specs = (P(("parts", "fsdp"), None), P("parts", "fsdp"), P("parts", "fsdp"))

    def program(*arrays):
        shard = arrays[2].shape[0] // devices
        rows = arrays[0].shape[0] // devices // 2
        adapter_tiles = arrays[3].shape[1] // devices // LANES
        fits = rows == 2 * BLOCK and 2 * adapter_tiles == LANES and shard % 512 == 0
        if mesh.shape["parts"] == 2 and devices % 4 == 0 and fits:
            body = functools.partial(ring_body, devices=devices)
        else:
            body = gather_body
        return jax.shard_map(
            body, mesh=mesh, in_specs=in_specs, out_specs=out_specs, check_vma=False
        )(*arrays)

    return program
```

```python
import functools

import jax
import jax.numpy as jnp
from jax import lax
from jax.experimental import pallas as pl
from jax.experimental.pallas import tpu as pltpu
from jax.sharding import PartitionSpec as P

ADAPTER_RANK = 16
ADAPTER_GROUP = 512
BLOCK = 128
LANES = 128
MIB = 1024 * 1024
ZERO_ROWS = 64
PARAMS = pltpu.CompilerParams(vmem_limit_bytes=16 * MIB)
WIDE_PARAMS = pltpu.CompilerParams(vmem_limit_bytes=24 * MIB)
IN_VMEM = pl.BlockSpec(memory_space=pltpu.VMEM)
IN_SMEM = pl.BlockSpec(memory_space=pltpu.SMEM)
IN_HBM = pl.BlockSpec(memory_space=pltpu.HBM)
SMALL = pl.CostEstimate(flops=1, bytes_accessed=1, transcendentals=0)
LONGER = pl.CostEstimate(flops=5_000_000_000, bytes_accessed=1, transcendentals=0)

adapter_scale = 2.0


def slot_lookup(padded_block_adapter, adapter_storage_row):
    matches = padded_block_adapter[:, None] == jnp.arange(ADAPTER_GROUP, dtype=jnp.int32)[None, :]
    return jnp.sum(jnp.where(matches, adapter_storage_row[None, :], 0), axis=1)


def in_hbm(value):
    return pltpu.with_memory_space_constraint(value, pltpu.HBM)


def as_it_is(value):
    return value


def column_blocks(devices):
    index, part = lax.axis_index("fsdp"), lax.axis_index("parts")
    chips = devices // 2
    chip, core = lax.div(index, 2), lax.rem(index, 2)
    way = 2 * core - 1
    odd = lax.rem(chip, 2) == 1
    place = jnp.where(odd, chips - lax.div(chip + 1, 2), lax.div(chip, 2))

    def at(steps):
        position = lax.rem(place + steps + chips, chips)
        return jnp.where(position < chips // 2, 2 * position, 2 * (chips - position) - 1)

    blocks = [index, index + 1 - 2 * core]
    for step in range(1, chips // 2):
        near, far = at(way * step), at(-way * step)
        blocks += [2 * near + part, 2 * far + part, 2 * near + 1 - part, 2 * far + 1 - part]
    last = at(chips // 2)
    for p in (part, 1 - part):
        blocks += [2 * (2 * last + p) + core, 2 * (2 * last + p) + 1 - core]
    return blocks


def iota(shape, axis):
    return lax.broadcasted_iota(jnp.int32, shape, axis)


def dot_t(a, b):
    return lax.dot_general(a, b, (((1,), (1,)), ((), ())), preferred_element_type=jnp.float32)


def dot_n(a, b, precision=None):
    return lax.dot_general(
        a, b, (((1,), (0,)), ((), ())), precision=precision, preferred_element_type=jnp.float32
    )


def dot_0(a, b):
    return lax.dot_general(a, b, (((0,), (0,)), ((), ())), preferred_element_type=jnp.float32)


def lane_cat(parts):
    return jnp.concatenate(parts, axis=-1)


def mask_kernel(live, cot, out):
    first = lax.axis_index("fsdp") * (cot.shape[0] // BLOCK)
    row = iota((BLOCK, cot.shape[1]), 0)
    for k in range(cot.shape[0] // BLOCK):
        rows = slice(k * BLOCK, (k + 1) * BLOCK)
        value = cot[rows, :].astype(jnp.float32)
        out[rows, :] = jnp.where(row < live[first + k], value, 0.0).astype(out.dtype)


def mask_rows(block_live_rows, cotangent):
    return pl.pallas_call(
        mask_kernel,
        in_specs=[IN_SMEM, IN_VMEM],
        out_specs=IN_VMEM,
        out_shape=jax.ShapeDtypeStruct(cotangent.shape, cotangent.dtype),
        compiler_params=PARAMS,
        cost_estimate=SMALL,
        name="mask_rows",
    )(in_hbm(block_live_rows), in_hbm(cotangent))


def rank_major_order():
    shape = (8 * LANES, 8 * LANES)
    a, b = iota(shape, 0), iota(shape, 1)
    return ((a % LANES) * 8 + a // LANES == b).astype(jnp.bfloat16)


def gather_kernel(
    adapter, storage, down, up, result, dbuf, ubuf, dscr, uscr, cols, payload, dsem, usem, rsem
):
    blocks = adapter.shape[0]
    devices = result.shape[0]
    group = dbuf.shape[1]
    per_down, per_up = down.shape[1] // LANES, up.shape[1] // LANES
    down_rows = 2 * per_down

    def copies(b):
        slot = storage[adapter[b]]
        start = pl.multiple_of((slot // group) * group, group)
        return (
            slot % group,
            start,
            pltpu.make_async_copy(down.at[pl.ds(start, group), :], dbuf.at[b], dsem.at[b]),
        )

    def begin(b, carry):
        copies(b)[2].start()
        return carry

    ups = pltpu.make_async_copy(up, ubuf, usem)
    ups.start()
    lax.fori_loop(0, blocks, begin, 0)
    order = rank_major_order()

    def one(j, carry):
        wide, narrow = [], []
        for k in range(2):
            b = 2 * j + k
            row, start, copy = copies(b)
            copy.wait()
            late = row >= 8
            line = row % 8
            value = dbuf[b].astype(jnp.float32)
            value = jnp.where(late, value[8:], value[:8])
            for t in range(per_down):
                dscr[k, 8 * t : 8 * t + 8, :] = value[:, t * LANES : (t + 1) * LANES]
            wide.append(dscr[k, pl.ds(line, per_down, stride=8), :])
            value = ubuf[pl.ds(start, group), :].astype(jnp.float32)
            value = jnp.where(late, value[8:], value[:8])
            for t in range(per_up):
                uscr[k, 8 * t : 8 * t + 8, :] = value[:, t * LANES : (t + 1) * LANES]
            narrow.append(uscr[k, pl.ds(line, per_up, stride=8), :])
        turned = jnp.concatenate(wide, axis=0).T
        start = pl.multiple_of(j * ADAPTER_RANK, ADAPTER_RANK)
        for lo in range(8):
            piece = turned[lo * ADAPTER_RANK : (lo + 1) * ADAPTER_RANK, :]
            cols[pl.ds(start, ADAPTER_RANK), lo * LANES : (lo + 1) * LANES] = piece.astype(cols.dtype)
        payload[j, down_rows:, :] = jnp.concatenate(narrow, axis=0).astype(payload.dtype)
        return carry

    ups.wait()
    stores = []
    parts = 2
    count = devices // parts
    for h in range(parts):
        lax.fori_loop(h * count, h * count + count, one, 0)
        rows = slice(h * count * ADAPTER_RANK, (h + 1) * count * ADAPTER_RANK)
        value = dot_n(cols[rows, :], order).astype(payload.dtype)
        value = value.reshape(count, ADAPTER_RANK, 8 * LANES)
        here = slice(h * count, h * count + count)
        for q in range(8):
            payload[here, q * ADAPTER_RANK : (q + 1) * ADAPTER_RANK, :] = value[
                :, :, q * LANES : (q + 1) * LANES
            ]
        part = pl.ds(h * count, count)
        stores.append(pltpu.make_async_copy(payload.at[part], result.at[part], rsem.at[h]))
        stores[-1].start()
    for copy in stores:
        copy.wait()


def gather_rows(padded_block_adapter, adapter_storage_row, down, up, devices):
    blocks = padded_block_adapter.shape[0]
    per_down, per_up = down.shape[1] // LANES, up.shape[1] // LANES
    group = 16
    rows = 2 * (per_down + per_up)
    shape = (devices, rows, LANES)
    return pl.pallas_call(
        gather_kernel,
        in_specs=[IN_SMEM, IN_SMEM, IN_HBM, IN_HBM],
        out_specs=IN_HBM,
        out_shape=jax.ShapeDtypeStruct(shape, jnp.bfloat16),
        scratch_shapes=[
            pltpu.VMEM((blocks, group, down.shape[1]), down.dtype),
            pltpu.VMEM(up.shape, up.dtype),
            pltpu.VMEM((2, 8 * per_down, LANES), jnp.float32),
            pltpu.VMEM((2, 8 * per_up, LANES), jnp.float32),
            pltpu.VMEM((devices * ADAPTER_RANK, 8 * LANES), jnp.bfloat16),
            pltpu.VMEM(shape, jnp.bfloat16),
            pltpu.SemaphoreType.DMA((blocks,)),
            pltpu.SemaphoreType.DMA,
            pltpu.SemaphoreType.DMA((2,)),
        ],
        compiler_params=WIDE_PARAMS,
        cost_estimate=SMALL,
        name="gather_rows",
    )(in_hbm(padded_block_adapter), in_hbm(adapter_storage_row), in_hbm(down), in_hbm(up))


def adapter_kernel(x, cot, recv, result, g_out, xbuf, sent, xsem, rsem):
    devices = recv.shape[0]
    blocks = x.shape[0] // BLOCK
    steps = xbuf.shape[0]
    span = xbuf.shape[2]
    tiles = cot.shape[1] // LANES
    up_chunk = tiles * ADAPTER_RANK // devices
    down_rows = recv.shape[1] - blocks * up_chunk
    per = down_rows // blocks // ADAPTER_RANK
    here = span // LANES // per

    loads = [
        pltpu.make_async_copy(x.at[:, i * span : (i + 1) * span], xbuf.at[i], xsem.at[i])
        for i in range(steps)
    ]
    for copy in loads:
        copy.start()
    lane = iota((BLOCK, LANES), 1)
    gather_rank = (iota((LANES, LANES), 0) // 8 == iota((LANES, LANES), 1)).astype(jnp.float32)
    b_all = recv[:, down_rows:, :].astype(jnp.float32)
    turned = []
    for k in range(blocks):
        m = cot[k * BLOCK : (k + 1) * BLOCK, :]
        b_flat = b_all[:, k * up_chunk : (k + 1) * up_chunk, :].reshape(LANES, LANES)
        b_flat = b_flat.astype(jnp.bfloat16)
        total = jnp.zeros((BLOCK, LANES), jnp.float32)
        for t in range(tiles):
            part = dot_t(m[:, t * LANES : (t + 1) * LANES], b_flat)
            total = total + jnp.where(lane % tiles == t, part, 0.0)
        g = dot_n(total, gather_rank, lax.Precision.HIGHEST).astype(jnp.bfloat16)
        g = (adapter_scale * g.astype(jnp.float32)).astype(jnp.bfloat16)
        g_out[k * BLOCK : (k + 1) * BLOCK, :] = g
        turned.append(g.astype(jnp.float32).T[:ADAPTER_RANK, :].astype(jnp.bfloat16))

    stores = []
    lows = [jnp.zeros((BLOCK, ADAPTER_RANK), jnp.float32) for _ in range(blocks)]
    for i in range(steps):
        loads[i].wait()
        for k in range(blocks):
            part = xbuf[i, k * BLOCK : (k + 1) * BLOCK, :]
            first = k * per * ADAPTER_RANK
            spots = [
                (i * here + j, first + q * ADAPTER_RANK) for j in range(here) for q in range(per)
            ]
            a = lane_cat([recv[j, at : at + ADAPTER_RANK, :] for j, at in spots])
            lows[k] = lows[k] + dot_t(part, a)
            grad = dot_n(turned[k], part).astype(sent.dtype)
            for tile, (j, at) in enumerate(spots):
                sent[j, at : at + ADAPTER_RANK, :] = grad[:, tile * LANES : (tile + 1) * LANES]
        part = (pl.ds(i * here, here), pl.ds(0, down_rows), slice(None))
        stores.append(pltpu.make_async_copy(sent.at[part], result.at[part], rsem.at[i]))
        stores[-1].start()

    ups = []
    row = iota((LANES, LANES), 0)
    spread = (iota((ADAPTER_RANK, LANES), 1) // 8 == iota((ADAPTER_RANK, LANES), 0)).astype(
        jnp.bfloat16
    )
    for k in range(blocks):
        low8 = dot_n(lows[k].astype(jnp.bfloat16), spread).astype(jnp.bfloat16)
        up = dot_0(low8, cot[k * BLOCK : (k + 1) * BLOCK, :])
        flat = jnp.zeros((LANES, LANES), jnp.float32)
        for t in range(tiles):
            flat = flat + jnp.where(row % tiles == t, up[:, t * LANES : (t + 1) * LANES], 0.0)
        ups.append((adapter_scale * flat).reshape(devices, up_chunk, LANES))
    sent[:, down_rows:, :] = jnp.concatenate(ups, axis=1).astype(sent.dtype)
    part = (slice(None), pl.ds(down_rows, sent.shape[1] - down_rows), slice(None))
    stores.append(pltpu.make_async_copy(sent.at[part], result.at[part], rsem.at[steps]))
    stores[-1].start()
    for copy in stores:
        copy.wait()


def adapter_terms(x, cot, recv):
    rows, width = x.shape
    steps = 8
    return pl.pallas_call(
        adapter_kernel,
        in_specs=[IN_HBM, IN_VMEM, IN_VMEM],
        out_specs=[IN_HBM, IN_VMEM],
        out_shape=[
            pltpu.HBM(recv.shape, jnp.bfloat16),
            jax.ShapeDtypeStruct((rows, LANES), jnp.bfloat16),
        ],
        scratch_shapes=[
            pltpu.VMEM((steps, rows, width // steps), x.dtype),
            pltpu.VMEM(recv.shape, jnp.bfloat16),
            pltpu.SemaphoreType.DMA((steps,)),
            pltpu.SemaphoreType.DMA((steps + 1,)),
        ],
        compiler_params=PARAMS,
        cost_estimate=SMALL,
        name="adapter_terms",
    )(in_hbm(x), cot, recv)


def zero_kernel(_, down, up, zeros, dsem, usem):
    zeros[...] = jnp.zeros_like(zeros)
    copies = []
    for i in range(down.shape[0] // ZERO_ROWS):
        rows = pl.ds(i * ZERO_ROWS, ZERO_ROWS)
        part = zeros.at[:, : up.shape[1]]
        copies.append(pltpu.make_async_copy(zeros, down.at[rows, :], dsem.at[i]))
        copies.append(pltpu.make_async_copy(part, up.at[rows, :], usem.at[i]))
    for copy in copies:
        copy.start()
    for copy in copies:
        copy.wait()


def zero_grads(earlier, down_shape, up_shape):
    count = down_shape[0] // ZERO_ROWS
    return pl.pallas_call(
        zero_kernel,
        in_specs=[pl.BlockSpec(memory_space=pl.ANY)],
        out_specs=[IN_HBM, IN_HBM],
        out_shape=[
            jax.ShapeDtypeStruct(down_shape, jnp.float32),
            jax.ShapeDtypeStruct(up_shape, jnp.float32),
        ],
        scratch_shapes=[
            pltpu.VMEM((ZERO_ROWS, down_shape[1]), jnp.float32),
            pltpu.SemaphoreType.DMA((count,)),
            pltpu.SemaphoreType.DMA((count,)),
        ],
        compiler_params=PARAMS,
        cost_estimate=SMALL,
        name="zero_grads",
    )(in_hbm(earlier))


def scatter_kernel(
    adapter, storage, recv, _down, _up, down, up, table, dacc, uacc, dscr, uscr, drow, urow, dsem, usem
):
    blocks = adapter.shape[0]
    devices = recv.shape[0]
    per_down, per_up = down.shape[1] // LANES, up.shape[1] // LANES
    down_rows = 2 * per_down

    def mark(i, carry):
        b = blocks - 1 - i
        table[storage[adapter[b]]] = b
        return carry

    lax.fori_loop(0, blocks, mark, 0)
    dacc[...] = jnp.zeros_like(dacc)
    uacc[...] = jnp.zeros_like(uacc)
    count = 8 * per_down
    a, b = iota((count, count), 0), iota((count, count), 1)
    order = ((b % per_down) * 8 + b // per_down == a).astype(jnp.bfloat16)
    values = []
    for k in range(2):
        tiles = [
            recv[:, q * ADAPTER_RANK : (q + 1) * ADAPTER_RANK, :] for q in range(4 * k, 4 * k + 4)
        ]
        values.append(dot_n(lane_cat(tiles).reshape(devices * ADAPTER_RANK, count), order))
    lower = iota((ADAPTER_RANK, LANES), 1) < per_down
    for j in range(devices):
        rows = []
        for t in range(4):
            first, second = [
                value[j * ADAPTER_RANK : (j + 1) * ADAPTER_RANK, t * LANES : (t + 1) * LANES]
                for value in values
            ]
            rows.append(jnp.where(lower, first, pltpu.roll(second, per_down, 1)))
            rows.append(jnp.where(lower, pltpu.roll(first, per_down, 1), second))
        turned = jnp.concatenate(rows, axis=0).T
        narrow = recv[j, down_rows:, :].astype(jnp.float32)
        for k in range(2):
            first = table[storage[adapter[2 * j + k]]]
            dacc[first] += turned[k * per_down : (k + 1) * per_down, :]
            uacc[first] += narrow[k * per_up : (k + 1) * per_up, :]
    def copies(b):
        slot = storage[adapter[b]]
        return (
            table[slot] == b,
            pltpu.make_async_copy(drow.at[pl.ds(b, 1), :], down.at[pl.ds(slot, 1), :], dsem.at[b]),
            pltpu.make_async_copy(urow.at[pl.ds(b, 1), :], up.at[pl.ds(slot, 1), :], usem.at[b]),
        )

    def begin(b, carry):
        mine, first, second = copies(b)

        @pl.when(mine)
        def _():
            first.start()
            second.start()

        return carry

    def end(b, carry):
        mine, first, second = copies(b)

        @pl.when(mine)
        def _():
            first.wait()
            second.wait()

        return carry

    for g in range(blocks // 8):
        for i in range(8):
            dscr[pl.ds(i, per_down, stride=8), :] = dacc[8 * g + i]
            uscr[pl.ds(i, per_up, stride=8), :] = uacc[8 * g + i]
        for t in range(per_down):
            drow[8 * g : 8 * g + 8, t * LANES : (t + 1) * LANES] = dscr[8 * t : 8 * t + 8, :]
        for t in range(per_up):
            urow[8 * g : 8 * g + 8, t * LANES : (t + 1) * LANES] = uscr[8 * t : 8 * t + 8, :]
        lax.fori_loop(8 * g, 8 * g + 8, begin, 0)
    lax.fori_loop(0, blocks, end, 0)


def scatter_rows(padded_block_adapter, adapter_storage_row, recv, down, up):
    blocks = padded_block_adapter.shape[0]
    per_down, per_up = down.shape[1] // LANES, up.shape[1] // LANES
    return pl.pallas_call(
        scatter_kernel,
        in_specs=[IN_SMEM, IN_SMEM, IN_VMEM, IN_HBM, IN_HBM],
        out_specs=[IN_HBM, IN_HBM],
        scratch_shapes=[
            pltpu.SMEM((ADAPTER_GROUP,), jnp.int32),
            pltpu.VMEM((blocks, per_down, LANES), jnp.float32),
            pltpu.VMEM((blocks, per_up, LANES), jnp.float32),
            pltpu.VMEM((8 * per_down, LANES), jnp.float32),
            pltpu.VMEM((8 * per_up, LANES), jnp.float32),
            pltpu.VMEM((blocks, per_down * LANES), jnp.float32),
            pltpu.VMEM((blocks, per_up * LANES), jnp.float32),
            pltpu.SemaphoreType.DMA((blocks,)),
            pltpu.SemaphoreType.DMA((blocks,)),
        ],
        out_shape=[
            jax.ShapeDtypeStruct(down.shape, down.dtype),
            jax.ShapeDtypeStruct(up.shape, up.dtype),
        ],
        input_output_aliases={3: 0, 4: 1},
        compiler_params=PARAMS,
        cost_estimate=SMALL,
        name="scatter_rows",
    )(in_hbm(padded_block_adapter), in_hbm(adapter_storage_row), recv, down, up)


def pick_kernel(own, other, out, sem):
    mine = lax.axis_index("parts") == lax.axis_index("fsdp") % 2

    @pl.when(mine)
    def _():
        copy = pltpu.make_async_copy(own, out, sem)
        copy.start()
        copy.wait()

    @pl.when(jnp.logical_not(mine))
    def _():
        copy = pltpu.make_async_copy(other, out, sem)
        copy.start()
        copy.wait()


def pick(own, other):
    return pl.pallas_call(
        pick_kernel,
        in_specs=[pl.BlockSpec(memory_space=pl.ANY)] * 2,
        out_specs=IN_VMEM,
        out_shape=jax.ShapeDtypeStruct(own.shape, own.dtype),
        scratch_shapes=[pltpu.SemaphoreType.DMA],
        compiler_params=PARAMS,
        cost_estimate=SMALL,
        name="pick",
    )(in_hbm(own), other)


def far_kernel(count, handed, *refs):
    cots, weight, outs = refs[:count], refs[count], refs[count + 1 : 2 * count + 1]
    wbuf, buffer, wsem, sems, hsem = refs[2 * count + 1 + handed :]
    tile = wbuf.shape[1]
    loads = [
        pltpu.make_async_copy(weight.at[i * tile : (i + 1) * tile, :], wbuf.at[i], wsem.at[i])
        for i in range(wbuf.shape[0])
    ]
    for copy in loads:
        copy.start()
    stores = [pltpu.make_async_copy(buffer.at[n], outs[n], sems.at[n]) for n in range(count)]
    for i, load in enumerate(loads):
        load.wait()
        for n, cot in enumerate(cots):
            value = dot_t(cot[...], wbuf[i]).astype(buffer.dtype)
            buffer[n, :, i * tile : (i + 1) * tile] = value
            if i == len(loads) - 1:
                stores[n].start()
    if handed:
        core = lax.axis_index("fsdp") % 2
        copy = pltpu.make_async_copy(wbuf.at[core], refs[2 * count + 1], hsem)
        copy.start()
        copy.wait()
    for copy in stores:
        copy.wait()


def far_products(cots, weight, pin=in_hbm, handed=False):
    count, rows, tile = len(cots), cots[0].shape[0], 256
    span, depth = weight.shape
    shape = pltpu.HBM((rows, span), jnp.bfloat16)
    half = [pltpu.HBM((tile, depth), weight.dtype)] if handed else []
    return pl.pallas_call(
        functools.partial(far_kernel, count, len(half)),
        in_specs=[IN_VMEM] * count + [pl.BlockSpec(memory_space=pl.ANY)],
        out_specs=[IN_HBM] * (count + len(half)),
        out_shape=[shape] * count + half,
        scratch_shapes=[
            pltpu.VMEM((span // tile, tile, depth), weight.dtype),
            pltpu.VMEM((count, rows, span), jnp.bfloat16),
            pltpu.SemaphoreType.DMA((span // tile,)),
            pltpu.SemaphoreType.DMA((count,)),
            pltpu.SemaphoreType.DMA,
        ],
        compiler_params=PARAMS,
        cost_estimate=SMALL,
        name="far_products",
    )(*cots, pin(weight))


def finish(devices, at, cot, weights, received, g, recv, out, width, columns, pin=in_hbm, cost=SMALL):
    rows = cot.shape[0]
    spans = [w.shape[0] for w in weights] + [r.shape[1] for r in received]
    count = len(spans)
    sources = [pin(source) for source in (*weights, *received)]
    per = columns // LANES

    def kernel(cot, g, recv, *rest):
        where = column_blocks(devices)
        given = rest[:count]
        result = rest[-4 - count]
        buffer, sems, loaded = rest[-3 - count], rest[-2 - count], rest[-1 - count : -1]
        load_sems = rest[-1]
        loads = [
            pltpu.make_async_copy(given[i], loaded[i], load_sems.at[i]) for i in range(count)
        ]
        for load in loads:
            load.start()
        copies = []
        for i in range(count):
            index, span = where[at[i]], spans[i]
            per_device = columns // span
            device, inner = index // per_device, (index % per_device) * (span // LANES)
            parts = []
            for k in range(rows // BLOCK):
                tiles = []
                for q in range(span // LANES):
                    first = pl.multiple_of((k * per + inner + q) * ADAPTER_RANK, ADAPTER_RANK)
                    tiles.append(recv[device, pl.ds(first, ADAPTER_RANK), :])
                ours = g[k * BLOCK : (k + 1) * BLOCK, :ADAPTER_RANK]
                parts.append(dot_n(ours, lane_cat(tiles)))
            value = jnp.concatenate(parts, axis=0)
            loads[i].wait()
            if i < len(weights):
                value = value + dot_t(cot[...], loaded[i][...])
            else:
                value = value + loaded[i][...].astype(jnp.float32)
            buffer[i, :, :span] = value.astype(buffer.dtype)
            start = pl.multiple_of(index * span, span)
            copies.append(
                pltpu.make_async_copy(
                    buffer.at[i, :, :span], result.at[:, pl.ds(start, span)], sems.at[i]
                )
            )
            copies[-1].start()
        for copy in copies:
            copy.wait()

    return pl.pallas_call(
        kernel,
        in_specs=[IN_VMEM] * 3
        + [pl.BlockSpec(memory_space=pl.ANY)] * count
        + ([] if out is None else [IN_HBM]),
        out_specs=IN_HBM,
        out_shape=jax.ShapeDtypeStruct((rows, width), jnp.bfloat16),
        input_output_aliases={} if out is None else {3 + count: 0},
        scratch_shapes=[
            pltpu.VMEM((count, rows, max(spans)), jnp.bfloat16),
            pltpu.SemaphoreType.DMA((count,)),
        ]
        + [pltpu.VMEM(source.shape, source.dtype) for source in sources]
        + [pltpu.SemaphoreType.DMA((count,))],
        compiler_params=WIDE_PARAMS,
        cost_estimate=cost,
        name="finish",
    )(cot, g, recv, *sources, *([] if out is None else [out]))


def ring_pairs(devices):
    chips = devices // 2
    order = list(range(0, chips, 2)) + list(range(chips - 1, 0, -2))
    place = {c: i for i, c in enumerate(order)}
    ring = []
    for c in range(chips):
        ring.append((2 * c, 2 * order[(place[c] + 1) % chips]))
        ring.append((2 * c + 1, 2 * order[(place[c] - 1) % chips] + 1))
    return ring


def ring_body(
    inputs,
    cotangent,
    frozen_value_weight,
    adapter_down_weights,
    adapter_up_weights,
    padded_block_adapter,
    block_live_rows,
    adapter_storage_row,
    *,
    devices,
):
    steps = devices // 4
    shard = frozen_value_weight.shape[0]
    width = inputs.shape[1]
    ring = ring_pairs(devices)
    cores = [(i, i ^ 1) for i in range(devices)]
    across = [(0, 1), (1, 0)]
    diagonal = [(p * devices + i, (1 - p) * devices + (i ^ 1)) for p in range(2) for i in range(devices)]

    def cross(products):
        return (
            lax.ppermute(products[0], "fsdp", cores),
            lax.ppermute(products[1], "parts", across),
            lax.ppermute(products[2], ("parts", "fsdp"), diagonal),
        )

    other_shard = lax.ppermute(frozen_value_weight, "fsdp", cores)
    masked = mask_rows(block_live_rows, cotangent)
    core_masked = lax.ppermute(masked, "fsdp", cores)
    far_masked = lax.ppermute(masked, "parts", across)
    travelling = pick(frozen_value_weight, other_shard)
    adapter, _, _ = after(padded_block_adapter, masked, travelling)
    payload = gather_rows(
        adapter, adapter_storage_row, adapter_down_weights, adapter_up_weights, devices
    )
    recv = lax.all_to_all(payload, "fsdp", split_axis=0, concat_axis=0, tiled=True)
    far_masked, _ = after(far_masked, payload)
    diagonal_masked = lax.ppermute(far_masked, "fsdp", cores)
    cots = (core_masked, far_masked, diagonal_masked)

    travelling = lax.ppermute(travelling, "fsdp", ring)

    firsts = [2 + 4 * step for step in range(steps)]
    pieces, received = [], []
    for step in range(steps):
        if step == 0:
            travelling, cots, _ = after(travelling, cots, payload)
        elif step == 1:
            travelling, sent, out, grads, received[0] = after(
                travelling, sent, out, grads, received[0]
            )
        pieces.append(travelling)
        if step < steps - 2:
            travelling = lax.ppermute(travelling, "fsdp", ring)
        pin = as_it_is if step >= steps - 2 else in_hbm
        products = far_products(cots, pieces[step], pin, step == steps - 2)
        if step == steps - 2:
            *products, travelling = products
            travelling, products, out, received[-1] = after(
                travelling, products, out, received[-1]
            )
            travelling = lax.ppermute(travelling, "fsdp", ring)
        if step == steps - 1:
            products, received[-1] = after(products, received[-1])
        received.append(cross(products))
        if step == 0:
            grads = zero_grads(products[0], adapter_down_weights.shape, adapter_up_weights.shape)
            recv, _ = after(recv, grads)
            sent, g = adapter_terms(inputs, masked, recv)
            weights = (frozen_value_weight, other_shard)
            out = finish(devices, [0, 1], masked, weights, (), g, recv, None, width, shard)
        if step == steps - 3:
            cot, _ = after(masked, products[0])
            at = firsts[: step + 1] + [firsts[0] + i for i in range(1, 4)]
            out = finish(devices, at, cot, pieces[:2], received[0], g, recv, out, width, shard)
            sent, out = after(sent, out)
            sums = lax.all_to_all(sent, "fsdp", split_axis=0, concat_axis=0, tiled=True)
            travelling, out = after(travelling, out)
        if step == steps - 2:
            out, _ = after(out, products)
            at = [firsts[step]] + [first + i for first in firsts[1:step] for i in range(1, 4)]
            early = sum(received[1:step], ())
            piece = pieces[step : step + 1]
            out = finish(devices, at, masked, piece, early, g, recv, out, width, shard)
            travelling, out = after(travelling, out)
    at = firsts[-1:] + [firsts[-2] + i for i in range(1, 4)]
    piece = pieces[-1:]
    out = finish(
        devices, at, masked, piece, received[-2], g, recv, out, width, shard, as_it_is, LONGER
    )
    sums, out = after(sums, out)
    down_grad, up_grad = scatter_rows(padded_block_adapter, adapter_storage_row, sums, *grads)
    out, up_grad = after(out, up_grad)
    at = [firsts[-1] + i for i in range(1, 4)]
    out = finish(devices, at, masked, (), received[-1], g, recv, out, width, shard, as_it_is)
    return (out, down_grad, up_grad)


def after(value, *earlier):
    return lax.optimization_barrier((value,) + earlier)


def gather_body(
    inputs,
    cotangent,
    frozen_value_weight,
    adapter_down_weights,
    adapter_up_weights,
    padded_block_adapter,
    block_live_rows,
    adapter_storage_row,
):
    hidden_width = inputs.shape[1]
    kv_width = cotangent.shape[1]
    token_rows = inputs.shape[0]
    block_count = token_rows // BLOCK
    first_block = lax.axis_index("fsdp") * block_count
    live_rows = lax.dynamic_slice_in_dim(block_live_rows, first_block, block_count)
    positions = jnp.arange(BLOCK, dtype=jnp.int32)
    live_mask = positions[None, :] < live_rows[:, None]
    blocked_cot = cotangent.reshape(block_count, BLOCK, kv_width)
    masked_blocks = jnp.where(live_mask[:, :, None], blocked_cot, jnp.zeros_like(blocked_cot))
    masked = masked_blocks.reshape(token_rows, kv_width)
    block_storage_row = slot_lookup(padded_block_adapter, adapter_storage_row)
    down_weight_rows = jnp.take(adapter_down_weights, block_storage_row, axis=0)
    up_weight_rows = jnp.take(adapter_up_weights, block_storage_row, axis=0)
    down_mine, up_mine = (
        lax.all_to_all(down_weight_rows, "fsdp", split_axis=0, concat_axis=1, tiled=True),
        lax.all_to_all(up_weight_rows, "fsdp", split_axis=0, concat_axis=1, tiled=True),
    )
    frozen_gradient = lax.dot_general(
        masked,
        lax.all_gather(frozen_value_weight, "fsdp", axis=0, tiled=True),
        (((1,), (1,)), ((), ())),
        preferred_element_type=jnp.float32,
    )
    down_weight_matrix = down_mine.reshape(block_count, hidden_width, ADAPTER_RANK)
    up_weight_matrix = up_mine.reshape(block_count, ADAPTER_RANK, kv_width)
    blocked_in = inputs.reshape(block_count, BLOCK, hidden_width)
    rank_projection = jnp.einsum(
        "kbd,kdr->kbr", blocked_in, down_weight_matrix, preferred_element_type=jnp.float32
    ).astype(jnp.bfloat16)
    rank_space_gradient = jnp.einsum(
        "kbv,krv->kbr", masked_blocks, up_weight_matrix, preferred_element_type=jnp.float32
    ).astype(jnp.bfloat16)
    adapter_gradient_term = adapter_scale * jnp.einsum(
        "kbr,kdr->kbd", rank_space_gradient, down_weight_matrix, preferred_element_type=jnp.float32
    )
    input_gradient = (
        frozen_gradient + adapter_gradient_term.reshape(token_rows, hidden_width)
    ).astype(jnp.bfloat16)
    partial_down_weight = adapter_scale * jnp.einsum(
        "kbd,kbr->kdr", blocked_in, rank_space_gradient, preferred_element_type=jnp.float32
    )
    partial_up_weight = adapter_scale * jnp.einsum(
        "kbr,kbv->krv", rank_projection, masked_blocks, preferred_element_type=jnp.float32
    )
    partial_down_weight = partial_down_weight.reshape(block_count, hidden_width * ADAPTER_RANK)
    partial_up_weight = partial_up_weight.reshape(block_count, ADAPTER_RANK * kv_width)
    recv_down, recv_up = (
        lax.all_to_all(partial_down_weight, "fsdp", split_axis=1, concat_axis=0, tiled=True),
        lax.all_to_all(partial_up_weight, "fsdp", split_axis=1, concat_axis=0, tiled=True),
    )
    onehot = (
        jnp.arange(ADAPTER_GROUP, dtype=jnp.int32)[:, None] == block_storage_row[None, :]
    ).astype(jnp.float32)
    highest_precision = lax.Precision.HIGHEST
    down_grad = jnp.dot(
        onehot, recv_down, precision=highest_precision, preferred_element_type=jnp.float32
    )
    up_grad = jnp.dot(
        onehot, recv_up, precision=highest_precision, preferred_element_type=jnp.float32
    )
    return (input_gradient, down_grad, up_grad)


def solution(mesh):
    devices = mesh.shape["fsdp"]
    in_specs = (
        P(("parts", "fsdp"), None),
        P(("parts", "fsdp"), None),
        P("fsdp", None),
        P("parts", "fsdp"),
        P("parts", "fsdp"),
        P("parts"),
        P("parts"),
        P("parts"),
    )
    out_specs = (P(("parts", "fsdp"), None), P("parts", "fsdp"), P("parts", "fsdp"))

    def program(*arrays):
        shard = arrays[2].shape[0] // devices
        rows = arrays[0].shape[0] // devices // 2
        adapter_tiles = arrays[3].shape[1] // devices // LANES
        fits = rows == 2 * BLOCK and 2 * adapter_tiles == LANES and shard % 512 == 0
        if mesh.shape["parts"] == 2 and devices % 4 == 0 and fits:
            body = functools.partial(ring_body, devices=devices)
        else:
            body = gather_body
        return jax.shard_map(
            body, mesh=mesh, in_specs=in_specs, out_specs=out_specs, check_vma=False
        )(*arrays)

    return program
```

```python
import functools

import jax
import jax.numpy as jnp
from jax import lax
from jax.experimental import pallas as pl
from jax.experimental.pallas import tpu as pltpu
from jax.sharding import PartitionSpec as P

ADAPTER_RANK = 16
ADAPTER_GROUP = 512
BLOCK = 128
LANES = 128
MIB = 1024 * 1024
ZERO_ROWS = 64
PARAMS = pltpu.CompilerParams(vmem_limit_bytes=16 * MIB)
WIDE_PARAMS = pltpu.CompilerParams(vmem_limit_bytes=24 * MIB)
IN_VMEM = pl.BlockSpec(memory_space=pltpu.VMEM)
IN_SMEM = pl.BlockSpec(memory_space=pltpu.SMEM)
IN_HBM = pl.BlockSpec(memory_space=pltpu.HBM)
SMALL = pl.CostEstimate(flops=1, bytes_accessed=1, transcendentals=0)
LONGER = pl.CostEstimate(flops=10_000_000_000, bytes_accessed=1, transcendentals=0)

adapter_scale = 2.0


def slot_lookup(padded_block_adapter, adapter_storage_row):
    matches = padded_block_adapter[:, None] == jnp.arange(ADAPTER_GROUP, dtype=jnp.int32)[None, :]
    return jnp.sum(jnp.where(matches, adapter_storage_row[None, :], 0), axis=1)


def in_hbm(value):
    return pltpu.with_memory_space_constraint(value, pltpu.HBM)


def as_it_is(value):
    return value


def column_blocks(devices):
    index, part = lax.axis_index("fsdp"), lax.axis_index("parts")
    chips = devices // 2
    chip, core = lax.div(index, 2), lax.rem(index, 2)
    way = jnp.where(core == part, -1, 1)
    odd = lax.rem(chip, 2) == 1
    place = jnp.where(odd, chips - lax.div(chip + 1, 2), lax.div(chip, 2))

    def at(steps):
        position = lax.rem(place + steps + chips, chips)
        return jnp.where(position < chips // 2, 2 * position, 2 * (chips - position) - 1)

    blocks = [index, index + 1 - 2 * core]
    for step in range(1, chips // 2):
        near, far = at(way * step), at(-way * step)
        blocks += [2 * near + core, 2 * far + 1 - core, 2 * far + core, 2 * near + 1 - core]
    last = at(chips // 2)
    for p in (part, 1 - part):
        blocks += [2 * (2 * last + core) + p, 2 * (2 * last + 1 - core) + p]
    return blocks


def iota(shape, axis):
    return lax.broadcasted_iota(jnp.int32, shape, axis)


def dot_t(a, b):
    return lax.dot_general(a, b, (((1,), (1,)), ((), ())), preferred_element_type=jnp.float32)


def dot_n(a, b, precision=None):
    return lax.dot_general(
        a, b, (((1,), (0,)), ((), ())), precision=precision, preferred_element_type=jnp.float32
    )


def dot_0(a, b):
    return lax.dot_general(a, b, (((0,), (0,)), ((), ())), preferred_element_type=jnp.float32)


def lane_cat(parts):
    return jnp.concatenate(parts, axis=-1)


def mask_kernel(live, cot, out):
    first = lax.axis_index("fsdp") * (cot.shape[0] // BLOCK)
    row = iota((BLOCK, cot.shape[1]), 0)
    for k in range(cot.shape[0] // BLOCK):
        rows = slice(k * BLOCK, (k + 1) * BLOCK)
        value = cot[rows, :].astype(jnp.float32)
        out[rows, :] = jnp.where(row < live[first + k], value, 0.0).astype(out.dtype)


def mask_rows(block_live_rows, cotangent):
    return pl.pallas_call(
        mask_kernel,
        in_specs=[IN_SMEM, IN_VMEM],
        out_specs=IN_VMEM,
        out_shape=jax.ShapeDtypeStruct(cotangent.shape, cotangent.dtype),
        compiler_params=PARAMS,
        cost_estimate=SMALL,
        name="mask_rows",
    )(in_hbm(block_live_rows), in_hbm(cotangent))


def rank_major_order():
    shape = (8 * LANES, 8 * LANES)
    a, b = iota(shape, 0), iota(shape, 1)
    return ((a % LANES) * 8 + a // LANES == b).astype(jnp.bfloat16)


def gather_kernel(
    adapter, storage, down, up, result, dbuf, ubuf, dscr, uscr, cols, payload, dsem, usem, rsem
):
    blocks = adapter.shape[0]
    devices = result.shape[0]
    group = dbuf.shape[1]
    per_down, per_up = down.shape[1] // LANES, up.shape[1] // LANES
    down_rows = 2 * per_down

    def copies(b):
        slot = storage[adapter[b]]
        start = pl.multiple_of((slot // group) * group, group)
        return (
            slot % group,
            start,
            pltpu.make_async_copy(down.at[pl.ds(start, group), :], dbuf.at[b], dsem.at[b]),
        )

    def begin(b, carry):
        copies(b)[2].start()
        return carry

    ups = pltpu.make_async_copy(up, ubuf, usem)
    ups.start()
    lax.fori_loop(0, blocks, begin, 0)
    order = rank_major_order()

    def one(j, carry):
        wide, narrow = [], []
        for k in range(2):
            b = 2 * j + k
            row, start, copy = copies(b)
            copy.wait()
            late = row >= 8
            line = row % 8
            value = dbuf[b].astype(jnp.float32)
            value = jnp.where(late, value[8:], value[:8])
            for t in range(per_down):
                dscr[k, 8 * t : 8 * t + 8, :] = value[:, t * LANES : (t + 1) * LANES]
            wide.append(dscr[k, pl.ds(line, per_down, stride=8), :])
            value = ubuf[pl.ds(start, group), :].astype(jnp.float32)
            value = jnp.where(late, value[8:], value[:8])
            for t in range(per_up):
                uscr[k, 8 * t : 8 * t + 8, :] = value[:, t * LANES : (t + 1) * LANES]
            narrow.append(uscr[k, pl.ds(line, per_up, stride=8), :])
        turned = jnp.concatenate(wide, axis=0).T
        start = pl.multiple_of(j * ADAPTER_RANK, ADAPTER_RANK)
        for lo in range(8):
            piece = turned[lo * ADAPTER_RANK : (lo + 1) * ADAPTER_RANK, :]
            cols[pl.ds(start, ADAPTER_RANK), lo * LANES : (lo + 1) * LANES] = piece.astype(cols.dtype)
        payload[j, down_rows:, :] = jnp.concatenate(narrow, axis=0).astype(payload.dtype)
        return carry

    ups.wait()
    stores = []
    parts = 2
    count = devices // parts
    for h in range(parts):
        lax.fori_loop(h * count, h * count + count, one, 0)
        rows = slice(h * count * ADAPTER_RANK, (h + 1) * count * ADAPTER_RANK)
        value = dot_n(cols[rows, :], order).astype(payload.dtype)
        value = value.reshape(count, ADAPTER_RANK, 8 * LANES)
        here = slice(h * count, h * count + count)
        for q in range(8):
            payload[here, q * ADAPTER_RANK : (q + 1) * ADAPTER_RANK, :] = value[
                :, :, q * LANES : (q + 1) * LANES
            ]
        part = pl.ds(h * count, count)
        stores.append(pltpu.make_async_copy(payload.at[part], result.at[part], rsem.at[h]))
        stores[-1].start()
    for copy in stores:
        copy.wait()


def gather_rows(padded_block_adapter, adapter_storage_row, down, up, devices):
    blocks = padded_block_adapter.shape[0]
    per_down, per_up = down.shape[1] // LANES, up.shape[1] // LANES
    group = 16
    rows = 2 * (per_down + per_up)
    shape = (devices, rows, LANES)
    return pl.pallas_call(
        gather_kernel,
        in_specs=[IN_SMEM, IN_SMEM, IN_HBM, IN_HBM],
        out_specs=IN_HBM,
        out_shape=jax.ShapeDtypeStruct(shape, jnp.bfloat16),
        scratch_shapes=[
            pltpu.VMEM((blocks, group, down.shape[1]), down.dtype),
            pltpu.VMEM(up.shape, up.dtype),
            pltpu.VMEM((2, 8 * per_down, LANES), jnp.float32),
            pltpu.VMEM((2, 8 * per_up, LANES), jnp.float32),
            pltpu.VMEM((devices * ADAPTER_RANK, 8 * LANES), jnp.bfloat16),
            pltpu.VMEM(shape, jnp.bfloat16),
            pltpu.SemaphoreType.DMA((blocks,)),
            pltpu.SemaphoreType.DMA,
            pltpu.SemaphoreType.DMA((2,)),
        ],
        compiler_params=WIDE_PARAMS,
        cost_estimate=SMALL,
        name="gather_rows",
    )(in_hbm(padded_block_adapter), in_hbm(adapter_storage_row), in_hbm(down), in_hbm(up))


def adapter_kernel(x, cot, recv, result, g_out, xbuf, sent, xsem, rsem):
    devices = recv.shape[0]
    blocks = x.shape[0] // BLOCK
    steps = xbuf.shape[0]
    span = xbuf.shape[2]
    tiles = cot.shape[1] // LANES
    up_chunk = tiles * ADAPTER_RANK // devices
    down_rows = recv.shape[1] - blocks * up_chunk
    per = down_rows // blocks // ADAPTER_RANK
    here = span // LANES // per

    loads = [
        pltpu.make_async_copy(x.at[:, i * span : (i + 1) * span], xbuf.at[i], xsem.at[i])
        for i in range(steps)
    ]
    for copy in loads:
        copy.start()
    lane = iota((BLOCK, LANES), 1)
    gather_rank = (iota((LANES, LANES), 0) // 8 == iota((LANES, LANES), 1)).astype(jnp.float32)
    b_all = recv[:, down_rows:, :].astype(jnp.float32)
    turned = []
    for k in range(blocks):
        m = cot[k * BLOCK : (k + 1) * BLOCK, :]
        b_flat = b_all[:, k * up_chunk : (k + 1) * up_chunk, :].reshape(LANES, LANES)
        b_flat = b_flat.astype(jnp.bfloat16)
        total = jnp.zeros((BLOCK, LANES), jnp.float32)
        for t in range(tiles):
            part = dot_t(m[:, t * LANES : (t + 1) * LANES], b_flat)
            total = total + jnp.where(lane % tiles == t, part, 0.0)
        g = dot_n(total, gather_rank, lax.Precision.HIGHEST).astype(jnp.bfloat16)
        g = (adapter_scale * g.astype(jnp.float32)).astype(jnp.bfloat16)
        g_out[k * BLOCK : (k + 1) * BLOCK, :] = g
        turned.append(g.astype(jnp.float32).T[:ADAPTER_RANK, :].astype(jnp.bfloat16))

    stores = []
    lows = [jnp.zeros((BLOCK, ADAPTER_RANK), jnp.float32) for _ in range(blocks)]
    for i in range(steps):
        loads[i].wait()
        for k in range(blocks):
            part = xbuf[i, k * BLOCK : (k + 1) * BLOCK, :]
            first = k * per * ADAPTER_RANK
            spots = [
                (i * here + j, first + q * ADAPTER_RANK) for j in range(here) for q in range(per)
            ]
            a = lane_cat([recv[j, at : at + ADAPTER_RANK, :] for j, at in spots])
            lows[k] = lows[k] + dot_t(part, a)
            grad = dot_n(turned[k], part).astype(sent.dtype)
            for tile, (j, at) in enumerate(spots):
                sent[j, at : at + ADAPTER_RANK, :] = grad[:, tile * LANES : (tile + 1) * LANES]
        part = (pl.ds(i * here, here), pl.ds(0, down_rows), slice(None))
        stores.append(pltpu.make_async_copy(sent.at[part], result.at[part], rsem.at[i]))
        stores[-1].start()

    ups = []
    row = iota((LANES, LANES), 0)
    spread = (iota((ADAPTER_RANK, LANES), 1) // 8 == iota((ADAPTER_RANK, LANES), 0)).astype(
        jnp.bfloat16
    )
    for k in range(blocks):
        low8 = dot_n(lows[k].astype(jnp.bfloat16), spread).astype(jnp.bfloat16)
        up = dot_0(low8, cot[k * BLOCK : (k + 1) * BLOCK, :])
        flat = jnp.zeros((LANES, LANES), jnp.float32)
        for t in range(tiles):
            flat = flat + jnp.where(row % tiles == t, up[:, t * LANES : (t + 1) * LANES], 0.0)
        ups.append((adapter_scale * flat).reshape(devices, up_chunk, LANES))
    sent[:, down_rows:, :] = jnp.concatenate(ups, axis=1).astype(sent.dtype)
    part = (slice(None), pl.ds(down_rows, sent.shape[1] - down_rows), slice(None))
    stores.append(pltpu.make_async_copy(sent.at[part], result.at[part], rsem.at[steps]))
    stores[-1].start()
    for copy in stores:
        copy.wait()


def adapter_terms(x, cot, recv):
    rows, width = x.shape
    steps = 8
    return pl.pallas_call(
        adapter_kernel,
        in_specs=[IN_HBM, IN_VMEM, IN_VMEM],
        out_specs=[IN_HBM, IN_VMEM],
        out_shape=[
            pltpu.HBM(recv.shape, jnp.bfloat16),
            jax.ShapeDtypeStruct((rows, LANES), jnp.bfloat16),
        ],
        scratch_shapes=[
            pltpu.VMEM((steps, rows, width // steps), x.dtype),
            pltpu.VMEM(recv.shape, jnp.bfloat16),
            pltpu.SemaphoreType.DMA((steps,)),
            pltpu.SemaphoreType.DMA((steps + 1,)),
        ],
        compiler_params=PARAMS,
        cost_estimate=SMALL,
        name="adapter_terms",
    )(in_hbm(x), cot, recv)


def zero_kernel(_, down, up, zeros, dsem, usem):
    zeros[...] = jnp.zeros_like(zeros)
    copies = []
    for i in range(down.shape[0] // ZERO_ROWS):
        rows = pl.ds(i * ZERO_ROWS, ZERO_ROWS)
        part = zeros.at[:, : up.shape[1]]
        copies.append(pltpu.make_async_copy(zeros, down.at[rows, :], dsem.at[i]))
        copies.append(pltpu.make_async_copy(part, up.at[rows, :], usem.at[i]))
    for copy in copies:
        copy.start()
    for copy in copies:
        copy.wait()


def zero_grads(earlier, down_shape, up_shape):
    count = down_shape[0] // ZERO_ROWS
    return pl.pallas_call(
        zero_kernel,
        in_specs=[pl.BlockSpec(memory_space=pl.ANY)],
        out_specs=[IN_HBM, IN_HBM],
        out_shape=[
            jax.ShapeDtypeStruct(down_shape, jnp.float32),
            jax.ShapeDtypeStruct(up_shape, jnp.float32),
        ],
        scratch_shapes=[
            pltpu.VMEM((ZERO_ROWS, down_shape[1]), jnp.float32),
            pltpu.SemaphoreType.DMA((count,)),
            pltpu.SemaphoreType.DMA((count,)),
        ],
        compiler_params=PARAMS,
        cost_estimate=SMALL,
        name="zero_grads",
    )(in_hbm(earlier))


def scatter_kernel(
    adapter_hbm, storage_hbm, recv, _down, _up, down, up, adapter, storage, isem, table, dacc, uacc, dscr, uscr, drow, urow, dsem, usem
):
    blocks = adapter_hbm.shape[0]
    devices = recv.shape[0]
    per_down, per_up = down.shape[1] // LANES, up.shape[1] // LANES
    down_rows = 2 * per_down

    indices = [
        pltpu.make_async_copy(adapter_hbm, adapter, isem.at[0]),
        pltpu.make_async_copy(storage_hbm, storage, isem.at[1]),
    ]
    for copy in indices:
        copy.start()
    dacc[...] = jnp.zeros_like(dacc)
    uacc[...] = jnp.zeros_like(uacc)
    count = 8 * per_down
    a, b = iota((count, count), 0), iota((count, count), 1)
    order = ((b % per_down) * 8 + b // per_down == a).astype(jnp.bfloat16)
    values = []
    for k in range(2):
        tiles = [
            recv[:, q * ADAPTER_RANK : (q + 1) * ADAPTER_RANK, :] for q in range(4 * k, 4 * k + 4)
        ]
        values.append(dot_n(lane_cat(tiles).reshape(devices * ADAPTER_RANK, count), order))
    for copy in indices:
        copy.wait()

    def mark(i, carry):
        b = blocks - 1 - i
        table[storage[adapter[b]]] = b
        return carry

    lax.fori_loop(0, blocks, mark, 0)
    lower = iota((ADAPTER_RANK, LANES), 1) < per_down
    for j in range(devices):
        rows = []
        for t in range(4):
            first, second = [
                value[j * ADAPTER_RANK : (j + 1) * ADAPTER_RANK, t * LANES : (t + 1) * LANES]
                for value in values
            ]
            rows.append(jnp.where(lower, first, pltpu.roll(second, per_down, 1)))
            rows.append(jnp.where(lower, pltpu.roll(first, per_down, 1), second))
        turned = jnp.concatenate(rows, axis=0).T
        narrow = recv[j, down_rows:, :].astype(jnp.float32)
        for k in range(2):
            first = table[storage[adapter[2 * j + k]]]
            dacc[first] += turned[k * per_down : (k + 1) * per_down, :]
            uacc[first] += narrow[k * per_up : (k + 1) * per_up, :]
    def copies(b):
        slot = storage[adapter[b]]
        return (
            table[slot] == b,
            pltpu.make_async_copy(drow.at[pl.ds(b, 1), :], down.at[pl.ds(slot, 1), :], dsem.at[b]),
            pltpu.make_async_copy(urow.at[pl.ds(b, 1), :], up.at[pl.ds(slot, 1), :], usem.at[b]),
        )

    def begin(b, carry):
        mine, first, second = copies(b)

        @pl.when(mine)
        def _():
            first.start()
            second.start()

        return carry

    def end(b, carry):
        mine, first, second = copies(b)

        @pl.when(mine)
        def _():
            first.wait()
            second.wait()

        return carry

    for g in range(blocks // 8):
        for i in range(8):
            dscr[pl.ds(i, per_down, stride=8), :] = dacc[8 * g + i]
            uscr[pl.ds(i, per_up, stride=8), :] = uacc[8 * g + i]
        for t in range(per_down):
            drow[8 * g : 8 * g + 8, t * LANES : (t + 1) * LANES] = dscr[8 * t : 8 * t + 8, :]
        for t in range(per_up):
            urow[8 * g : 8 * g + 8, t * LANES : (t + 1) * LANES] = uscr[8 * t : 8 * t + 8, :]
        lax.fori_loop(8 * g, 8 * g + 8, begin, 0)
    lax.fori_loop(0, blocks, end, 0)


def scatter_rows(padded_block_adapter, adapter_storage_row, recv, down, up):
    blocks = padded_block_adapter.shape[0]
    per_down, per_up = down.shape[1] // LANES, up.shape[1] // LANES
    return pl.pallas_call(
        scatter_kernel,
        in_specs=[IN_HBM, IN_HBM, IN_VMEM, IN_HBM, IN_HBM],
        out_specs=[IN_HBM, IN_HBM],
        scratch_shapes=[
            pltpu.SMEM((blocks,), jnp.int32),
            pltpu.SMEM(adapter_storage_row.shape, jnp.int32),
            pltpu.SemaphoreType.DMA((2,)),
            pltpu.SMEM((ADAPTER_GROUP,), jnp.int32),
            pltpu.VMEM((blocks, per_down, LANES), jnp.float32),
            pltpu.VMEM((blocks, per_up, LANES), jnp.float32),
            pltpu.VMEM((8 * per_down, LANES), jnp.float32),
            pltpu.VMEM((8 * per_up, LANES), jnp.float32),
            pltpu.VMEM((blocks, per_down * LANES), jnp.float32),
            pltpu.VMEM((blocks, per_up * LANES), jnp.float32),
            pltpu.SemaphoreType.DMA((blocks,)),
            pltpu.SemaphoreType.DMA((blocks,)),
        ],
        out_shape=[
            jax.ShapeDtypeStruct(down.shape, down.dtype),
            jax.ShapeDtypeStruct(up.shape, up.dtype),
        ],
        input_output_aliases={3: 0, 4: 1},
        compiler_params=PARAMS,
        cost_estimate=SMALL,
        name="scatter_rows",
    )(in_hbm(padded_block_adapter), in_hbm(adapter_storage_row), recv, down, up)


def far_kernel(count, handed, *refs):
    cots, weight, outs = refs[:count], refs[count], refs[count + 1 : 2 * count + 1]
    wbuf, buffer, wsem, sems, hsem = refs[2 * count + 1 + handed :]
    tile = wbuf.shape[1]
    loads = [
        pltpu.make_async_copy(weight.at[i * tile : (i + 1) * tile, :], wbuf.at[i], wsem.at[i])
        for i in range(wbuf.shape[0])
    ]
    for copy in loads:
        copy.start()
    stores = [pltpu.make_async_copy(buffer.at[n], outs[n], sems.at[n]) for n in range(count)]
    for i, load in enumerate(loads):
        load.wait()
        for n, cot in enumerate(cots):
            value = dot_t(cot[...], wbuf[i]).astype(buffer.dtype)
            buffer[n, :, i * tile : (i + 1) * tile] = value
            if i == len(loads) - 1:
                stores[n].start()
    if handed:
        copy = pltpu.make_async_copy(wbuf.at[lax.axis_index("parts")], refs[2 * count + 1], hsem)
        copy.start()
        copy.wait()
    for copy in stores:
        copy.wait()


def far_products(cots, weight, pin=in_hbm, handed=False):
    count, rows, tile = len(cots), cots[0].shape[0], 256
    span, depth = weight.shape
    shape = pltpu.HBM((rows, span), jnp.bfloat16)
    half = [pltpu.HBM((tile, depth), weight.dtype)] if handed else []
    return pl.pallas_call(
        functools.partial(far_kernel, count, len(half)),
        in_specs=[IN_VMEM] * count + [pl.BlockSpec(memory_space=pl.ANY)],
        out_specs=[IN_HBM] * (count + len(half)),
        out_shape=[shape] * count + half,
        scratch_shapes=[
            pltpu.VMEM((span // tile, tile, depth), weight.dtype),
            pltpu.VMEM((count, rows, span), jnp.bfloat16),
            pltpu.SemaphoreType.DMA((span // tile,)),
            pltpu.SemaphoreType.DMA((count,)),
            pltpu.SemaphoreType.DMA,
        ],
        compiler_params=PARAMS,
        cost_estimate=SMALL,
        name="far_products",
    )(*cots, pin(weight))


def finish(devices, at, cot, weights, received, g, recv, out, width, columns, pin=in_hbm, cost=SMALL):
    rows = cot.shape[0]
    spans = [w.shape[0] for w in weights] + [r.shape[1] for r in received]
    count = len(spans)
    sources = [pin(source) for source in (*weights, *received)]
    per = columns // LANES

    def kernel(cot, g, recv, *rest):
        where = column_blocks(devices)
        given = rest[:count]
        result = rest[-4 - count]
        buffer, sems, loaded = rest[-3 - count], rest[-2 - count], rest[-1 - count : -1]
        load_sems = rest[-1]
        loads = [
            pltpu.make_async_copy(given[i], loaded[i], load_sems.at[i]) for i in range(count)
        ]
        for load in loads:
            load.start()
        copies = []
        for i in range(count):
            index, span = where[at[i]], spans[i]
            per_device = columns // span
            device, inner = index // per_device, (index % per_device) * (span // LANES)
            parts = []
            for k in range(rows // BLOCK):
                tiles = []
                for q in range(span // LANES):
                    first = pl.multiple_of((k * per + inner + q) * ADAPTER_RANK, ADAPTER_RANK)
                    tiles.append(recv[device, pl.ds(first, ADAPTER_RANK), :])
                ours = g[k * BLOCK : (k + 1) * BLOCK, :ADAPTER_RANK]
                parts.append(dot_n(ours, lane_cat(tiles)))
            value = jnp.concatenate(parts, axis=0)
            loads[i].wait()
            if i < len(weights):
                value = value + dot_t(cot[...], loaded[i][...])
            else:
                value = value + loaded[i][...].astype(jnp.float32)
            buffer[i, :, :span] = value.astype(buffer.dtype)
            start = pl.multiple_of(index * span, span)
            copies.append(
                pltpu.make_async_copy(
                    buffer.at[i, :, :span], result.at[:, pl.ds(start, span)], sems.at[i]
                )
            )
            copies[-1].start()
        for copy in copies:
            copy.wait()

    return pl.pallas_call(
        kernel,
        in_specs=[IN_VMEM] * 3
        + [pl.BlockSpec(memory_space=pl.ANY)] * count
        + ([] if out is None else [IN_HBM]),
        out_specs=IN_HBM,
        out_shape=jax.ShapeDtypeStruct((rows, width), jnp.bfloat16),
        input_output_aliases={} if out is None else {3 + count: 0},
        scratch_shapes=[
            pltpu.VMEM((count, rows, max(spans)), jnp.bfloat16),
            pltpu.SemaphoreType.DMA((count,)),
        ]
        + [pltpu.VMEM(source.shape, source.dtype) for source in sources]
        + [pltpu.SemaphoreType.DMA((count,))],
        compiler_params=WIDE_PARAMS,
        cost_estimate=cost,
        name="finish",
    )(cot, g, recv, *sources, *([] if out is None else [out]))


def ring_pairs(devices):
    chips = devices // 2
    order = list(range(0, chips, 2)) + list(range(chips - 1, 0, -2))
    pairs = []
    for part in range(2):
        for i, chip in enumerate(order):
            for core in range(2):
                other = order[(i + (1 if core == part else -1)) % chips]
                pairs.append((part * devices + 2 * chip + core, part * devices + 2 * other + core))
    return pairs


def ring_body(
    inputs,
    cotangent,
    frozen_value_weight,
    adapter_down_weights,
    adapter_up_weights,
    padded_block_adapter,
    block_live_rows,
    adapter_storage_row,
    *,
    devices,
):
    steps = devices // 4
    shard = frozen_value_weight.shape[0]
    width = inputs.shape[1]
    ring = ring_pairs(devices)
    cores = [(i, i ^ 1) for i in range(devices)]
    across = [(0, 1), (1, 0)]
    diagonal = [(p * devices + i, (1 - p) * devices + (i ^ 1)) for p in range(2) for i in range(devices)]

    def cross(products):
        return (
            lax.ppermute(products[0], "fsdp", cores),
            lax.ppermute(products[1], "parts", across),
            lax.ppermute(products[2], ("parts", "fsdp"), diagonal),
        )

    other_shard = lax.ppermute(frozen_value_weight, "fsdp", cores)
    masked = mask_rows(block_live_rows, cotangent)
    core_masked = lax.ppermute(masked, "fsdp", cores)
    far_masked = lax.ppermute(masked, "parts", across)
    adapter, _ = after(padded_block_adapter, masked)
    payload = gather_rows(
        adapter, adapter_storage_row, adapter_down_weights, adapter_up_weights, devices
    )
    recv = lax.all_to_all(payload, "fsdp", split_axis=0, concat_axis=0, tiled=True)

    travelling = lax.ppermute(frozen_value_weight, ("parts", "fsdp"), ring)

    firsts = [2 + 4 * step for step in range(steps)]
    pieces, received = [], []
    for step in range(steps):
        if step == 0:
            travelling, far_masked, _ = after(travelling, far_masked, payload)
            diagonal_masked = lax.ppermute(far_masked, "fsdp", cores)
            cots = (core_masked, far_masked, diagonal_masked)
        elif step == 1:
            travelling, sent, out, grads, received[0] = after(
                travelling, sent, out, grads, received[0]
            )
        pieces.append(travelling)
        if step < steps - 2:
            travelling = lax.ppermute(travelling, ("parts", "fsdp"), ring)
        pin = as_it_is if step >= steps - 2 else in_hbm
        products = far_products(cots, pieces[step], pin, step == steps - 2)
        if step == steps - 2:
            *products, travelling = products
            travelling, products, out, received[-1] = after(
                travelling, products, out, received[-1]
            )
            travelling = lax.ppermute(travelling, ("parts", "fsdp"), ring)
            sent, products = after(sent, products)
            sums = lax.all_to_all(sent, "fsdp", split_axis=0, concat_axis=0, tiled=True)
        received.append(cross(products))
        if step == 0:
            grads = zero_grads(products[0], adapter_down_weights.shape, adapter_up_weights.shape)
            recv, _ = after(recv, grads)
            sent, g = adapter_terms(inputs, masked, recv)
            weights = (frozen_value_weight, other_shard)
            out = finish(devices, [0, 1], masked, weights, (), g, recv, None, width, shard)
        if step == steps - 3:
            cot, _ = after(masked, products[0])
            at = firsts[: step + 1] + [firsts[0] + i for i in range(1, 4)]
            out = finish(devices, at, cot, pieces[:2], received[0], g, recv, out, width, shard)
            travelling, out = after(travelling, out)
        if step == steps - 2:
            out, _ = after(out, products)
            at = [firsts[step]] + [first + i for first in firsts[1:step] for i in range(1, 4)]
            early = sum(received[1:step], ())
            piece = pieces[step : step + 1]
            out = finish(devices, at, masked, piece, early, g, recv, out, width, shard)
            travelling, out = after(travelling, out)
    at = firsts[-1:] + [firsts[-2] + i for i in range(1, 4)]
    piece = pieces[-1:]
    out = finish(
        devices, at, masked, piece, received[-2], g, recv, out, width, shard, as_it_is, LONGER
    )
    at = [firsts[-1] + i for i in range(1, 4)]
    out = finish(devices, at, masked, (), received[-1], g, recv, out, width, shard, as_it_is)
    sums, out = after(sums, out)
    down_grad, up_grad = scatter_rows(padded_block_adapter, adapter_storage_row, sums, *grads)
    return (out, down_grad, up_grad)


def after(value, *earlier):
    return lax.optimization_barrier((value,) + earlier)


def gather_body(
    inputs,
    cotangent,
    frozen_value_weight,
    adapter_down_weights,
    adapter_up_weights,
    padded_block_adapter,
    block_live_rows,
    adapter_storage_row,
):
    hidden_width = inputs.shape[1]
    kv_width = cotangent.shape[1]
    token_rows = inputs.shape[0]
    block_count = token_rows // BLOCK
    first_block = lax.axis_index("fsdp") * block_count
    live_rows = lax.dynamic_slice_in_dim(block_live_rows, first_block, block_count)
    positions = jnp.arange(BLOCK, dtype=jnp.int32)
    live_mask = positions[None, :] < live_rows[:, None]
    blocked_cot = cotangent.reshape(block_count, BLOCK, kv_width)
    masked_blocks = jnp.where(live_mask[:, :, None], blocked_cot, jnp.zeros_like(blocked_cot))
    masked = masked_blocks.reshape(token_rows, kv_width)
    block_storage_row = slot_lookup(padded_block_adapter, adapter_storage_row)
    down_weight_rows = jnp.take(adapter_down_weights, block_storage_row, axis=0)
    up_weight_rows = jnp.take(adapter_up_weights, block_storage_row, axis=0)
    down_mine, up_mine = (
        lax.all_to_all(down_weight_rows, "fsdp", split_axis=0, concat_axis=1, tiled=True),
        lax.all_to_all(up_weight_rows, "fsdp", split_axis=0, concat_axis=1, tiled=True),
    )
    frozen_gradient = lax.dot_general(
        masked,
        lax.all_gather(frozen_value_weight, "fsdp", axis=0, tiled=True),
        (((1,), (1,)), ((), ())),
        preferred_element_type=jnp.float32,
    )
    down_weight_matrix = down_mine.reshape(block_count, hidden_width, ADAPTER_RANK)
    up_weight_matrix = up_mine.reshape(block_count, ADAPTER_RANK, kv_width)
    blocked_in = inputs.reshape(block_count, BLOCK, hidden_width)
    rank_projection = jnp.einsum(
        "kbd,kdr->kbr", blocked_in, down_weight_matrix, preferred_element_type=jnp.float32
    ).astype(jnp.bfloat16)
    rank_space_gradient = jnp.einsum(
        "kbv,krv->kbr", masked_blocks, up_weight_matrix, preferred_element_type=jnp.float32
    ).astype(jnp.bfloat16)
    adapter_gradient_term = adapter_scale * jnp.einsum(
        "kbr,kdr->kbd", rank_space_gradient, down_weight_matrix, preferred_element_type=jnp.float32
    )
    input_gradient = (
        frozen_gradient + adapter_gradient_term.reshape(token_rows, hidden_width)
    ).astype(jnp.bfloat16)
    partial_down_weight = adapter_scale * jnp.einsum(
        "kbd,kbr->kdr", blocked_in, rank_space_gradient, preferred_element_type=jnp.float32
    )
    partial_up_weight = adapter_scale * jnp.einsum(
        "kbr,kbv->krv", rank_projection, masked_blocks, preferred_element_type=jnp.float32
    )
    partial_down_weight = partial_down_weight.reshape(block_count, hidden_width * ADAPTER_RANK)
    partial_up_weight = partial_up_weight.reshape(block_count, ADAPTER_RANK * kv_width)
    recv_down, recv_up = (
        lax.all_to_all(partial_down_weight, "fsdp", split_axis=1, concat_axis=0, tiled=True),
        lax.all_to_all(partial_up_weight, "fsdp", split_axis=1, concat_axis=0, tiled=True),
    )
    onehot = (
        jnp.arange(ADAPTER_GROUP, dtype=jnp.int32)[:, None] == block_storage_row[None, :]
    ).astype(jnp.float32)
    highest_precision = lax.Precision.HIGHEST
    down_grad = jnp.dot(
        onehot, recv_down, precision=highest_precision, preferred_element_type=jnp.float32
    )
    up_grad = jnp.dot(
        onehot, recv_up, precision=highest_precision, preferred_element_type=jnp.float32
    )
    return (input_gradient, down_grad, up_grad)


def solution(mesh):
    devices = mesh.shape["fsdp"]
    in_specs = (
        P(("parts", "fsdp"), None),
        P(("parts", "fsdp"), None),
        P("fsdp", None),
        P("parts", "fsdp"),
        P("parts", "fsdp"),
        P("parts"),
        P("parts"),
        P("parts"),
    )
    out_specs = (P(("parts", "fsdp"), None), P("parts", "fsdp"), P("parts", "fsdp"))

    def program(*arrays):
        shard = arrays[2].shape[0] // devices
        rows = arrays[0].shape[0] // devices // 2
        adapter_tiles = arrays[3].shape[1] // devices // LANES
        fits = rows == 2 * BLOCK and 2 * adapter_tiles == LANES and shard % 512 == 0
        if mesh.shape["parts"] == 2 and devices % 4 == 0 and fits:
            body = functools.partial(ring_body, devices=devices)
        else:
            body = gather_body
        return jax.shard_map(
            body, mesh=mesh, in_specs=in_specs, out_specs=out_specs, check_vma=False
        )(*arrays)

    return program
```

```python
import functools

import jax
import jax.numpy as jnp
from jax import lax
from jax.experimental import pallas as pl
from jax.experimental.pallas import tpu as pltpu
from jax.sharding import PartitionSpec as P

ADAPTER_RANK = 16
ADAPTER_GROUP = 512
BLOCK = 128
LANES = 128
MIB = 1024 * 1024
ZERO_ROWS = 64
PARAMS = pltpu.CompilerParams(vmem_limit_bytes=16 * MIB)
WIDE_PARAMS = pltpu.CompilerParams(vmem_limit_bytes=24 * MIB)
IN_VMEM = pl.BlockSpec(memory_space=pltpu.VMEM)
IN_SMEM = pl.BlockSpec(memory_space=pltpu.SMEM)
IN_HBM = pl.BlockSpec(memory_space=pltpu.HBM)
SMALL = pl.CostEstimate(flops=1, bytes_accessed=1, transcendentals=0)
LONGER = pl.CostEstimate(flops=10_000_000_000, bytes_accessed=1, transcendentals=0)

adapter_scale = 2.0


def slot_lookup(padded_block_adapter, adapter_storage_row):
    matches = padded_block_adapter[:, None] == jnp.arange(ADAPTER_GROUP, dtype=jnp.int32)[None, :]
    return jnp.sum(jnp.where(matches, adapter_storage_row[None, :], 0), axis=1)


def in_hbm(value):
    return pltpu.with_memory_space_constraint(value, pltpu.HBM)


def as_it_is(value):
    return value


def column_blocks(devices):
    index, part = lax.axis_index("fsdp"), lax.axis_index("parts")
    chips = devices // 2
    chip, core = lax.div(index, 2), lax.rem(index, 2)
    way = jnp.where(core == part, -1, 1)
    odd = lax.rem(chip, 2) == 1
    place = jnp.where(odd, chips - lax.div(chip + 1, 2), lax.div(chip, 2))

    def at(steps):
        position = lax.rem(place + steps + chips, chips)
        return jnp.where(position < chips // 2, 2 * position, 2 * (chips - position) - 1)

    blocks = [index, index + 1 - 2 * core]
    for step in range(1, chips // 2):
        near, far = at(way * step), at(-way * step)
        blocks += [2 * near + core, 2 * far + 1 - core, 2 * far + core, 2 * near + 1 - core]
    last = at(chips // 2)
    for p in (part, 1 - part):
        blocks += [2 * (2 * last + core) + p, 2 * (2 * last + 1 - core) + p]
    return blocks


def iota(shape, axis):
    return lax.broadcasted_iota(jnp.int32, shape, axis)


def dot_t(a, b):
    return lax.dot_general(a, b, (((1,), (1,)), ((), ())), preferred_element_type=jnp.float32)


def dot_n(a, b, precision=None):
    return lax.dot_general(
        a, b, (((1,), (0,)), ((), ())), precision=precision, preferred_element_type=jnp.float32
    )


def dot_0(a, b):
    return lax.dot_general(a, b, (((0,), (0,)), ((), ())), preferred_element_type=jnp.float32)


def lane_cat(parts):
    return jnp.concatenate(parts, axis=-1)


def mask_kernel(live, cot, out):
    first = lax.axis_index("fsdp") * (cot.shape[0] // BLOCK)
    row = iota((BLOCK, cot.shape[1]), 0)
    for k in range(cot.shape[0] // BLOCK):
        rows = slice(k * BLOCK, (k + 1) * BLOCK)
        value = cot[rows, :].astype(jnp.float32)
        out[rows, :] = jnp.where(row < live[first + k], value, 0.0).astype(out.dtype)


def mask_rows(block_live_rows, cotangent):
    return pl.pallas_call(
        mask_kernel,
        in_specs=[IN_SMEM, IN_VMEM],
        out_specs=IN_VMEM,
        out_shape=jax.ShapeDtypeStruct(cotangent.shape, cotangent.dtype),
        compiler_params=PARAMS,
        cost_estimate=SMALL,
        name="mask_rows",
    )(in_hbm(block_live_rows), in_hbm(cotangent))


def rank_major_order():
    shape = (8 * LANES, 8 * LANES)
    a, b = iota(shape, 0), iota(shape, 1)
    return ((a % LANES) * 8 + a // LANES == b).astype(jnp.bfloat16)


def gather_kernel(
    adapter, storage, down, up, result, dbuf, ubuf, dscr, uscr, cols, payload, dsem, usem, rsem
):
    blocks = adapter.shape[0]
    devices = result.shape[0]
    group = dbuf.shape[1]
    per_down, per_up = down.shape[1] // LANES, up.shape[1] // LANES
    down_rows = 2 * per_down

    def copies(b):
        slot = storage[adapter[b]]
        start = pl.multiple_of((slot // group) * group, group)
        return (
            slot % group,
            start,
            pltpu.make_async_copy(down.at[pl.ds(start, group), :], dbuf.at[b], dsem.at[b]),
        )

    def begin(b, carry):
        copies(b)[2].start()
        return carry

    ups = pltpu.make_async_copy(up, ubuf, usem)
    ups.start()
    lax.fori_loop(0, blocks, begin, 0)
    order = rank_major_order()

    def one(j, carry):
        wide, narrow = [], []
        for k in range(2):
            b = 2 * j + k
            row, start, copy = copies(b)
            copy.wait()
            late = row >= 8
            line = row % 8
            value = dbuf[b].astype(jnp.float32)
            value = jnp.where(late, value[8:], value[:8])
            for t in range(per_down):
                dscr[k, 8 * t : 8 * t + 8, :] = value[:, t * LANES : (t + 1) * LANES]
            wide.append(dscr[k, pl.ds(line, per_down, stride=8), :])
            value = ubuf[pl.ds(start, group), :].astype(jnp.float32)
            value = jnp.where(late, value[8:], value[:8])
            for t in range(per_up):
                uscr[k, 8 * t : 8 * t + 8, :] = value[:, t * LANES : (t + 1) * LANES]
            narrow.append(uscr[k, pl.ds(line, per_up, stride=8), :])
        turned = jnp.concatenate(wide, axis=0).T
        start = pl.multiple_of(j * ADAPTER_RANK, ADAPTER_RANK)
        for lo in range(8):
            piece = turned[lo * ADAPTER_RANK : (lo + 1) * ADAPTER_RANK, :]
            cols[pl.ds(start, ADAPTER_RANK), lo * LANES : (lo + 1) * LANES] = piece.astype(cols.dtype)
        payload[j, down_rows:, :] = jnp.concatenate(narrow, axis=0).astype(payload.dtype)
        return carry

    ups.wait()
    stores = []
    parts = 2
    count = devices // parts
    for h in range(parts):
        lax.fori_loop(h * count, h * count + count, one, 0)
        rows = slice(h * count * ADAPTER_RANK, (h + 1) * count * ADAPTER_RANK)
        value = dot_n(cols[rows, :], order).astype(payload.dtype)
        value = value.reshape(count, ADAPTER_RANK, 8 * LANES)
        here = slice(h * count, h * count + count)
        for q in range(8):
            payload[here, q * ADAPTER_RANK : (q + 1) * ADAPTER_RANK, :] = value[
                :, :, q * LANES : (q + 1) * LANES
            ]
        part = pl.ds(h * count, count)
        stores.append(pltpu.make_async_copy(payload.at[part], result.at[part], rsem.at[h]))
        stores[-1].start()
    for copy in stores:
        copy.wait()


def gather_rows(padded_block_adapter, adapter_storage_row, down, up, devices):
    blocks = padded_block_adapter.shape[0]
    per_down, per_up = down.shape[1] // LANES, up.shape[1] // LANES
    group = 16
    rows = 2 * (per_down + per_up)
    shape = (devices, rows, LANES)
    return pl.pallas_call(
        gather_kernel,
        in_specs=[IN_SMEM, IN_SMEM, IN_HBM, IN_HBM],
        out_specs=IN_HBM,
        out_shape=jax.ShapeDtypeStruct(shape, jnp.bfloat16),
        scratch_shapes=[
            pltpu.VMEM((blocks, group, down.shape[1]), down.dtype),
            pltpu.VMEM(up.shape, up.dtype),
            pltpu.VMEM((2, 8 * per_down, LANES), jnp.float32),
            pltpu.VMEM((2, 8 * per_up, LANES), jnp.float32),
            pltpu.VMEM((devices * ADAPTER_RANK, 8 * LANES), jnp.bfloat16),
            pltpu.VMEM(shape, jnp.bfloat16),
            pltpu.SemaphoreType.DMA((blocks,)),
            pltpu.SemaphoreType.DMA,
            pltpu.SemaphoreType.DMA((2,)),
        ],
        compiler_params=WIDE_PARAMS,
        cost_estimate=SMALL,
        name="gather_rows",
    )(in_hbm(padded_block_adapter), in_hbm(adapter_storage_row), in_hbm(down), in_hbm(up))


def adapter_kernel(x, cot, recv, result, g_out, xbuf, sent, xsem, rsem):
    devices = recv.shape[0]
    blocks = x.shape[0] // BLOCK
    steps = xbuf.shape[0]
    span = xbuf.shape[2]
    tiles = cot.shape[1] // LANES
    up_chunk = tiles * ADAPTER_RANK // devices
    down_rows = recv.shape[1] - blocks * up_chunk
    per = down_rows // blocks // ADAPTER_RANK
    here = span // LANES // per

    loads = [
        pltpu.make_async_copy(x.at[:, i * span : (i + 1) * span], xbuf.at[i], xsem.at[i])
        for i in range(steps)
    ]
    for copy in loads:
        copy.start()
    lane = iota((BLOCK, LANES), 1)
    gather_rank = (iota((LANES, LANES), 0) // 8 == iota((LANES, LANES), 1)).astype(jnp.float32)
    b_all = recv[:, down_rows:, :].astype(jnp.float32)
    turned = []
    for k in range(blocks):
        m = cot[k * BLOCK : (k + 1) * BLOCK, :]
        b_flat = b_all[:, k * up_chunk : (k + 1) * up_chunk, :].reshape(LANES, LANES)
        b_flat = b_flat.astype(jnp.bfloat16)
        total = jnp.zeros((BLOCK, LANES), jnp.float32)
        for t in range(tiles):
            part = dot_t(m[:, t * LANES : (t + 1) * LANES], b_flat)
            total = total + jnp.where(lane % tiles == t, part, 0.0)
        g = dot_n(total, gather_rank, lax.Precision.HIGHEST).astype(jnp.bfloat16)
        g = (adapter_scale * g.astype(jnp.float32)).astype(jnp.bfloat16)
        g_out[k * BLOCK : (k + 1) * BLOCK, :] = g
        turned.append(g.astype(jnp.float32).T[:ADAPTER_RANK, :].astype(jnp.bfloat16))

    stores = []
    lows = [jnp.zeros((BLOCK, ADAPTER_RANK), jnp.float32) for _ in range(blocks)]
    for i in range(steps):
        loads[i].wait()
        for k in range(blocks):
            part = xbuf[i, k * BLOCK : (k + 1) * BLOCK, :]
            first = k * per * ADAPTER_RANK
            spots = [
                (i * here + j, first + q * ADAPTER_RANK) for j in range(here) for q in range(per)
            ]
            a = lane_cat([recv[j, at : at + ADAPTER_RANK, :] for j, at in spots])
            lows[k] = lows[k] + dot_t(part, a)
            grad = dot_n(turned[k], part).astype(sent.dtype)
            for tile, (j, at) in enumerate(spots):
                sent[j, at : at + ADAPTER_RANK, :] = grad[:, tile * LANES : (tile + 1) * LANES]
        part = (pl.ds(i * here, here), pl.ds(0, down_rows), slice(None))
        stores.append(pltpu.make_async_copy(sent.at[part], result.at[part], rsem.at[i]))
        stores[-1].start()

    ups = []
    row = iota((LANES, LANES), 0)
    spread = (iota((ADAPTER_RANK, LANES), 1) // 8 == iota((ADAPTER_RANK, LANES), 0)).astype(
        jnp.bfloat16
    )
    for k in range(blocks):
        low8 = dot_n(lows[k].astype(jnp.bfloat16), spread).astype(jnp.bfloat16)
        up = dot_0(low8, cot[k * BLOCK : (k + 1) * BLOCK, :])
        flat = jnp.zeros((LANES, LANES), jnp.float32)
        for t in range(tiles):
            flat = flat + jnp.where(row % tiles == t, up[:, t * LANES : (t + 1) * LANES], 0.0)
        ups.append((adapter_scale * flat).reshape(devices, up_chunk, LANES))
    sent[:, down_rows:, :] = jnp.concatenate(ups, axis=1).astype(sent.dtype)
    part = (slice(None), pl.ds(down_rows, sent.shape[1] - down_rows), slice(None))
    stores.append(pltpu.make_async_copy(sent.at[part], result.at[part], rsem.at[steps]))
    stores[-1].start()
    for copy in stores:
        copy.wait()


def adapter_terms(x, cot, recv):
    rows, width = x.shape
    steps = 8
    return pl.pallas_call(
        adapter_kernel,
        in_specs=[IN_HBM, IN_VMEM, IN_VMEM],
        out_specs=[IN_HBM, IN_VMEM],
        out_shape=[
            pltpu.HBM(recv.shape, jnp.bfloat16),
            jax.ShapeDtypeStruct((rows, LANES), jnp.bfloat16),
        ],
        scratch_shapes=[
            pltpu.VMEM((steps, rows, width // steps), x.dtype),
            pltpu.VMEM(recv.shape, jnp.bfloat16),
            pltpu.SemaphoreType.DMA((steps,)),
            pltpu.SemaphoreType.DMA((steps + 1,)),
        ],
        compiler_params=PARAMS,
        cost_estimate=SMALL,
        name="adapter_terms",
    )(in_hbm(x), cot, recv)


def zero_kernel(_, down, up, zeros, dsem, usem):
    zeros[...] = jnp.zeros_like(zeros)
    copies = []
    for i in range(down.shape[0] // ZERO_ROWS):
        rows = pl.ds(i * ZERO_ROWS, ZERO_ROWS)
        part = zeros.at[:, : up.shape[1]]
        copies.append(pltpu.make_async_copy(zeros, down.at[rows, :], dsem.at[i]))
        copies.append(pltpu.make_async_copy(part, up.at[rows, :], usem.at[i]))
    for copy in copies:
        copy.start()
    for copy in copies:
        copy.wait()


def zero_grads(earlier, down_shape, up_shape):
    count = down_shape[0] // ZERO_ROWS
    return pl.pallas_call(
        zero_kernel,
        in_specs=[pl.BlockSpec(memory_space=pl.ANY)],
        out_specs=[IN_HBM, IN_HBM],
        out_shape=[
            jax.ShapeDtypeStruct(down_shape, jnp.float32),
            jax.ShapeDtypeStruct(up_shape, jnp.float32),
        ],
        scratch_shapes=[
            pltpu.VMEM((ZERO_ROWS, down_shape[1]), jnp.float32),
            pltpu.SemaphoreType.DMA((count,)),
            pltpu.SemaphoreType.DMA((count,)),
        ],
        compiler_params=PARAMS,
        cost_estimate=SMALL,
        name="zero_grads",
    )(in_hbm(earlier))


def scatter_kernel(
    adapter_hbm, storage_hbm, recv, _down, _up, down, up, adapter, storage, isem, table, dacc, uacc, dscr, uscr, drow, urow, dsem, usem
):
    blocks = adapter_hbm.shape[0]
    devices = recv.shape[0]
    per_down, per_up = down.shape[1] // LANES, up.shape[1] // LANES
    down_rows = 2 * per_down

    indices = [
        pltpu.make_async_copy(adapter_hbm, adapter, isem.at[0]),
        pltpu.make_async_copy(storage_hbm, storage, isem.at[1]),
    ]
    for copy in indices:
        copy.start()
    dacc[...] = jnp.zeros_like(dacc)
    uacc[...] = jnp.zeros_like(uacc)
    count = 8 * per_down
    a, b = iota((count, count), 0), iota((count, count), 1)
    order = ((b % per_down) * 8 + b // per_down == a).astype(jnp.bfloat16)
    values = []
    for k in range(2):
        tiles = [
            recv[:, q * ADAPTER_RANK : (q + 1) * ADAPTER_RANK, :] for q in range(4 * k, 4 * k + 4)
        ]
        values.append(dot_n(lane_cat(tiles).reshape(devices * ADAPTER_RANK, count), order))
    for copy in indices:
        copy.wait()

    def mark(i, carry):
        b = blocks - 1 - i
        table[storage[adapter[b]]] = b
        return carry

    lax.fori_loop(0, blocks, mark, 0)
    lower = iota((ADAPTER_RANK, LANES), 1) < per_down
    for j in range(devices):
        rows = []
        for t in range(4):
            first, second = [
                value[j * ADAPTER_RANK : (j + 1) * ADAPTER_RANK, t * LANES : (t + 1) * LANES]
                for value in values
            ]
            rows.append(jnp.where(lower, first, pltpu.roll(second, per_down, 1)))
            rows.append(jnp.where(lower, pltpu.roll(first, per_down, 1), second))
        turned = jnp.concatenate(rows, axis=0).T
        narrow = recv[j, down_rows:, :].astype(jnp.float32)
        for k in range(2):
            first = table[storage[adapter[2 * j + k]]]
            dacc[first] += turned[k * per_down : (k + 1) * per_down, :]
            uacc[first] += narrow[k * per_up : (k + 1) * per_up, :]
    def copies(b):
        slot = storage[adapter[b]]
        return (
            table[slot] == b,
            pltpu.make_async_copy(drow.at[pl.ds(b, 1), :], down.at[pl.ds(slot, 1), :], dsem.at[b]),
            pltpu.make_async_copy(urow.at[pl.ds(b, 1), :], up.at[pl.ds(slot, 1), :], usem.at[b]),
        )

    def begin(b, carry):
        mine, first, second = copies(b)

        @pl.when(mine)
        def _():
            first.start()
            second.start()

        return carry

    def end(b, carry):
        mine, first, second = copies(b)

        @pl.when(mine)
        def _():
            first.wait()
            second.wait()

        return carry

    for g in range(blocks // 8):
        for i in range(8):
            dscr[pl.ds(i, per_down, stride=8), :] = dacc[8 * g + i]
            uscr[pl.ds(i, per_up, stride=8), :] = uacc[8 * g + i]
        for t in range(per_down):
            drow[8 * g : 8 * g + 8, t * LANES : (t + 1) * LANES] = dscr[8 * t : 8 * t + 8, :]
        for t in range(per_up):
            urow[8 * g : 8 * g + 8, t * LANES : (t + 1) * LANES] = uscr[8 * t : 8 * t + 8, :]
        lax.fori_loop(8 * g, 8 * g + 8, begin, 0)
    lax.fori_loop(0, blocks, end, 0)


def scatter_rows(padded_block_adapter, adapter_storage_row, recv, down, up):
    blocks = padded_block_adapter.shape[0]
    per_down, per_up = down.shape[1] // LANES, up.shape[1] // LANES
    return pl.pallas_call(
        scatter_kernel,
        in_specs=[IN_HBM, IN_HBM, IN_VMEM, IN_HBM, IN_HBM],
        out_specs=[IN_HBM, IN_HBM],
        scratch_shapes=[
            pltpu.SMEM((blocks,), jnp.int32),
            pltpu.SMEM(adapter_storage_row.shape, jnp.int32),
            pltpu.SemaphoreType.DMA((2,)),
            pltpu.SMEM((ADAPTER_GROUP,), jnp.int32),
            pltpu.VMEM((blocks, per_down, LANES), jnp.float32),
            pltpu.VMEM((blocks, per_up, LANES), jnp.float32),
            pltpu.VMEM((8 * per_down, LANES), jnp.float32),
            pltpu.VMEM((8 * per_up, LANES), jnp.float32),
            pltpu.VMEM((blocks, per_down * LANES), jnp.float32),
            pltpu.VMEM((blocks, per_up * LANES), jnp.float32),
            pltpu.SemaphoreType.DMA((blocks,)),
            pltpu.SemaphoreType.DMA((blocks,)),
        ],
        out_shape=[
            jax.ShapeDtypeStruct(down.shape, down.dtype),
            jax.ShapeDtypeStruct(up.shape, up.dtype),
        ],
        input_output_aliases={3: 0, 4: 1},
        compiler_params=PARAMS,
        cost_estimate=SMALL,
        name="scatter_rows",
    )(in_hbm(padded_block_adapter), in_hbm(adapter_storage_row), recv, down, up)


def far_kernel(count, handed, *refs):
    cots, weight, outs = refs[:count], refs[count], refs[count + 1 : 2 * count + 1]
    wbuf, wsem, sems, hsem, *buffers = refs[2 * count + 1 + handed :]
    tile = wbuf.shape[1]
    loads = [
        pltpu.make_async_copy(weight.at[i * tile : (i + 1) * tile, :], wbuf.at[i], wsem.at[i])
        for i in range(wbuf.shape[0])
    ]
    for copy in loads:
        copy.start()
    stores = [pltpu.make_async_copy(buffers[n], outs[n], sems.at[n]) for n in range(count)]
    for i, load in enumerate(loads):
        load.wait()
        for n, cot in enumerate(cots):
            value = dot_t(cot[...], wbuf[i]).astype(buffers[n].dtype)
            buffers[n][:, i * tile : (i + 1) * tile] = value
            if i == len(loads) - 1:
                stores[n].start()
    if handed:
        copy = pltpu.make_async_copy(wbuf.at[lax.axis_index("parts")], refs[2 * count + 1], hsem)
        copy.start()
        copy.wait()
    for copy in stores:
        copy.wait()


def far_products(cots, weight, pin=in_hbm, handed=False, owned=False):
    count, rows, tile = len(cots), cots[0].shape[0], 256
    span, depth = weight.shape
    types = [jnp.bfloat16] * count
    if owned:
        types[-1] = jnp.float32
    half = [pltpu.HBM((tile, depth), weight.dtype)] if handed else []
    return pl.pallas_call(
        functools.partial(far_kernel, count, len(half)),
        in_specs=[IN_VMEM] * count + [pl.BlockSpec(memory_space=pl.ANY)],
        out_specs=[IN_HBM] * (count + len(half)),
        out_shape=[pltpu.HBM((rows, span), kind) for kind in types] + half,
        scratch_shapes=[
            pltpu.VMEM((span // tile, tile, depth), weight.dtype),
            pltpu.SemaphoreType.DMA((span // tile,)),
            pltpu.SemaphoreType.DMA((count,)),
            pltpu.SemaphoreType.DMA,
        ]
        + [pltpu.VMEM((rows, span), kind) for kind in types],
        compiler_params=PARAMS,
        cost_estimate=SMALL,
        name="far_products",
    )(*cots, pin(weight))


def finish(devices, at, cot, weights, received, g, recv, out, width, columns, pin=in_hbm, cost=SMALL):
    rows = cot.shape[0]
    spans = [w.shape[0] for w in weights] + [r.shape[1] for r in received]
    count = len(spans)
    sources = [pin(source) for source in (*weights, *received)]
    per = columns // LANES

    def kernel(cot, g, recv, *rest):
        where = column_blocks(devices)
        given = rest[:count]
        result = rest[-4 - count]
        buffer, sems, loaded = rest[-3 - count], rest[-2 - count], rest[-1 - count : -1]
        load_sems = rest[-1]
        loads = [
            pltpu.make_async_copy(given[i], loaded[i], load_sems.at[i]) for i in range(count)
        ]
        for load in loads:
            load.start()
        copies = []
        for i in range(count):
            index, span = where[at[i]], spans[i]
            per_device = columns // span
            device, inner = index // per_device, (index % per_device) * (span // LANES)
            parts = []
            for k in range(rows // BLOCK):
                tiles = []
                for q in range(span // LANES):
                    first = pl.multiple_of((k * per + inner + q) * ADAPTER_RANK, ADAPTER_RANK)
                    tiles.append(recv[device, pl.ds(first, ADAPTER_RANK), :])
                ours = g[k * BLOCK : (k + 1) * BLOCK, :ADAPTER_RANK]
                parts.append(dot_n(ours, lane_cat(tiles)))
            value = jnp.concatenate(parts, axis=0)
            loads[i].wait()
            if i < len(weights):
                value = value + dot_t(cot[...], loaded[i][...])
            else:
                value = value + loaded[i][...].astype(jnp.float32)
            buffer[i, :, :span] = value.astype(buffer.dtype)
            start = pl.multiple_of(index * span, span)
            copies.append(
                pltpu.make_async_copy(
                    buffer.at[i, :, :span], result.at[:, pl.ds(start, span)], sems.at[i]
                )
            )
            copies[-1].start()
        for copy in copies:
            copy.wait()

    return pl.pallas_call(
        kernel,
        in_specs=[IN_VMEM] * 3
        + [pl.BlockSpec(memory_space=pl.ANY)] * count
        + ([] if out is None else [IN_HBM]),
        out_specs=IN_HBM,
        out_shape=jax.ShapeDtypeStruct((rows, width), jnp.bfloat16),
        input_output_aliases={} if out is None else {3 + count: 0},
        scratch_shapes=[
            pltpu.VMEM((count, rows, max(spans)), jnp.bfloat16),
            pltpu.SemaphoreType.DMA((count,)),
        ]
        + [pltpu.VMEM(source.shape, source.dtype) for source in sources]
        + [pltpu.SemaphoreType.DMA((count,))],
        compiler_params=WIDE_PARAMS,
        cost_estimate=cost,
        name="finish",
    )(cot, g, recv, *sources, *([] if out is None else [out]))


def ring_pairs(devices):
    chips = devices // 2
    order = list(range(0, chips, 2)) + list(range(chips - 1, 0, -2))
    pairs = []
    for part in range(2):
        for i, chip in enumerate(order):
            for core in range(2):
                other = order[(i + (1 if core == part else -1)) % chips]
                pairs.append((part * devices + 2 * chip + core, part * devices + 2 * other + core))
    return pairs


def ring_body(
    inputs,
    cotangent,
    frozen_value_weight,
    adapter_down_weights,
    adapter_up_weights,
    padded_block_adapter,
    block_live_rows,
    adapter_storage_row,
    *,
    devices,
):
    steps = devices // 4
    shard = frozen_value_weight.shape[0]
    width = inputs.shape[1]
    ring = ring_pairs(devices)
    cores = [(i, i ^ 1) for i in range(devices)]
    across = [(0, 1), (1, 0)]
    diagonal = [(p * devices + i, (1 - p) * devices + (i ^ 1)) for p in range(2) for i in range(devices)]

    def cross(products):
        return (
            lax.ppermute(products[0], "fsdp", cores),
            lax.ppermute(products[1], "parts", across),
            lax.ppermute(products[2], ("parts", "fsdp"), diagonal),
        )

    other_shard = lax.ppermute(frozen_value_weight, "fsdp", cores)
    masked = mask_rows(block_live_rows, cotangent)
    core_masked = lax.ppermute(masked, "fsdp", cores)
    far_masked = lax.ppermute(masked, "parts", across)
    adapter, _ = after(padded_block_adapter, masked)
    payload = gather_rows(
        adapter, adapter_storage_row, adapter_down_weights, adapter_up_weights, devices
    )
    recv = lax.all_to_all(payload, "fsdp", split_axis=0, concat_axis=0, tiled=True)

    travelling = lax.ppermute(frozen_value_weight, ("parts", "fsdp"), ring)

    firsts = [2 + 4 * step for step in range(steps)]
    pieces, received = [], []
    for step in range(steps):
        if step == 0:
            travelling, far_masked, _ = after(travelling, far_masked, payload)
            diagonal_masked = lax.ppermute(far_masked, "fsdp", cores)
            cots = (core_masked, far_masked, diagonal_masked)
        elif step == 1:
            travelling, sent, out, grads, received[0] = after(
                travelling, sent, out, grads, received[0]
            )
        pieces.append(travelling)
        if step < steps - 2:
            travelling = lax.ppermute(travelling, ("parts", "fsdp"), ring)
        pin = as_it_is if step >= steps - 2 else in_hbm
        owned = step >= steps - 2
        if owned:
            cots = (*cots[:3], masked)
        products = far_products(cots, pieces[step], pin, step == steps - 2, owned)
        if step == steps - 2:
            *products, own, travelling = products
            travelling, products, out, received[-1] = after(
                travelling, products, out, received[-1]
            )
            travelling = lax.ppermute(travelling, ("parts", "fsdp"), ring)
            sent, products = after(sent, products)
            sums = lax.all_to_all(sent, "fsdp", split_axis=0, concat_axis=0, tiled=True)
        if step == steps - 1:
            *products, last_own = products
        received.append(cross(products))
        if step == 0:
            grads = zero_grads(products[0], adapter_down_weights.shape, adapter_up_weights.shape)
            recv, _ = after(recv, grads)
            sent, g = adapter_terms(inputs, masked, recv)
            weights = (frozen_value_weight, other_shard)
            out = finish(devices, [0, 1], masked, weights, (), g, recv, None, width, shard)
        if step == steps - 3:
            cot, _ = after(masked, products[0])
            at = firsts[: step + 1] + [firsts[0] + i for i in range(1, 4)]
            out = finish(devices, at, cot, pieces[:2], received[0], g, recv, out, width, shard)
            travelling, out = after(travelling, out)
        if step == steps - 2:
            out, _ = after(out, products)
            at = [firsts[step]] + [first + i for first in firsts[1:step] for i in range(1, 4)]
            early = (own, *sum(received[1:step], ()))
            out = finish(devices, at, masked, (), early, g, recv, out, width, shard)
            travelling, out = after(travelling, out)
    at = firsts[-1:] + [firsts[-2] + i for i in range(1, 4)]
    late = (last_own, *received[-2])
    out = finish(devices, at, masked, (), late, g, recv, out, width, shard, in_hbm, LONGER)
    at = [firsts[-1] + i for i in range(1, 4)]
    out = finish(devices, at, masked, (), received[-1], g, recv, out, width, shard, as_it_is)
    sums, out = after(sums, out)
    down_grad, up_grad = scatter_rows(padded_block_adapter, adapter_storage_row, sums, *grads)
    return (out, down_grad, up_grad)


def after(value, *earlier):
    return lax.optimization_barrier((value,) + earlier)


def gather_body(
    inputs,
    cotangent,
    frozen_value_weight,
    adapter_down_weights,
    adapter_up_weights,
    padded_block_adapter,
    block_live_rows,
    adapter_storage_row,
):
    hidden_width = inputs.shape[1]
    kv_width = cotangent.shape[1]
    token_rows = inputs.shape[0]
    block_count = token_rows // BLOCK
    first_block = lax.axis_index("fsdp") * block_count
    live_rows = lax.dynamic_slice_in_dim(block_live_rows, first_block, block_count)
    positions = jnp.arange(BLOCK, dtype=jnp.int32)
    live_mask = positions[None, :] < live_rows[:, None]
    blocked_cot = cotangent.reshape(block_count, BLOCK, kv_width)
    masked_blocks = jnp.where(live_mask[:, :, None], blocked_cot, jnp.zeros_like(blocked_cot))
    masked = masked_blocks.reshape(token_rows, kv_width)
    block_storage_row = slot_lookup(padded_block_adapter, adapter_storage_row)
    down_weight_rows = jnp.take(adapter_down_weights, block_storage_row, axis=0)
    up_weight_rows = jnp.take(adapter_up_weights, block_storage_row, axis=0)
    down_mine, up_mine = (
        lax.all_to_all(down_weight_rows, "fsdp", split_axis=0, concat_axis=1, tiled=True),
        lax.all_to_all(up_weight_rows, "fsdp", split_axis=0, concat_axis=1, tiled=True),
    )
    frozen_gradient = lax.dot_general(
        masked,
        lax.all_gather(frozen_value_weight, "fsdp", axis=0, tiled=True),
        (((1,), (1,)), ((), ())),
        preferred_element_type=jnp.float32,
    )
    down_weight_matrix = down_mine.reshape(block_count, hidden_width, ADAPTER_RANK)
    up_weight_matrix = up_mine.reshape(block_count, ADAPTER_RANK, kv_width)
    blocked_in = inputs.reshape(block_count, BLOCK, hidden_width)
    rank_projection = jnp.einsum(
        "kbd,kdr->kbr", blocked_in, down_weight_matrix, preferred_element_type=jnp.float32
    ).astype(jnp.bfloat16)
    rank_space_gradient = jnp.einsum(
        "kbv,krv->kbr", masked_blocks, up_weight_matrix, preferred_element_type=jnp.float32
    ).astype(jnp.bfloat16)
    adapter_gradient_term = adapter_scale * jnp.einsum(
        "kbr,kdr->kbd", rank_space_gradient, down_weight_matrix, preferred_element_type=jnp.float32
    )
    input_gradient = (
        frozen_gradient + adapter_gradient_term.reshape(token_rows, hidden_width)
    ).astype(jnp.bfloat16)
    partial_down_weight = adapter_scale * jnp.einsum(
        "kbd,kbr->kdr", blocked_in, rank_space_gradient, preferred_element_type=jnp.float32
    )
    partial_up_weight = adapter_scale * jnp.einsum(
        "kbr,kbv->krv", rank_projection, masked_blocks, preferred_element_type=jnp.float32
    )
    partial_down_weight = partial_down_weight.reshape(block_count, hidden_width * ADAPTER_RANK)
    partial_up_weight = partial_up_weight.reshape(block_count, ADAPTER_RANK * kv_width)
    recv_down, recv_up = (
        lax.all_to_all(partial_down_weight, "fsdp", split_axis=1, concat_axis=0, tiled=True),
        lax.all_to_all(partial_up_weight, "fsdp", split_axis=1, concat_axis=0, tiled=True),
    )
    onehot = (
        jnp.arange(ADAPTER_GROUP, dtype=jnp.int32)[:, None] == block_storage_row[None, :]
    ).astype(jnp.float32)
    highest_precision = lax.Precision.HIGHEST
    down_grad = jnp.dot(
        onehot, recv_down, precision=highest_precision, preferred_element_type=jnp.float32
    )
    up_grad = jnp.dot(
        onehot, recv_up, precision=highest_precision, preferred_element_type=jnp.float32
    )
    return (input_gradient, down_grad, up_grad)


def solution(mesh):
    devices = mesh.shape["fsdp"]
    in_specs = (
        P(("parts", "fsdp"), None),
        P(("parts", "fsdp"), None),
        P("fsdp", None),
        P("parts", "fsdp"),
        P("parts", "fsdp"),
        P("parts"),
        P("parts"),
        P("parts"),
    )
    out_specs = (P(("parts", "fsdp"), None), P("parts", "fsdp"), P("parts", "fsdp"))

    def program(*arrays):
        shard = arrays[2].shape[0] // devices
        rows = arrays[0].shape[0] // devices // 2
        adapter_tiles = arrays[3].shape[1] // devices // LANES
        fits = rows == 2 * BLOCK and 2 * adapter_tiles == LANES and shard % 512 == 0
        if mesh.shape["parts"] == 2 and devices % 4 == 0 and fits:
            body = functools.partial(ring_body, devices=devices)
        else:
            body = gather_body
        return jax.shard_map(
            body, mesh=mesh, in_specs=in_specs, out_specs=out_specs, check_vma=False
        )(*arrays)

    return program
```

```python
import functools

import jax
import jax.numpy as jnp
from jax import lax
from jax.experimental import pallas as pl
from jax.experimental.pallas import tpu as pltpu
from jax.sharding import PartitionSpec as P

ADAPTER_RANK = 16
ADAPTER_GROUP = 512
BLOCK = 128
LANES = 128
MIB = 1024 * 1024
ZERO_ROWS = 64
PARAMS = pltpu.CompilerParams(vmem_limit_bytes=16 * MIB)
WIDE_PARAMS = pltpu.CompilerParams(vmem_limit_bytes=24 * MIB)
IN_VMEM = pl.BlockSpec(memory_space=pltpu.VMEM)
IN_SMEM = pl.BlockSpec(memory_space=pltpu.SMEM)
IN_HBM = pl.BlockSpec(memory_space=pltpu.HBM)
SMALL = pl.CostEstimate(flops=1, bytes_accessed=1, transcendentals=0)
LONGER = pl.CostEstimate(flops=10_000_000_000, bytes_accessed=1, transcendentals=0)

adapter_scale = 2.0


def slot_lookup(padded_block_adapter, adapter_storage_row):
    matches = padded_block_adapter[:, None] == jnp.arange(ADAPTER_GROUP, dtype=jnp.int32)[None, :]
    return jnp.sum(jnp.where(matches, adapter_storage_row[None, :], 0), axis=1)


def in_hbm(value):
    return pltpu.with_memory_space_constraint(value, pltpu.HBM)


def as_it_is(value):
    return value


def column_blocks(devices):
    index, part = lax.axis_index("fsdp"), lax.axis_index("parts")
    chips = devices // 2
    chip, core = lax.div(index, 2), lax.rem(index, 2)
    way = jnp.where(core == part, -1, 1)
    odd = lax.rem(chip, 2) == 1
    place = jnp.where(odd, chips - lax.div(chip + 1, 2), lax.div(chip, 2))

    def at(steps):
        position = lax.rem(place + steps + chips, chips)
        return jnp.where(position < chips // 2, 2 * position, 2 * (chips - position) - 1)

    blocks = [index, index + 1 - 2 * core]
    for step in range(1, chips // 2):
        near, far = at(way * step), at(-way * step)
        blocks += [2 * near + core, 2 * far + 1 - core, 2 * far + core, 2 * near + 1 - core]
    last = at(chips // 2)
    for p in (part, 1 - part):
        blocks += [2 * (2 * last + core) + p, 2 * (2 * last + 1 - core) + p]
    return blocks


def iota(shape, axis):
    return lax.broadcasted_iota(jnp.int32, shape, axis)


def dot_t(a, b):
    return lax.dot_general(a, b, (((1,), (1,)), ((), ())), preferred_element_type=jnp.float32)


def dot_n(a, b, precision=None):
    return lax.dot_general(
        a, b, (((1,), (0,)), ((), ())), precision=precision, preferred_element_type=jnp.float32
    )


def dot_0(a, b):
    return lax.dot_general(a, b, (((0,), (0,)), ((), ())), preferred_element_type=jnp.float32)


def lane_cat(parts):
    return jnp.concatenate(parts, axis=-1)


def mask_kernel(live, cot, out):
    first = lax.axis_index("fsdp") * (cot.shape[0] // BLOCK)
    row = iota((BLOCK, cot.shape[1]), 0)
    for k in range(cot.shape[0] // BLOCK):
        rows = slice(k * BLOCK, (k + 1) * BLOCK)
        value = cot[rows, :].astype(jnp.float32)
        out[rows, :] = jnp.where(row < live[first + k], value, 0.0).astype(out.dtype)


def mask_rows(block_live_rows, cotangent):
    return pl.pallas_call(
        mask_kernel,
        in_specs=[IN_SMEM, IN_VMEM],
        out_specs=IN_VMEM,
        out_shape=jax.ShapeDtypeStruct(cotangent.shape, cotangent.dtype),
        compiler_params=PARAMS,
        cost_estimate=SMALL,
        name="mask_rows",
    )(in_hbm(block_live_rows), in_hbm(cotangent))


def rank_major_order():
    shape = (8 * LANES, 8 * LANES)
    a, b = iota(shape, 0), iota(shape, 1)
    return ((a % LANES) * 8 + a // LANES == b).astype(jnp.bfloat16)


def gather_kernel(
    adapter, storage, down, up, result, dbuf, ubuf, dscr, uscr, cols, payload, dsem, usem, rsem
):
    blocks = adapter.shape[0]
    devices = result.shape[0]
    group = dbuf.shape[1]
    per_down, per_up = down.shape[1] // LANES, up.shape[1] // LANES
    down_rows = 2 * per_down

    def copies(b):
        slot = storage[adapter[b]]
        start = pl.multiple_of((slot // group) * group, group)
        return (
            slot % group,
            start,
            pltpu.make_async_copy(down.at[pl.ds(start, group), :], dbuf.at[b], dsem.at[b]),
        )

    def begin(b, carry):
        copies(b)[2].start()
        return carry

    ups = pltpu.make_async_copy(up, ubuf, usem)
    ups.start()
    lax.fori_loop(0, blocks, begin, 0)
    order = rank_major_order()

    def one(j, carry):
        wide, narrow = [], []
        for k in range(2):
            b = 2 * j + k
            row, start, copy = copies(b)
            copy.wait()
            late = row >= 8
            line = row % 8
            value = dbuf[b].astype(jnp.float32)
            value = jnp.where(late, value[8:], value[:8])
            for t in range(per_down):
                dscr[k, 8 * t : 8 * t + 8, :] = value[:, t * LANES : (t + 1) * LANES]
            wide.append(dscr[k, pl.ds(line, per_down, stride=8), :])
            value = ubuf[pl.ds(start, group), :].astype(jnp.float32)
            value = jnp.where(late, value[8:], value[:8])
            for t in range(per_up):
                uscr[k, 8 * t : 8 * t + 8, :] = value[:, t * LANES : (t + 1) * LANES]
            narrow.append(uscr[k, pl.ds(line, per_up, stride=8), :])
        turned = jnp.concatenate(wide, axis=0).T
        start = pl.multiple_of(j * ADAPTER_RANK, ADAPTER_RANK)
        for lo in range(8):
            piece = turned[lo * ADAPTER_RANK : (lo + 1) * ADAPTER_RANK, :]
            cols[pl.ds(start, ADAPTER_RANK), lo * LANES : (lo + 1) * LANES] = piece.astype(cols.dtype)
        payload[j, down_rows:, :] = jnp.concatenate(narrow, axis=0).astype(payload.dtype)
        return carry

    ups.wait()
    stores = []
    parts = 2
    count = devices // parts
    for h in range(parts):
        lax.fori_loop(h * count, h * count + count, one, 0)
        rows = slice(h * count * ADAPTER_RANK, (h + 1) * count * ADAPTER_RANK)
        value = dot_n(cols[rows, :], order).astype(payload.dtype)
        value = value.reshape(count, ADAPTER_RANK, 8 * LANES)
        here = slice(h * count, h * count + count)
        for q in range(8):
            payload[here, q * ADAPTER_RANK : (q + 1) * ADAPTER_RANK, :] = value[
                :, :, q * LANES : (q + 1) * LANES
            ]
        part = pl.ds(h * count, count)
        stores.append(pltpu.make_async_copy(payload.at[part], result.at[part], rsem.at[h]))
        stores[-1].start()
    for copy in stores:
        copy.wait()


def gather_rows(padded_block_adapter, adapter_storage_row, down, up, devices):
    blocks = padded_block_adapter.shape[0]
    per_down, per_up = down.shape[1] // LANES, up.shape[1] // LANES
    group = 16
    rows = 2 * (per_down + per_up)
    shape = (devices, rows, LANES)
    return pl.pallas_call(
        gather_kernel,
        in_specs=[IN_SMEM, IN_SMEM, IN_HBM, IN_HBM],
        out_specs=IN_HBM,
        out_shape=jax.ShapeDtypeStruct(shape, jnp.bfloat16),
        scratch_shapes=[
            pltpu.VMEM((blocks, group, down.shape[1]), down.dtype),
            pltpu.VMEM(up.shape, up.dtype),
            pltpu.VMEM((2, 8 * per_down + 8, LANES), jnp.float32),
            pltpu.VMEM((2, 8 * per_up + 8, LANES), jnp.float32),
            pltpu.VMEM((devices * ADAPTER_RANK, 8 * LANES), jnp.bfloat16),
            pltpu.VMEM(shape, jnp.bfloat16),
            pltpu.SemaphoreType.DMA((blocks,)),
            pltpu.SemaphoreType.DMA,
            pltpu.SemaphoreType.DMA((2,)),
        ],
        compiler_params=WIDE_PARAMS,
        cost_estimate=SMALL,
        name="gather_rows",
    )(in_hbm(padded_block_adapter), in_hbm(adapter_storage_row), in_hbm(down), in_hbm(up))


def adapter_kernel(x, cot, recv, result, g_out, xbuf, sent, xsem, rsem):
    devices = recv.shape[0]
    blocks = x.shape[0] // BLOCK
    steps = xbuf.shape[0]
    span = xbuf.shape[2]
    tiles = cot.shape[1] // LANES
    up_chunk = tiles * ADAPTER_RANK // devices
    down_rows = recv.shape[1] - blocks * up_chunk
    per = down_rows // blocks // ADAPTER_RANK
    here = span // LANES // per

    loads = [
        pltpu.make_async_copy(x.at[:, i * span : (i + 1) * span], xbuf.at[i], xsem.at[i])
        for i in range(steps)
    ]
    for copy in loads:
        copy.start()
    lane = iota((BLOCK, LANES), 1)
    gather_rank = (iota((LANES, LANES), 0) // 8 == iota((LANES, LANES), 1)).astype(jnp.float32)
    b_all = recv[:, down_rows:, :].astype(jnp.float32)
    turned = []
    for k in range(blocks):
        m = cot[k * BLOCK : (k + 1) * BLOCK, :]
        b_flat = b_all[:, k * up_chunk : (k + 1) * up_chunk, :].reshape(LANES, LANES)
        b_flat = b_flat.astype(jnp.bfloat16)
        total = jnp.zeros((BLOCK, LANES), jnp.float32)
        for t in range(tiles):
            part = dot_t(m[:, t * LANES : (t + 1) * LANES], b_flat)
            total = total + jnp.where(lane % tiles == t, part, 0.0)
        g = dot_n(total, gather_rank, lax.Precision.HIGHEST).astype(jnp.bfloat16)
        g = (adapter_scale * g.astype(jnp.float32)).astype(jnp.bfloat16)
        g_out[k * BLOCK : (k + 1) * BLOCK, :] = g
        turned.append(g.astype(jnp.float32).T[:ADAPTER_RANK, :].astype(jnp.bfloat16))

    stores = []
    lows = [jnp.zeros((BLOCK, ADAPTER_RANK), jnp.float32) for _ in range(blocks)]
    for i in range(steps):
        loads[i].wait()
        for k in range(blocks):
            part = xbuf[i, k * BLOCK : (k + 1) * BLOCK, :]
            first = k * per * ADAPTER_RANK
            spots = [
                (i * here + j, first + q * ADAPTER_RANK) for j in range(here) for q in range(per)
            ]
            a = lane_cat([recv[j, at : at + ADAPTER_RANK, :] for j, at in spots])
            lows[k] = lows[k] + dot_t(part, a)
            grad = dot_n(turned[k], part).astype(sent.dtype)
            for tile, (j, at) in enumerate(spots):
                sent[j, at : at + ADAPTER_RANK, :] = grad[:, tile * LANES : (tile + 1) * LANES]
        part = (pl.ds(i * here, here), pl.ds(0, down_rows), slice(None))
        stores.append(pltpu.make_async_copy(sent.at[part], result.at[part], rsem.at[i]))
        stores[-1].start()

    ups = []
    row = iota((LANES, LANES), 0)
    spread = (iota((ADAPTER_RANK, LANES), 1) // 8 == iota((ADAPTER_RANK, LANES), 0)).astype(
        jnp.bfloat16
    )
    for k in range(blocks):
        low8 = dot_n(lows[k].astype(jnp.bfloat16), spread).astype(jnp.bfloat16)
        up = dot_0(low8, cot[k * BLOCK : (k + 1) * BLOCK, :])
        flat = jnp.zeros((LANES, LANES), jnp.float32)
        for t in range(tiles):
            flat = flat + jnp.where(row % tiles == t, up[:, t * LANES : (t + 1) * LANES], 0.0)
        ups.append((adapter_scale * flat).reshape(devices, up_chunk, LANES))
    sent[:, down_rows:, :] = jnp.concatenate(ups, axis=1).astype(sent.dtype)
    part = (slice(None), pl.ds(down_rows, sent.shape[1] - down_rows), slice(None))
    stores.append(pltpu.make_async_copy(sent.at[part], result.at[part], rsem.at[steps]))
    stores[-1].start()
    for copy in stores:
        copy.wait()


def adapter_terms(x, cot, recv):
    rows, width = x.shape
    steps = 8
    return pl.pallas_call(
        adapter_kernel,
        in_specs=[IN_HBM, IN_VMEM, IN_VMEM],
        out_specs=[IN_HBM, IN_VMEM],
        out_shape=[
            pltpu.HBM(recv.shape, jnp.bfloat16),
            jax.ShapeDtypeStruct((rows, LANES), jnp.bfloat16),
        ],
        scratch_shapes=[
            pltpu.VMEM((steps, rows, width // steps), x.dtype),
            pltpu.VMEM(recv.shape, jnp.bfloat16),
            pltpu.SemaphoreType.DMA((steps,)),
            pltpu.SemaphoreType.DMA((steps + 1,)),
        ],
        compiler_params=PARAMS,
        cost_estimate=SMALL,
        name="adapter_terms",
    )(in_hbm(x), cot, recv)


def zero_kernel(_, down, up, zeros, dsem, usem):
    zeros[...] = jnp.zeros_like(zeros)
    copies = []
    for i in range(down.shape[0] // ZERO_ROWS):
        rows = pl.ds(i * ZERO_ROWS, ZERO_ROWS)
        part = zeros.at[:, : up.shape[1]]
        copies.append(pltpu.make_async_copy(zeros, down.at[rows, :], dsem.at[i]))
        copies.append(pltpu.make_async_copy(part, up.at[rows, :], usem.at[i]))
    for copy in copies:
        copy.start()
    for copy in copies:
        copy.wait()


def zero_grads(earlier, down_shape, up_shape):
    count = down_shape[0] // ZERO_ROWS
    return pl.pallas_call(
        zero_kernel,
        in_specs=[pl.BlockSpec(memory_space=pl.ANY)],
        out_specs=[IN_HBM, IN_HBM],
        out_shape=[
            jax.ShapeDtypeStruct(down_shape, jnp.float32),
            jax.ShapeDtypeStruct(up_shape, jnp.float32),
        ],
        scratch_shapes=[
            pltpu.VMEM((ZERO_ROWS, down_shape[1]), jnp.float32),
            pltpu.SemaphoreType.DMA((count,)),
            pltpu.SemaphoreType.DMA((count,)),
        ],
        compiler_params=PARAMS,
        cost_estimate=SMALL,
        name="zero_grads",
    )(in_hbm(earlier))


def scatter_kernel(
    adapter_hbm, storage_hbm, recv, _down, _up, down, up, adapter, storage, isem, table, dacc, uacc, dscr, uscr, drow, urow, dsem, usem
):
    blocks = adapter_hbm.shape[0]
    devices = recv.shape[0]
    per_down, per_up = down.shape[1] // LANES, up.shape[1] // LANES
    down_rows = 2 * per_down

    indices = [
        pltpu.make_async_copy(adapter_hbm, adapter, isem.at[0]),
        pltpu.make_async_copy(storage_hbm, storage, isem.at[1]),
    ]
    for copy in indices:
        copy.start()
    dacc[...] = jnp.zeros_like(dacc)
    uacc[...] = jnp.zeros_like(uacc)
    count = 8 * per_down
    a, b = iota((count, count), 0), iota((count, count), 1)
    order = ((b % per_down) * 8 + b // per_down == a).astype(jnp.bfloat16)
    values = []
    for k in range(2):
        tiles = [
            recv[:, q * ADAPTER_RANK : (q + 1) * ADAPTER_RANK, :] for q in range(4 * k, 4 * k + 4)
        ]
        values.append(dot_n(lane_cat(tiles).reshape(devices * ADAPTER_RANK, count), order))
    for copy in indices:
        copy.wait()

    def mark(i, carry):
        b = blocks - 1 - i
        table[storage[adapter[b]]] = b
        return carry

    lax.fori_loop(0, blocks, mark, 0)
    lower = iota((ADAPTER_RANK, LANES), 1) < per_down
    for j in range(devices):
        rows = []
        for t in range(4):
            first, second = [
                value[j * ADAPTER_RANK : (j + 1) * ADAPTER_RANK, t * LANES : (t + 1) * LANES]
                for value in values
            ]
            rows.append(jnp.where(lower, first, pltpu.roll(second, per_down, 1)))
            rows.append(jnp.where(lower, pltpu.roll(first, per_down, 1), second))
        turned = jnp.concatenate(rows, axis=0).T
        narrow = recv[j, down_rows:, :].astype(jnp.float32)
        for k in range(2):
            first = table[storage[adapter[2 * j + k]]]
            dacc[first] += turned[k * per_down : (k + 1) * per_down, :]
            uacc[first] += narrow[k * per_up : (k + 1) * per_up, :]
    def copies(b):
        slot = storage[adapter[b]]
        return (
            table[slot] == b,
            pltpu.make_async_copy(drow.at[pl.ds(b, 1), :], down.at[pl.ds(slot, 1), :], dsem.at[b]),
            pltpu.make_async_copy(urow.at[pl.ds(b, 1), :], up.at[pl.ds(slot, 1), :], usem.at[b]),
        )

    def begin(b, carry):
        mine, first, second = copies(b)

        @pl.when(mine)
        def _():
            first.start()
            second.start()

        return carry

    def end(b, carry):
        mine, first, second = copies(b)

        @pl.when(mine)
        def _():
            first.wait()
            second.wait()

        return carry

    for g in range(blocks // 8):
        for i in range(8):
            dscr[pl.ds(i, per_down, stride=8), :] = dacc[8 * g + i]
            uscr[pl.ds(i, per_up, stride=8), :] = uacc[8 * g + i]
        for t in range(per_down):
            drow[8 * g : 8 * g + 8, t * LANES : (t + 1) * LANES] = dscr[8 * t : 8 * t + 8, :]
        for t in range(per_up):
            urow[8 * g : 8 * g + 8, t * LANES : (t + 1) * LANES] = uscr[8 * t : 8 * t + 8, :]
        lax.fori_loop(8 * g, 8 * g + 8, begin, 0)
    lax.fori_loop(0, blocks, end, 0)


def scatter_rows(padded_block_adapter, adapter_storage_row, recv, down, up):
    blocks = padded_block_adapter.shape[0]
    per_down, per_up = down.shape[1] // LANES, up.shape[1] // LANES
    return pl.pallas_call(
        scatter_kernel,
        in_specs=[IN_HBM, IN_HBM, IN_VMEM, IN_HBM, IN_HBM],
        out_specs=[IN_HBM, IN_HBM],
        scratch_shapes=[
            pltpu.SMEM((blocks,), jnp.int32),
            pltpu.SMEM(adapter_storage_row.shape, jnp.int32),
            pltpu.SemaphoreType.DMA((2,)),
            pltpu.SMEM((ADAPTER_GROUP,), jnp.int32),
            pltpu.VMEM((blocks, per_down, LANES), jnp.float32),
            pltpu.VMEM((blocks, per_up, LANES), jnp.float32),
            pltpu.VMEM((8 * per_down + 8, LANES), jnp.float32),
            pltpu.VMEM((8 * per_up + 8, LANES), jnp.float32),
            pltpu.VMEM((blocks, per_down * LANES), jnp.float32),
            pltpu.VMEM((blocks, per_up * LANES), jnp.float32),
            pltpu.SemaphoreType.DMA((blocks,)),
            pltpu.SemaphoreType.DMA((blocks,)),
        ],
        out_shape=[
            jax.ShapeDtypeStruct(down.shape, down.dtype),
            jax.ShapeDtypeStruct(up.shape, up.dtype),
        ],
        input_output_aliases={3: 0, 4: 1},
        compiler_params=PARAMS,
        cost_estimate=SMALL,
        name="scatter_rows",
    )(in_hbm(padded_block_adapter), in_hbm(adapter_storage_row), recv, down, up)


def far_kernel(count, handed, *refs):
    cots, weight, outs = refs[:count], refs[count], refs[count + 1 : 2 * count + 1]
    wbuf, wsem, sems, hsem, *buffers = refs[2 * count + 1 + handed :]
    tile = wbuf.shape[1]
    loads = [
        pltpu.make_async_copy(weight.at[i * tile : (i + 1) * tile, :], wbuf.at[i], wsem.at[i])
        for i in range(wbuf.shape[0])
    ]
    for copy in loads:
        copy.start()
    stores = [pltpu.make_async_copy(buffers[n], outs[n], sems.at[n]) for n in range(count)]
    for i, load in enumerate(loads):
        load.wait()
        for n, cot in enumerate(cots):
            value = dot_t(cot[...], wbuf[i]).astype(buffers[n].dtype)
            buffers[n][:, i * tile : (i + 1) * tile] = value
            if i == len(loads) - 1:
                stores[n].start()
    if handed:
        copy = pltpu.make_async_copy(wbuf.at[lax.axis_index("parts")], refs[2 * count + 1], hsem)
        copy.start()
        copy.wait()
    for copy in stores:
        copy.wait()


def far_products(cots, weight, pin=in_hbm, handed=False, owned=False):
    count, rows, tile = len(cots), cots[0].shape[0], 256
    span, depth = weight.shape
    types = [jnp.bfloat16] * count
    if owned:
        types[-1] = jnp.float32
    half = [pltpu.HBM((tile, depth), weight.dtype)] if handed else []
    return pl.pallas_call(
        functools.partial(far_kernel, count, len(half)),
        in_specs=[IN_VMEM] * count + [pl.BlockSpec(memory_space=pl.ANY)],
        out_specs=[IN_HBM] * (count + len(half)),
        out_shape=[pltpu.HBM((rows, span), kind) for kind in types] + half,
        scratch_shapes=[
            pltpu.VMEM((span // tile, tile, depth), weight.dtype),
            pltpu.SemaphoreType.DMA((span // tile,)),
            pltpu.SemaphoreType.DMA((count,)),
            pltpu.SemaphoreType.DMA,
        ]
        + [pltpu.VMEM((rows, span), kind) for kind in types],
        compiler_params=PARAMS,
        cost_estimate=SMALL,
        name="far_products",
    )(*cots, pin(weight))


def finish(devices, at, cot, weights, received, g, recv, out, width, columns, pin=in_hbm, cost=SMALL):
    rows = cot.shape[0]
    spans = [w.shape[0] for w in weights] + [r.shape[1] for r in received]
    count = len(spans)
    sources = [pin(source) for source in (*weights, *received)]
    per = columns // LANES

    def kernel(cot, g, recv, *rest):
        where = column_blocks(devices)
        given = rest[:count]
        result = rest[-4 - count]
        buffer, sems, loaded = rest[-3 - count], rest[-2 - count], rest[-1 - count : -1]
        load_sems = rest[-1]
        loads = [
            pltpu.make_async_copy(given[i], loaded[i], load_sems.at[i]) for i in range(count)
        ]
        for load in loads:
            load.start()
        copies = []
        for i in range(count):
            index, span = where[at[i]], spans[i]
            per_device = columns // span
            device, inner = index // per_device, (index % per_device) * (span // LANES)
            parts = []
            for k in range(rows // BLOCK):
                tiles = []
                for q in range(span // LANES):
                    first = pl.multiple_of((k * per + inner + q) * ADAPTER_RANK, ADAPTER_RANK)
                    tiles.append(recv[device, pl.ds(first, ADAPTER_RANK), :])
                ours = g[k * BLOCK : (k + 1) * BLOCK, :ADAPTER_RANK]
                parts.append(dot_n(ours, lane_cat(tiles)))
            value = jnp.concatenate(parts, axis=0)
            loads[i].wait()
            if i < len(weights):
                value = value + dot_t(cot[...], loaded[i][...])
            else:
                value = value + loaded[i][...].astype(jnp.float32)
            buffer[i, :, :span] = value.astype(buffer.dtype)
            start = pl.multiple_of(index * span, span)
            copies.append(
                pltpu.make_async_copy(
                    buffer.at[i, :, :span], result.at[:, pl.ds(start, span)], sems.at[i]
                )
            )
            copies[-1].start()
        for copy in copies:
            copy.wait()

    return pl.pallas_call(
        kernel,
        in_specs=[IN_VMEM] * 3
        + [pl.BlockSpec(memory_space=pl.ANY)] * count
        + ([] if out is None else [IN_HBM]),
        out_specs=IN_HBM,
        out_shape=jax.ShapeDtypeStruct((rows, width), jnp.bfloat16),
        input_output_aliases={} if out is None else {3 + count: 0},
        scratch_shapes=[
            pltpu.VMEM((count, rows, max(spans)), jnp.bfloat16),
            pltpu.SemaphoreType.DMA((count,)),
        ]
        + [pltpu.VMEM(source.shape, source.dtype) for source in sources]
        + [pltpu.SemaphoreType.DMA((count,))],
        compiler_params=WIDE_PARAMS,
        cost_estimate=cost,
        name="finish",
    )(cot, g, recv, *sources, *([] if out is None else [out]))


def ring_pairs(devices):
    chips = devices // 2
    order = list(range(0, chips, 2)) + list(range(chips - 1, 0, -2))
    pairs = []
    for part in range(2):
        for i, chip in enumerate(order):
            for core in range(2):
                other = order[(i + (1 if core == part else -1)) % chips]
                pairs.append((part * devices + 2 * chip + core, part * devices + 2 * other + core))
    return pairs


def ring_body(
    inputs,
    cotangent,
    frozen_value_weight,
    adapter_down_weights,
    adapter_up_weights,
    padded_block_adapter,
    block_live_rows,
    adapter_storage_row,
    *,
    devices,
):
    steps = devices // 4
    shard = frozen_value_weight.shape[0]
    width = inputs.shape[1]
    ring = ring_pairs(devices)
    cores = [(i, i ^ 1) for i in range(devices)]
    across = [(0, 1), (1, 0)]
    diagonal = [(p * devices + i, (1 - p) * devices + (i ^ 1)) for p in range(2) for i in range(devices)]

    def cross(products):
        return (
            lax.ppermute(products[0], "fsdp", cores),
            lax.ppermute(products[1], "parts", across),
            lax.ppermute(products[2], ("parts", "fsdp"), diagonal),
        )

    other_shard = lax.ppermute(frozen_value_weight, "fsdp", cores)
    masked = mask_rows(block_live_rows, cotangent)
    core_masked = lax.ppermute(masked, "fsdp", cores)
    far_masked = lax.ppermute(masked, "parts", across)
    adapter, _ = after(padded_block_adapter, masked)
    payload = gather_rows(
        adapter, adapter_storage_row, adapter_down_weights, adapter_up_weights, devices
    )
    recv = lax.all_to_all(payload, "fsdp", split_axis=0, concat_axis=0, tiled=True)

    travelling = lax.ppermute(frozen_value_weight, ("parts", "fsdp"), ring)

    firsts = [2 + 4 * step for step in range(steps)]
    pieces, received = [], []
    for step in range(steps):
        if step == 0:
            travelling, far_masked, _ = after(travelling, far_masked, payload)
            diagonal_masked = lax.ppermute(far_masked, "fsdp", cores)
            cots = (core_masked, far_masked, diagonal_masked)
        elif step == 1:
            travelling, sent, grads, received[0] = after(travelling, sent, grads, received[0])
        pieces.append(travelling)
        if step < steps - 2:
            travelling = lax.ppermute(travelling, ("parts", "fsdp"), ring)
        pin = as_it_is if step >= steps - 2 else in_hbm
        owned = step >= steps - 2
        if owned:
            cots = (*cots[:3], masked)
        products = far_products(cots, pieces[step], pin, step == steps - 2, owned)
        if step == steps - 2:
            *products, own, travelling = products
            travelling, products, out, received[-1] = after(
                travelling, products, out, received[-1]
            )
            travelling = lax.ppermute(travelling, ("parts", "fsdp"), ring)
            sent, products = after(sent, products)
            sums = lax.all_to_all(sent, "fsdp", split_axis=0, concat_axis=0, tiled=True)
        if step == steps - 1:
            *products, last_own = products
        received.append(cross(products))
        if step == 0:
            grads = zero_grads(products[0], adapter_down_weights.shape, adapter_up_weights.shape)
            recv, _ = after(recv, grads)
            sent, g = adapter_terms(inputs, masked, recv)
        if step == steps - 3:
            cot, _ = after(masked, products[0])
            at = [0, 1, *firsts[: step + 1]] + [firsts[0] + i for i in range(1, 4)]
            weights = (frozen_value_weight, other_shard, *pieces[:2])
            out = finish(devices, at, cot, weights, received[0], g, recv, None, width, shard)
            travelling, out = after(travelling, out)
        if step == steps - 2:
            out, _ = after(out, products)
            at = [firsts[step]] + [first + i for first in firsts[1:step] for i in range(1, 4)]
            early = (own, *sum(received[1:step], ()))
            out = finish(devices, at, masked, (), early, g, recv, out, width, shard)
            travelling, out = after(travelling, out)
    at = firsts[-1:] + [firsts[-2] + i for i in range(1, 4)]
    late = (last_own, *received[-2])
    out = finish(devices, at, masked, (), late, g, recv, out, width, shard, in_hbm, LONGER)
    at = [firsts[-1] + i for i in range(1, 4)]
    out = finish(devices, at, masked, (), received[-1], g, recv, out, width, shard, as_it_is)
    sums, out = after(sums, out)
    down_grad, up_grad = scatter_rows(padded_block_adapter, adapter_storage_row, sums, *grads)
    return (out, down_grad, up_grad)


def after(value, *earlier):
    return lax.optimization_barrier((value,) + earlier)


def gather_body(
    inputs,
    cotangent,
    frozen_value_weight,
    adapter_down_weights,
    adapter_up_weights,
    padded_block_adapter,
    block_live_rows,
    adapter_storage_row,
):
    hidden_width = inputs.shape[1]
    kv_width = cotangent.shape[1]
    token_rows = inputs.shape[0]
    block_count = token_rows // BLOCK
    first_block = lax.axis_index("fsdp") * block_count
    live_rows = lax.dynamic_slice_in_dim(block_live_rows, first_block, block_count)
    positions = jnp.arange(BLOCK, dtype=jnp.int32)
    live_mask = positions[None, :] < live_rows[:, None]
    blocked_cot = cotangent.reshape(block_count, BLOCK, kv_width)
    masked_blocks = jnp.where(live_mask[:, :, None], blocked_cot, jnp.zeros_like(blocked_cot))
    masked = masked_blocks.reshape(token_rows, kv_width)
    block_storage_row = slot_lookup(padded_block_adapter, adapter_storage_row)
    down_weight_rows = jnp.take(adapter_down_weights, block_storage_row, axis=0)
    up_weight_rows = jnp.take(adapter_up_weights, block_storage_row, axis=0)
    down_mine, up_mine = (
        lax.all_to_all(down_weight_rows, "fsdp", split_axis=0, concat_axis=1, tiled=True),
        lax.all_to_all(up_weight_rows, "fsdp", split_axis=0, concat_axis=1, tiled=True),
    )
    frozen_gradient = lax.dot_general(
        masked,
        lax.all_gather(frozen_value_weight, "fsdp", axis=0, tiled=True),
        (((1,), (1,)), ((), ())),
        preferred_element_type=jnp.float32,
    )
    down_weight_matrix = down_mine.reshape(block_count, hidden_width, ADAPTER_RANK)
    up_weight_matrix = up_mine.reshape(block_count, ADAPTER_RANK, kv_width)
    blocked_in = inputs.reshape(block_count, BLOCK, hidden_width)
    rank_projection = jnp.einsum(
        "kbd,kdr->kbr", blocked_in, down_weight_matrix, preferred_element_type=jnp.float32
    ).astype(jnp.bfloat16)
    rank_space_gradient = jnp.einsum(
        "kbv,krv->kbr", masked_blocks, up_weight_matrix, preferred_element_type=jnp.float32
    ).astype(jnp.bfloat16)
    adapter_gradient_term = adapter_scale * jnp.einsum(
        "kbr,kdr->kbd", rank_space_gradient, down_weight_matrix, preferred_element_type=jnp.float32
    )
    input_gradient = (
        frozen_gradient + adapter_gradient_term.reshape(token_rows, hidden_width)
    ).astype(jnp.bfloat16)
    partial_down_weight = adapter_scale * jnp.einsum(
        "kbd,kbr->kdr", blocked_in, rank_space_gradient, preferred_element_type=jnp.float32
    )
    partial_up_weight = adapter_scale * jnp.einsum(
        "kbr,kbv->krv", rank_projection, masked_blocks, preferred_element_type=jnp.float32
    )
    partial_down_weight = partial_down_weight.reshape(block_count, hidden_width * ADAPTER_RANK)
    partial_up_weight = partial_up_weight.reshape(block_count, ADAPTER_RANK * kv_width)
    recv_down, recv_up = (
        lax.all_to_all(partial_down_weight, "fsdp", split_axis=1, concat_axis=0, tiled=True),
        lax.all_to_all(partial_up_weight, "fsdp", split_axis=1, concat_axis=0, tiled=True),
    )
    onehot = (
        jnp.arange(ADAPTER_GROUP, dtype=jnp.int32)[:, None] == block_storage_row[None, :]
    ).astype(jnp.float32)
    highest_precision = lax.Precision.HIGHEST
    down_grad = jnp.dot(
        onehot, recv_down, precision=highest_precision, preferred_element_type=jnp.float32
    )
    up_grad = jnp.dot(
        onehot, recv_up, precision=highest_precision, preferred_element_type=jnp.float32
    )
    return (input_gradient, down_grad, up_grad)


def solution(mesh):
    devices = mesh.shape["fsdp"]
    in_specs = (
        P(("parts", "fsdp"), None),
        P(("parts", "fsdp"), None),
        P("fsdp", None),
        P("parts", "fsdp"),
        P("parts", "fsdp"),
        P("parts"),
        P("parts"),
        P("parts"),
    )
    out_specs = (P(("parts", "fsdp"), None), P("parts", "fsdp"), P("parts", "fsdp"))

    def program(*arrays):
        shard = arrays[2].shape[0] // devices
        rows = arrays[0].shape[0] // devices // 2
        adapter_tiles = arrays[3].shape[1] // devices // LANES
        fits = rows == 2 * BLOCK and 2 * adapter_tiles == LANES and shard % 512 == 0
        if mesh.shape["parts"] == 2 and devices % 4 == 0 and fits:
            body = functools.partial(ring_body, devices=devices)
        else:
            body = gather_body
        return jax.shard_map(
            body, mesh=mesh, in_specs=in_specs, out_specs=out_specs, check_vma=False
        )(*arrays)

    return program
```

```python
import functools

import jax
import jax.numpy as jnp
from jax import lax
from jax.experimental import pallas as pl
from jax.experimental.pallas import tpu as pltpu
from jax.sharding import PartitionSpec as P

ADAPTER_RANK = 16
ADAPTER_GROUP = 512
BLOCK = 128
LANES = 128
MIB = 1024 * 1024
ZERO_ROWS = 64
PARAMS = pltpu.CompilerParams(vmem_limit_bytes=16 * MIB)
WIDE_PARAMS = pltpu.CompilerParams(vmem_limit_bytes=24 * MIB)
IN_VMEM = pl.BlockSpec(memory_space=pltpu.VMEM)
IN_SMEM = pl.BlockSpec(memory_space=pltpu.SMEM)
IN_HBM = pl.BlockSpec(memory_space=pltpu.HBM)
SMALL = pl.CostEstimate(flops=1, bytes_accessed=1, transcendentals=0)
LONGER = pl.CostEstimate(flops=10_000_000_000, bytes_accessed=1, transcendentals=0)

adapter_scale = 2.0


def slot_lookup(padded_block_adapter, adapter_storage_row):
    matches = padded_block_adapter[:, None] == jnp.arange(ADAPTER_GROUP, dtype=jnp.int32)[None, :]
    return jnp.sum(jnp.where(matches, adapter_storage_row[None, :], 0), axis=1)


def in_hbm(value):
    return pltpu.with_memory_space_constraint(value, pltpu.HBM)


def as_it_is(value):
    return value


def column_blocks(devices):
    index, part = lax.axis_index("fsdp"), lax.axis_index("parts")
    chips = devices // 2
    chip, core = lax.div(index, 2), lax.rem(index, 2)
    way = jnp.where(core == part, -1, 1)
    odd = lax.rem(chip, 2) == 1
    place = jnp.where(odd, chips - lax.div(chip + 1, 2), lax.div(chip, 2))

    def at(steps):
        position = lax.rem(place + steps + chips, chips)
        return jnp.where(position < chips // 2, 2 * position, 2 * (chips - position) - 1)

    blocks = [index, index + 1 - 2 * core]
    for step in range(1, chips // 2):
        near, far = at(way * step), at(-way * step)
        blocks += [2 * near + core, 2 * far + 1 - core, 2 * far + core, 2 * near + 1 - core]
    last = at(chips // 2)
    for p in (part, 1 - part):
        blocks += [2 * (2 * last + core) + p, 2 * (2 * last + 1 - core) + p]
    return blocks


def iota(shape, axis):
    return lax.broadcasted_iota(jnp.int32, shape, axis)


def dot_t(a, b):
    return lax.dot_general(a, b, (((1,), (1,)), ((), ())), preferred_element_type=jnp.float32)


def dot_n(a, b, precision=None):
    return lax.dot_general(
        a, b, (((1,), (0,)), ((), ())), precision=precision, preferred_element_type=jnp.float32
    )


def dot_0(a, b):
    return lax.dot_general(a, b, (((0,), (0,)), ((), ())), preferred_element_type=jnp.float32)


def lane_cat(parts):
    return jnp.concatenate(parts, axis=-1)


def mask_kernel(live, cot, out):
    first = lax.axis_index("fsdp") * (cot.shape[0] // BLOCK)
    row = iota((BLOCK, cot.shape[1]), 0)
    for k in range(cot.shape[0] // BLOCK):
        rows = slice(k * BLOCK, (k + 1) * BLOCK)
        value = cot[rows, :].astype(jnp.float32)
        out[rows, :] = jnp.where(row < live[first + k], value, 0.0).astype(out.dtype)


def mask_rows(block_live_rows, cotangent):
    return pl.pallas_call(
        mask_kernel,
        in_specs=[IN_SMEM, IN_VMEM],
        out_specs=IN_VMEM,
        out_shape=jax.ShapeDtypeStruct(cotangent.shape, cotangent.dtype),
        compiler_params=PARAMS,
        cost_estimate=SMALL,
        name="mask_rows",
    )(in_hbm(block_live_rows), in_hbm(cotangent))


def rank_major_order():
    shape = (8 * LANES, 8 * LANES)
    a, b = iota(shape, 0), iota(shape, 1)
    return ((a % LANES) * 8 + a // LANES == b).astype(jnp.bfloat16)


def gather_kernel(
    adapter, storage, down, up, result, dbuf, ubuf, dscr, uscr, cols, payload, dsem, usem, rsem
):
    blocks = adapter.shape[0]
    devices = result.shape[0]
    group = dbuf.shape[1]
    per_down, per_up = down.shape[1] // LANES, up.shape[1] // LANES
    down_rows = 2 * per_down

    def copies(b):
        slot = storage[adapter[b]]
        start = pl.multiple_of((slot // group) * group, group)
        return (
            slot % group,
            start,
            pltpu.make_async_copy(down.at[pl.ds(start, group), :], dbuf.at[b], dsem.at[b]),
        )

    def begin(b, carry):
        copies(b)[2].start()
        return carry

    ups = pltpu.make_async_copy(up, ubuf, usem)
    ups.start()
    lax.fori_loop(0, blocks, begin, 0)
    order = rank_major_order()

    def one(j, carry):
        wide, narrow = [], []
        for k in range(2):
            b = 2 * j + k
            row, start, copy = copies(b)
            copy.wait()
            late = row >= 8
            line = row % 8
            value = dbuf[b].astype(jnp.float32)
            value = jnp.where(late, value[8:], value[:8])
            for t in range(per_down):
                dscr[k, 8 * t : 8 * t + 8, :] = value[:, t * LANES : (t + 1) * LANES]
            wide.append(dscr[k, pl.ds(line, per_down, stride=8), :])
            value = ubuf[pl.ds(start, group), :].astype(jnp.float32)
            value = jnp.where(late, value[8:], value[:8])
            for t in range(per_up):
                uscr[k, 8 * t : 8 * t + 8, :] = value[:, t * LANES : (t + 1) * LANES]
            narrow.append(uscr[k, pl.ds(line, per_up, stride=8), :])
        turned = jnp.concatenate(wide, axis=0).T
        start = pl.multiple_of(j * ADAPTER_RANK, ADAPTER_RANK)
        for lo in range(8):
            piece = turned[lo * ADAPTER_RANK : (lo + 1) * ADAPTER_RANK, :]
            cols[pl.ds(start, ADAPTER_RANK), lo * LANES : (lo + 1) * LANES] = piece.astype(cols.dtype)
        payload[j, down_rows:, :] = jnp.concatenate(narrow, axis=0).astype(payload.dtype)
        return carry

    ups.wait()
    stores = []
    parts = 2
    count = devices // parts
    for h in range(parts):
        lax.fori_loop(h * count, h * count + count, one, 0)
        rows = slice(h * count * ADAPTER_RANK, (h + 1) * count * ADAPTER_RANK)
        value = dot_n(cols[rows, :], order).astype(payload.dtype)
        value = value.reshape(count, ADAPTER_RANK, 8 * LANES)
        here = slice(h * count, h * count + count)
        for q in range(8):
            payload[here, q * ADAPTER_RANK : (q + 1) * ADAPTER_RANK, :] = value[
                :, :, q * LANES : (q + 1) * LANES
            ]
        part = pl.ds(h * count, count)
        stores.append(pltpu.make_async_copy(payload.at[part], result.at[part], rsem.at[h]))
        stores[-1].start()
    for copy in stores:
        copy.wait()


def gather_rows(padded_block_adapter, adapter_storage_row, down, up, devices):
    blocks = padded_block_adapter.shape[0]
    per_down, per_up = down.shape[1] // LANES, up.shape[1] // LANES
    group = 16
    rows = 2 * (per_down + per_up)
    shape = (devices, rows, LANES)
    return pl.pallas_call(
        gather_kernel,
        in_specs=[IN_SMEM, IN_SMEM, IN_HBM, IN_HBM],
        out_specs=IN_HBM,
        out_shape=jax.ShapeDtypeStruct(shape, jnp.bfloat16),
        scratch_shapes=[
            pltpu.VMEM((blocks, group, down.shape[1]), down.dtype),
            pltpu.VMEM(up.shape, up.dtype),
            pltpu.VMEM((2, 8 * per_down + 8, LANES), jnp.float32),
            pltpu.VMEM((2, 8 * per_up + 8, LANES), jnp.float32),
            pltpu.VMEM((devices * ADAPTER_RANK, 8 * LANES), jnp.bfloat16),
            pltpu.VMEM(shape, jnp.bfloat16),
            pltpu.SemaphoreType.DMA((blocks,)),
            pltpu.SemaphoreType.DMA,
            pltpu.SemaphoreType.DMA((2,)),
        ],
        compiler_params=WIDE_PARAMS,
        cost_estimate=SMALL,
        name="gather_rows",
    )(in_hbm(padded_block_adapter), in_hbm(adapter_storage_row), in_hbm(down), in_hbm(up))


def adapter_kernel(x, cot, recv, result, g_out, xbuf, sent, xsem, rsem):
    devices = recv.shape[0]
    blocks = x.shape[0] // BLOCK
    steps = xbuf.shape[0]
    span = xbuf.shape[2]
    tiles = cot.shape[1] // LANES
    up_chunk = tiles * ADAPTER_RANK // devices
    down_rows = recv.shape[1] - blocks * up_chunk
    per = down_rows // blocks // ADAPTER_RANK
    here = span // LANES // per

    loads = [
        pltpu.make_async_copy(x.at[:, i * span : (i + 1) * span], xbuf.at[i], xsem.at[i])
        for i in range(steps)
    ]
    for copy in loads:
        copy.start()
    lane = iota((BLOCK, LANES), 1)
    gather_rank = (iota((LANES, LANES), 0) // 8 == iota((LANES, LANES), 1)).astype(jnp.float32)
    b_all = recv[:, down_rows:, :].astype(jnp.float32)
    turned = []
    for k in range(blocks):
        m = cot[k * BLOCK : (k + 1) * BLOCK, :]
        b_flat = b_all[:, k * up_chunk : (k + 1) * up_chunk, :].reshape(LANES, LANES)
        b_flat = b_flat.astype(jnp.bfloat16)
        total = jnp.zeros((BLOCK, LANES), jnp.float32)
        for t in range(tiles):
            part = dot_t(m[:, t * LANES : (t + 1) * LANES], b_flat)
            total = total + jnp.where(lane % tiles == t, part, 0.0)
        g = dot_n(total, gather_rank, lax.Precision.HIGHEST).astype(jnp.bfloat16)
        g = (adapter_scale * g.astype(jnp.float32)).astype(jnp.bfloat16)
        g_out[k * BLOCK : (k + 1) * BLOCK, :] = g
        turned.append(g.astype(jnp.float32).T[:ADAPTER_RANK, :].astype(jnp.bfloat16))

    stores = []
    lows = [jnp.zeros((BLOCK, ADAPTER_RANK), jnp.float32) for _ in range(blocks)]
    for i in range(steps):
        loads[i].wait()
        for k in range(blocks):
            part = xbuf[i, k * BLOCK : (k + 1) * BLOCK, :]
            first = k * per * ADAPTER_RANK
            spots = [
                (i * here + j, first + q * ADAPTER_RANK) for j in range(here) for q in range(per)
            ]
            a = lane_cat([recv[j, at : at + ADAPTER_RANK, :] for j, at in spots])
            lows[k] = lows[k] + dot_t(part, a)
            grad = dot_n(turned[k], part).astype(sent.dtype)
            for tile, (j, at) in enumerate(spots):
                sent[j, at : at + ADAPTER_RANK, :] = grad[:, tile * LANES : (tile + 1) * LANES]
        part = (pl.ds(i * here, here), pl.ds(0, down_rows), slice(None))
        stores.append(pltpu.make_async_copy(sent.at[part], result.at[part], rsem.at[i]))
        stores[-1].start()

    ups = []
    row = iota((LANES, LANES), 0)
    spread = (iota((ADAPTER_RANK, LANES), 1) // 8 == iota((ADAPTER_RANK, LANES), 0)).astype(
        jnp.bfloat16
    )
    for k in range(blocks):
        low8 = dot_n(lows[k].astype(jnp.bfloat16), spread).astype(jnp.bfloat16)
        up = dot_0(low8, cot[k * BLOCK : (k + 1) * BLOCK, :])
        flat = jnp.zeros((LANES, LANES), jnp.float32)
        for t in range(tiles):
            flat = flat + jnp.where(row % tiles == t, up[:, t * LANES : (t + 1) * LANES], 0.0)
        ups.append((adapter_scale * flat).reshape(devices, up_chunk, LANES))
    sent[:, down_rows:, :] = jnp.concatenate(ups, axis=1).astype(sent.dtype)
    part = (slice(None), pl.ds(down_rows, sent.shape[1] - down_rows), slice(None))
    stores.append(pltpu.make_async_copy(sent.at[part], result.at[part], rsem.at[steps]))
    stores[-1].start()
    for copy in stores:
        copy.wait()


def adapter_terms(x, cot, recv):
    rows, width = x.shape
    steps = 8
    return pl.pallas_call(
        adapter_kernel,
        in_specs=[IN_HBM, IN_VMEM, IN_VMEM],
        out_specs=[IN_HBM, IN_VMEM],
        out_shape=[
            pltpu.HBM(recv.shape, jnp.bfloat16),
            jax.ShapeDtypeStruct((rows, LANES), jnp.bfloat16),
        ],
        scratch_shapes=[
            pltpu.VMEM((steps, rows, width // steps), x.dtype),
            pltpu.VMEM(recv.shape, jnp.bfloat16),
            pltpu.SemaphoreType.DMA((steps,)),
            pltpu.SemaphoreType.DMA((steps + 1,)),
        ],
        compiler_params=PARAMS,
        cost_estimate=SMALL,
        name="adapter_terms",
    )(in_hbm(x), cot, recv)


def zero_kernel(_, down, up, zeros, dsem, usem):
    zeros[...] = jnp.zeros_like(zeros)
    copies = []
    for i in range(down.shape[0] // ZERO_ROWS):
        rows = pl.ds(i * ZERO_ROWS, ZERO_ROWS)
        part = zeros.at[:, : up.shape[1]]
        copies.append(pltpu.make_async_copy(zeros, down.at[rows, :], dsem.at[i]))
        copies.append(pltpu.make_async_copy(part, up.at[rows, :], usem.at[i]))
    for copy in copies:
        copy.start()
    for copy in copies:
        copy.wait()


def zero_grads(earlier, down_shape, up_shape):
    count = down_shape[0] // ZERO_ROWS
    return pl.pallas_call(
        zero_kernel,
        in_specs=[pl.BlockSpec(memory_space=pl.ANY)],
        out_specs=[IN_HBM, IN_HBM],
        out_shape=[
            jax.ShapeDtypeStruct(down_shape, jnp.float32),
            jax.ShapeDtypeStruct(up_shape, jnp.float32),
        ],
        scratch_shapes=[
            pltpu.VMEM((ZERO_ROWS, down_shape[1]), jnp.float32),
            pltpu.SemaphoreType.DMA((count,)),
            pltpu.SemaphoreType.DMA((count,)),
        ],
        compiler_params=PARAMS,
        cost_estimate=SMALL,
        name="zero_grads",
    )(in_hbm(earlier))


def scatter_kernel(
    adapter_hbm, storage_hbm, recv, _down, _up, down, up, adapter, storage, isem, table, dacc, uacc, dscr, uscr, drow, urow, dsem, usem
):
    blocks = adapter_hbm.shape[0]
    devices = recv.shape[0]
    per_down, per_up = down.shape[1] // LANES, up.shape[1] // LANES
    down_rows = 2 * per_down

    indices = [
        pltpu.make_async_copy(adapter_hbm, adapter, isem.at[0]),
        pltpu.make_async_copy(storage_hbm, storage, isem.at[1]),
    ]
    for copy in indices:
        copy.start()
    dacc[...] = jnp.zeros_like(dacc)
    uacc[...] = jnp.zeros_like(uacc)
    count = 8 * per_down
    a, b = iota((count, count), 0), iota((count, count), 1)
    order = ((b % per_down) * 8 + b // per_down == a).astype(jnp.bfloat16)
    values = []
    for k in range(2):
        tiles = [
            recv[:, q * ADAPTER_RANK : (q + 1) * ADAPTER_RANK, :] for q in range(4 * k, 4 * k + 4)
        ]
        values.append(dot_n(lane_cat(tiles).reshape(devices * ADAPTER_RANK, count), order))
    for copy in indices:
        copy.wait()

    def mark(i, carry):
        b = blocks - 1 - i
        table[storage[adapter[b]]] = b
        return carry

    lax.fori_loop(0, blocks, mark, 0)
    lower = iota((ADAPTER_RANK, LANES), 1) < per_down
    for j in range(devices):
        rows = []
        for t in range(4):
            first, second = [
                value[j * ADAPTER_RANK : (j + 1) * ADAPTER_RANK, t * LANES : (t + 1) * LANES]
                for value in values
            ]
            rows.append(jnp.where(lower, first, pltpu.roll(second, per_down, 1)))
            rows.append(jnp.where(lower, pltpu.roll(first, per_down, 1), second))
        turned = jnp.concatenate(rows, axis=0).T
        narrow = recv[j, down_rows:, :].astype(jnp.float32)
        for k in range(2):
            first = table[storage[adapter[2 * j + k]]]
            dacc[first] += turned[k * per_down : (k + 1) * per_down, :]
            uacc[first] += narrow[k * per_up : (k + 1) * per_up, :]
    def copies(b):
        slot = storage[adapter[b]]
        return (
            table[slot] == b,
            pltpu.make_async_copy(drow.at[pl.ds(b, 1), :], down.at[pl.ds(slot, 1), :], dsem.at[b]),
            pltpu.make_async_copy(urow.at[pl.ds(b, 1), :], up.at[pl.ds(slot, 1), :], usem.at[b]),
        )

    def begin(b, carry):
        mine, first, second = copies(b)

        @pl.when(mine)
        def _():
            first.start()
            second.start()

        return carry

    def end(b, carry):
        mine, first, second = copies(b)

        @pl.when(mine)
        def _():
            first.wait()
            second.wait()

        return carry

    for g in range(blocks // 8):
        for i in range(8):
            dscr[pl.ds(i, per_down, stride=8), :] = dacc[8 * g + i]
            uscr[pl.ds(i, per_up, stride=8), :] = uacc[8 * g + i]
        for t in range(per_down):
            drow[8 * g : 8 * g + 8, t * LANES : (t + 1) * LANES] = dscr[8 * t : 8 * t + 8, :]
        for t in range(per_up):
            urow[8 * g : 8 * g + 8, t * LANES : (t + 1) * LANES] = uscr[8 * t : 8 * t + 8, :]
        lax.fori_loop(8 * g, 8 * g + 8, begin, 0)
    lax.fori_loop(0, blocks, end, 0)


def scatter_rows(padded_block_adapter, adapter_storage_row, recv, down, up):
    blocks = padded_block_adapter.shape[0]
    per_down, per_up = down.shape[1] // LANES, up.shape[1] // LANES
    return pl.pallas_call(
        scatter_kernel,
        in_specs=[IN_HBM, IN_HBM, IN_VMEM, IN_HBM, IN_HBM],
        out_specs=[IN_HBM, IN_HBM],
        scratch_shapes=[
            pltpu.SMEM((blocks,), jnp.int32),
            pltpu.SMEM(adapter_storage_row.shape, jnp.int32),
            pltpu.SemaphoreType.DMA((2,)),
            pltpu.SMEM((ADAPTER_GROUP,), jnp.int32),
            pltpu.VMEM((blocks, per_down, LANES), jnp.float32),
            pltpu.VMEM((blocks, per_up, LANES), jnp.float32),
            pltpu.VMEM((8 * per_down + 8, LANES), jnp.float32),
            pltpu.VMEM((8 * per_up + 8, LANES), jnp.float32),
            pltpu.VMEM((blocks, per_down * LANES), jnp.float32),
            pltpu.VMEM((blocks, per_up * LANES), jnp.float32),
            pltpu.SemaphoreType.DMA((blocks,)),
            pltpu.SemaphoreType.DMA((blocks,)),
        ],
        out_shape=[
            jax.ShapeDtypeStruct(down.shape, down.dtype),
            jax.ShapeDtypeStruct(up.shape, up.dtype),
        ],
        input_output_aliases={3: 0, 4: 1},
        compiler_params=PARAMS,
        cost_estimate=SMALL,
        name="scatter_rows",
    )(in_hbm(padded_block_adapter), in_hbm(adapter_storage_row), recv, down, up)


def far_kernel(count, handed, *refs):
    cots, weight, outs = refs[:count], refs[count], refs[count + 1 : 2 * count + 1]
    wbuf, wsem, sems, hsem, *buffers = refs[2 * count + 1 + handed :]
    tile = wbuf.shape[1]
    loads = [
        pltpu.make_async_copy(weight.at[i * tile : (i + 1) * tile, :], wbuf.at[i], wsem.at[i])
        for i in range(wbuf.shape[0])
    ]
    for copy in loads:
        copy.start()
    stores = [pltpu.make_async_copy(buffers[n], outs[n], sems.at[n]) for n in range(count)]
    for i, load in enumerate(loads):
        load.wait()
        for n, cot in enumerate(cots):
            value = dot_t(cot[...], wbuf[i]).astype(buffers[n].dtype)
            buffers[n][:, i * tile : (i + 1) * tile] = value
            if i == len(loads) - 1:
                stores[n].start()
    if handed:
        copy = pltpu.make_async_copy(wbuf.at[lax.axis_index("parts")], refs[2 * count + 1], hsem)
        copy.start()
        copy.wait()
    for copy in stores:
        copy.wait()


def far_products(cots, weight, pin=in_hbm, handed=False, owned=False):
    count, rows, tile = len(cots), cots[0].shape[0], 256
    span, depth = weight.shape
    types = [jnp.bfloat16] * count
    if owned:
        types[-1] = jnp.float32
    half = [pltpu.HBM((tile, depth), weight.dtype)] if handed else []
    return pl.pallas_call(
        functools.partial(far_kernel, count, len(half)),
        in_specs=[IN_VMEM] * count + [pl.BlockSpec(memory_space=pl.ANY)],
        out_specs=[IN_HBM] * (count + len(half)),
        out_shape=[pltpu.HBM((rows, span), kind) for kind in types] + half,
        scratch_shapes=[
            pltpu.VMEM((span // tile, tile, depth), weight.dtype),
            pltpu.SemaphoreType.DMA((span // tile,)),
            pltpu.SemaphoreType.DMA((count,)),
            pltpu.SemaphoreType.DMA,
        ]
        + [pltpu.VMEM((rows, span), kind) for kind in types],
        compiler_params=PARAMS,
        cost_estimate=SMALL,
        name="far_products",
    )(*cots, pin(weight))


def finish(devices, at, cot, weights, received, g, recv, out, width, columns, pin=in_hbm, cost=SMALL):
    rows = cot.shape[0]
    spans = [w.shape[0] for w in weights] + [r.shape[1] for r in received]
    count = len(spans)
    sources = [pin(source) for source in (*weights, *received)]
    per = columns // LANES

    def kernel(cot, g, recv, *rest):
        where = column_blocks(devices)
        given = rest[:count]
        result = rest[-4 - count]
        buffer, sems, loaded = rest[-3 - count], rest[-2 - count], rest[-1 - count : -1]
        load_sems = rest[-1]
        loads = [
            pltpu.make_async_copy(given[i], loaded[i], load_sems.at[i]) for i in range(count)
        ]
        for load in loads:
            load.start()
        copies = []
        for i in range(count):
            index, span = where[at[i]], spans[i]
            per_device = columns // span
            device, inner = index // per_device, (index % per_device) * (span // LANES)
            parts = []
            for k in range(rows // BLOCK):
                tiles = []
                for q in range(span // LANES):
                    first = pl.multiple_of((k * per + inner + q) * ADAPTER_RANK, ADAPTER_RANK)
                    tiles.append(recv[device, pl.ds(first, ADAPTER_RANK), :])
                ours = g[k * BLOCK : (k + 1) * BLOCK, :ADAPTER_RANK]
                parts.append(dot_n(ours, lane_cat(tiles)))
            value = jnp.concatenate(parts, axis=0)
            loads[i].wait()
            if i < len(weights):
                value = value + dot_t(cot[...], loaded[i][...])
            else:
                value = value + loaded[i][...].astype(jnp.float32)
            buffer[i, :, :span] = value.astype(buffer.dtype)
            start = pl.multiple_of(index * span, span)
            copies.append(
                pltpu.make_async_copy(
                    buffer.at[i, :, :span], result.at[:, pl.ds(start, span)], sems.at[i]
                )
            )
            copies[-1].start()
        for copy in copies:
            copy.wait()

    return pl.pallas_call(
        kernel,
        in_specs=[IN_VMEM] * 3
        + [pl.BlockSpec(memory_space=pl.ANY)] * count
        + ([] if out is None else [IN_HBM]),
        out_specs=IN_HBM,
        out_shape=jax.ShapeDtypeStruct((rows, width), jnp.bfloat16),
        input_output_aliases={} if out is None else {3 + count: 0},
        scratch_shapes=[
            pltpu.VMEM((count, rows, max(spans)), jnp.bfloat16),
            pltpu.SemaphoreType.DMA((count,)),
        ]
        + [pltpu.VMEM(source.shape, source.dtype) for source in sources]
        + [pltpu.SemaphoreType.DMA((count,))],
        compiler_params=WIDE_PARAMS,
        cost_estimate=cost,
        name="finish",
    )(cot, g, recv, *sources, *([] if out is None else [out]))


def ring_pairs(devices):
    chips = devices // 2
    order = list(range(0, chips, 2)) + list(range(chips - 1, 0, -2))
    pairs = []
    for part in range(2):
        for i, chip in enumerate(order):
            for core in range(2):
                other = order[(i + (1 if core == part else -1)) % chips]
                pairs.append((part * devices + 2 * chip + core, part * devices + 2 * other + core))
    return pairs


def ring_body(
    inputs,
    cotangent,
    frozen_value_weight,
    adapter_down_weights,
    adapter_up_weights,
    padded_block_adapter,
    block_live_rows,
    adapter_storage_row,
    *,
    devices,
):
    steps = devices // 4
    shard = frozen_value_weight.shape[0]
    width = inputs.shape[1]
    ring = ring_pairs(devices)
    cores = [(i, i ^ 1) for i in range(devices)]
    across = [(0, 1), (1, 0)]
    diagonal = [(p * devices + i, (1 - p) * devices + (i ^ 1)) for p in range(2) for i in range(devices)]

    def cross(products):
        return (
            lax.ppermute(products[0], "fsdp", cores),
            lax.ppermute(products[1], "parts", across),
            lax.ppermute(products[2], ("parts", "fsdp"), diagonal),
        )

    other_shard = lax.ppermute(frozen_value_weight, "fsdp", cores)
    masked = mask_rows(block_live_rows, cotangent)
    core_masked = lax.ppermute(masked, "fsdp", cores)
    far_masked = lax.ppermute(masked, "parts", across)
    adapter, _ = after(padded_block_adapter, masked)
    payload = gather_rows(
        adapter, adapter_storage_row, adapter_down_weights, adapter_up_weights, devices
    )
    recv = lax.all_to_all(payload, "fsdp", split_axis=0, concat_axis=0, tiled=True)

    travelling = lax.ppermute(frozen_value_weight, ("parts", "fsdp"), ring)

    firsts = [2 + 4 * step for step in range(steps)]
    pieces, received = [], []
    for step in range(steps):
        if step == 0:
            travelling, far_masked, _ = after(travelling, far_masked, payload)
            diagonal_masked = lax.ppermute(far_masked, "fsdp", cores)
            grads = zero_grads(payload, adapter_down_weights.shape, adapter_up_weights.shape)
            (far_masked, grads) = after(far_masked, grads)
            cots = (core_masked, far_masked, diagonal_masked)
        elif step == 1:
            travelling, sent, grads, received[0] = after(travelling, sent, grads, received[0])
        pieces.append(travelling)
        if step < steps - 2:
            travelling = lax.ppermute(travelling, ("parts", "fsdp"), ring)
        pin = as_it_is if step >= steps - 2 else in_hbm
        owned = step >= steps - 2
        if owned:
            cots = (*cots[:3], masked)
        products = far_products(cots, pieces[step], pin, step == steps - 2, owned)
        if step == steps - 2:
            *products, own, travelling = products
            travelling, products, out, received[-1] = after(
                travelling, products, out, received[-1]
            )
            travelling = lax.ppermute(travelling, ("parts", "fsdp"), ring)
            sent, products = after(sent, products)
            sums = lax.all_to_all(sent, "fsdp", split_axis=0, concat_axis=0, tiled=True)
        if step == steps - 1:
            *products, last_own = products
        received.append(cross(products))
        if step == 0:
            recv, _ = after(recv, products[0])
            sent, g = adapter_terms(inputs, masked, recv)
        if step == steps - 3:
            cot, _ = after(masked, products[0])
            at = [0, 1, *firsts[: step + 1]] + [firsts[0] + i for i in range(1, 4)]
            weights = (frozen_value_weight, other_shard, *pieces[:2])
            out = finish(devices, at, cot, weights, received[0], g, recv, None, width, shard)
            travelling, out = after(travelling, out)
        if step == steps - 2:
            out, _ = after(out, products)
            at = [firsts[step]] + [first + i for first in firsts[1:step] for i in range(1, 4)]
            early = (own, *sum(received[1:step], ()))
            out = finish(devices, at, masked, (), early, g, recv, out, width, shard)
            travelling, out = after(travelling, out)
    at = firsts[-1:] + [firsts[-2] + i for i in range(1, 4)]
    late = (last_own, *received[-2])
    out = finish(devices, at, masked, (), late, g, recv, out, width, shard, in_hbm, LONGER)
    at = [firsts[-1] + i for i in range(1, 4)]
    out = finish(devices, at, masked, (), received[-1], g, recv, out, width, shard, as_it_is)
    sums, out = after(sums, out)
    down_grad, up_grad = scatter_rows(padded_block_adapter, adapter_storage_row, sums, *grads)
    return (out, down_grad, up_grad)


def after(value, *earlier):
    return lax.optimization_barrier((value,) + earlier)


def gather_body(
    inputs,
    cotangent,
    frozen_value_weight,
    adapter_down_weights,
    adapter_up_weights,
    padded_block_adapter,
    block_live_rows,
    adapter_storage_row,
):
    hidden_width = inputs.shape[1]
    kv_width = cotangent.shape[1]
    token_rows = inputs.shape[0]
    block_count = token_rows // BLOCK
    first_block = lax.axis_index("fsdp") * block_count
    live_rows = lax.dynamic_slice_in_dim(block_live_rows, first_block, block_count)
    positions = jnp.arange(BLOCK, dtype=jnp.int32)
    live_mask = positions[None, :] < live_rows[:, None]
    blocked_cot = cotangent.reshape(block_count, BLOCK, kv_width)
    masked_blocks = jnp.where(live_mask[:, :, None], blocked_cot, jnp.zeros_like(blocked_cot))
    masked = masked_blocks.reshape(token_rows, kv_width)
    block_storage_row = slot_lookup(padded_block_adapter, adapter_storage_row)
    down_weight_rows = jnp.take(adapter_down_weights, block_storage_row, axis=0)
    up_weight_rows = jnp.take(adapter_up_weights, block_storage_row, axis=0)
    down_mine, up_mine = (
        lax.all_to_all(down_weight_rows, "fsdp", split_axis=0, concat_axis=1, tiled=True),
        lax.all_to_all(up_weight_rows, "fsdp", split_axis=0, concat_axis=1, tiled=True),
    )
    frozen_gradient = lax.dot_general(
        masked,
        lax.all_gather(frozen_value_weight, "fsdp", axis=0, tiled=True),
        (((1,), (1,)), ((), ())),
        preferred_element_type=jnp.float32,
    )
    down_weight_matrix = down_mine.reshape(block_count, hidden_width, ADAPTER_RANK)
    up_weight_matrix = up_mine.reshape(block_count, ADAPTER_RANK, kv_width)
    blocked_in = inputs.reshape(block_count, BLOCK, hidden_width)
    rank_projection = jnp.einsum(
        "kbd,kdr->kbr", blocked_in, down_weight_matrix, preferred_element_type=jnp.float32
    ).astype(jnp.bfloat16)
    rank_space_gradient = jnp.einsum(
        "kbv,krv->kbr", masked_blocks, up_weight_matrix, preferred_element_type=jnp.float32
    ).astype(jnp.bfloat16)
    adapter_gradient_term = adapter_scale * jnp.einsum(
        "kbr,kdr->kbd", rank_space_gradient, down_weight_matrix, preferred_element_type=jnp.float32
    )
    input_gradient = (
        frozen_gradient + adapter_gradient_term.reshape(token_rows, hidden_width)
    ).astype(jnp.bfloat16)
    partial_down_weight = adapter_scale * jnp.einsum(
        "kbd,kbr->kdr", blocked_in, rank_space_gradient, preferred_element_type=jnp.float32
    )
    partial_up_weight = adapter_scale * jnp.einsum(
        "kbr,kbv->krv", rank_projection, masked_blocks, preferred_element_type=jnp.float32
    )
    partial_down_weight = partial_down_weight.reshape(block_count, hidden_width * ADAPTER_RANK)
    partial_up_weight = partial_up_weight.reshape(block_count, ADAPTER_RANK * kv_width)
    recv_down, recv_up = (
        lax.all_to_all(partial_down_weight, "fsdp", split_axis=1, concat_axis=0, tiled=True),
        lax.all_to_all(partial_up_weight, "fsdp", split_axis=1, concat_axis=0, tiled=True),
    )
    onehot = (
        jnp.arange(ADAPTER_GROUP, dtype=jnp.int32)[:, None] == block_storage_row[None, :]
    ).astype(jnp.float32)
    highest_precision = lax.Precision.HIGHEST
    down_grad = jnp.dot(
        onehot, recv_down, precision=highest_precision, preferred_element_type=jnp.float32
    )
    up_grad = jnp.dot(
        onehot, recv_up, precision=highest_precision, preferred_element_type=jnp.float32
    )
    return (input_gradient, down_grad, up_grad)


def solution(mesh):
    devices = mesh.shape["fsdp"]
    in_specs = (
        P(("parts", "fsdp"), None),
        P(("parts", "fsdp"), None),
        P("fsdp", None),
        P("parts", "fsdp"),
        P("parts", "fsdp"),
        P("parts"),
        P("parts"),
        P("parts"),
    )
    out_specs = (P(("parts", "fsdp"), None), P("parts", "fsdp"), P("parts", "fsdp"))

    def program(*arrays):
        shard = arrays[2].shape[0] // devices
        rows = arrays[0].shape[0] // devices // 2
        adapter_tiles = arrays[3].shape[1] // devices // LANES
        fits = rows == 2 * BLOCK and 2 * adapter_tiles == LANES and shard % 512 == 0
        if mesh.shape["parts"] == 2 and devices % 4 == 0 and fits:
            body = functools.partial(ring_body, devices=devices)
        else:
            body = gather_body
        return jax.shard_map(
            body, mesh=mesh, in_specs=in_specs, out_specs=out_specs, check_vma=False
        )(*arrays)

    return program
```
